32 devices in a mesh: slab: 2 (over y), gx: 4 (over z), gy: 4 (over x, core).
Axes of the slice: x: 2, y: 2, z: 4, core: 2. Of those that a mesh axis runs over, the one named last changes fastest.
Arguments:
- charge: float32 [32, 512, 512], P(None, ('slab', 'gx'), 'gy'), parts along dimension 1, may hold values from -6 to 6
- surface_charge: float32 [2, 512, 512], P(None, ('slab', 'gx'), 'gy'), parts along dimension 1, may hold values from -6 to 6
Outputs:
- potential: float32 [32, 512, 512], P(None, ('slab', 'gx'), 'gy'), parts along dimension 1
- interface_residual: float32 [32, 512, 512], P(None, ('slab', 'gx'), 'gy'), parts along dimension 1
The draws below stay inside these ranges and needn't reach their ends.
There are 2 independent parts, one for each index of `slab`. The reference program is written for one: setup_inputs(seed, part) draws one part's arguments, and reference() takes and returns one part's arrays. A program takes and returns all parts, laid end to end along the dimension named above; each array names one. Nothing has to cross between parts.
All inputs are finite; a program needn't handle non-finite values.
Results may differ from the reference program's by a relative error of at most 0.0003.
Values sent between devices are 32-bit elements; how exact they have to be, the bound alone decides.
A program may use at most 64 MiB of HBM per device.

```python
import jax
import jax.numpy as jnp
from jax import lax

BLOCK_X = 64
BLOCK_Y = 128
DEPTH = 32
ITERS = 2
NX = 256
NY = 512
N_GX = 4
N_GY = 4


def levels(key, dims, pieces, least, largest):
    level, own = 1.0, jax.random.fold_in(key, 6)
    for axis_at, blocks in pieces:
        heights = jnp.exp(jax.random.uniform(jax.random.fold_in(own, axis_at), (blocks,), jnp.float32, least / len(pieces), largest / len(pieces)))
        level = level * jnp.repeat(heights, dims[axis_at] // blocks).reshape([-1 if axis == axis_at else 1 for axis in range(len(dims))])
    return level


def noise(rng, extent, width, most, split=(), dtype=jnp.bfloat16):
    loudness = levels(rng, extent, split, -0.22, 0.18) if split else 1.0
    result = jax.random.normal(rng, extent, jnp.float32) * width * loudness
    return jnp.minimum(jnp.maximum(result, -most), most).astype(dtype)


def setup_inputs(seed: int = 0, part: int = 0) -> dict:
    key_of = jax.random.split(jax.random.key(seed), 3)
    own_keys = jax.random.split(jax.random.fold_in(key_of[2], part), 3)
    return {
        "charge": noise(own_keys[0], (DEPTH, NX, NY), 1.0, 6.0, ((1, 4), (2, 4)), jnp.float32),
        "surface_charge": noise(own_keys[1], (2, NX, NY), 1.0, 6.0, ((1, 4), (2, 4)), jnp.float32),
    }


SCREEN = 0.02

def sine_table(count):
    index = jnp.arange(1, count).astype(jnp.float32)
    return jnp.sqrt(2.0 / count) * jnp.sin(jnp.pi * jnp.outer(index, index) / count)

def cosine_table(count):
    place = jnp.arange(count).astype(jnp.float32) + 0.5
    order = jnp.arange(count).astype(jnp.float32)
    factor = jnp.where(order == 0.0, jnp.sqrt(1.0 / count), jnp.sqrt(2.0 / count))
    return factor[None, :] * jnp.cos(jnp.pi * jnp.outer(place, order) / count)

def spectrum_table():
    across = 2.0 - 2.0 * jnp.cos(jnp.pi * jnp.arange(1, BLOCK_X).astype(jnp.float32) / BLOCK_X)
    along = 2.0 - 2.0 * jnp.cos(jnp.pi * jnp.arange(1, BLOCK_Y).astype(jnp.float32) / BLOCK_Y)
    vertical = 2.0 - 2.0 * jnp.cos(jnp.pi * jnp.arange(DEPTH).astype(jnp.float32) / DEPTH)
    return SCREEN + vertical[:, None, None] + across[None, :, None] + along[None, None, :]

def apply_full(field):
    beside = jnp.roll(field, -1, 1) + jnp.roll(field, 1, 1) + jnp.roll(field, -1, 2) + jnp.roll(field, 1, 2)
    upper = jnp.concatenate([field[1:], field[-1:]], 0)
    lower = jnp.concatenate([field[:1], field[:-1]], 0)
    return (6.0 + SCREEN) * field - beside - upper - lower

def solve_interior(field):
    high = lax.Precision.HIGHEST
    sines_x = sine_table(BLOCK_X)
    sines_y = sine_table(BLOCK_Y)
    cosines = cosine_table(DEPTH)
    spectrum = spectrum_table()
    blocks = field.reshape(DEPTH, N_GX, BLOCK_X, N_GY, BLOCK_Y)[:, :, 1:, :, 1:]
    hat = jnp.einsum('zk,zgxhy->kgxhy', cosines, blocks, precision=high)
    hat = jnp.einsum('xa,kgxhy->kgahy', sines_x, hat, precision=high)
    hat = jnp.einsum('yb,kgahy->kgahb', sines_y, hat, precision=high)
    hat = hat / spectrum[:, None, :, None, :]
    back = jnp.einsum('yb,kgahb->kgahy', sines_y, hat, precision=high)
    back = jnp.einsum('xa,kgahy->kgxhy', sines_x, back, precision=high)
    back = jnp.einsum('zk,kgxhy->zgxhy', cosines, back, precision=high)
    back = jnp.pad(back, ((0, 0), (0, 0), (1, 0), (0, 0), (1, 0)))
    return back.reshape(DEPTH, N_GX * BLOCK_X, N_GY * BLOCK_Y)

def reference(charge, surface_charge):
    size_x = charge.shape[1]
    size_y = charge.shape[2]
    edge_x = jnp.arange(size_x) % BLOCK_X == 0
    edge_y = jnp.arange(size_y) % BLOCK_Y == 0
    gamma = jnp.where(edge_x[:, None] | edge_y[None, :], 1.0, 0.0).astype(jnp.float32)[None]
    source = charge.at[0].add(surface_charge[0]).at[-1].add(surface_charge[1])
    base = solve_interior(source)
    reduced = gamma * (source - apply_full(base))

    def schur(probe):
        lifted = -solve_interior(apply_full(probe))
        return gamma * apply_full(probe + lifted)
    iterate = jnp.zeros_like(reduced)
    residual = reduced
    direction = reduced
    norm_now = jnp.sum(residual * residual)
    for step in range(ITERS):
        image = schur(direction)
        alpha = norm_now / jnp.sum(direction * image)
        iterate = iterate + alpha * direction
        residual = residual - alpha * image
        norm_next = jnp.sum(residual * residual)
        direction = residual + norm_next / norm_now * direction
        norm_now = norm_next
    potential = iterate + base - solve_interior(apply_full(iterate))
    return (potential, residual)
```

```python
import functools

import jax
import jax.numpy as jnp
import ml_dtypes
import numpy as np
from jax import lax
from jax.experimental import pallas as pl
from jax.experimental.pallas import tpu as pltpu
from jax.sharding import PartitionSpec as P

ITERS = 2


SCREEN = 0.02


def padded(block, sides, width):
    for axis, dim in sides:
        count = lax.axis_size(axis)
        forward = [(i, i + 1) for i in range(count - 1)]
        forward.append((count - 1, 0))
        backward = [(target, source) for source, target in forward]
        low = lax.ppermute(
            lax.slice_in_dim(block, block.shape[dim] - width, None, axis=dim), axis, forward
        )
        high = lax.ppermute(lax.slice_in_dim(block, 0, width, axis=dim), axis, backward)
        block = jnp.concatenate([low, block, high], axis=dim)
    return block


def sine_full(count):
    index = jnp.arange(count).astype(jnp.float32)
    return jnp.sqrt(2.0 / count) * jnp.sin(jnp.pi * jnp.outer(index, index) / count)


def cosine_table(count):
    place = jnp.arange(count).astype(jnp.float32) + 0.5
    order = jnp.arange(count).astype(jnp.float32)
    factor = jnp.where(order == 0.0, jnp.sqrt(1.0 / count), jnp.sqrt(2.0 / count))
    return factor[None, :] * jnp.cos(jnp.pi * jnp.outer(place, order) / count)


def spectrum_table(depth, width, height):
    across = 2.0 - 2.0 * jnp.cos(jnp.pi * jnp.arange(width).astype(jnp.float32) / width)
    along = 2.0 - 2.0 * jnp.cos(jnp.pi * jnp.arange(height).astype(jnp.float32) / height)
    vertical = 2.0 - 2.0 * jnp.cos(jnp.pi * jnp.arange(depth).astype(jnp.float32) / depth)
    return SCREEN + vertical[:, None, None] + across[None, :, None] + along[None, None, :]


def apply_full(field):
    row_rims = jnp.stack([field[:, 0, :], field[:, -1, :]], 1)
    row_ext = padded(row_rims, (("gx", 1),), 1)
    col_rims = jnp.stack([field[:, :, 0], field[:, :, -1]], 0)
    col_ext = padded(col_rims, (("gy", 0),), 1)
    from_below_x = jnp.concatenate([row_ext[:, 0:1, :], field[:, :-1, :]], 1)
    from_above_x = jnp.concatenate([field[:, 1:, :], row_ext[:, 3:4, :]], 1)
    from_below_y = jnp.concatenate([col_ext[0][:, :, None], field[:, :, :-1]], 2)
    from_above_y = jnp.concatenate([field[:, :, 1:], col_ext[3][:, :, None]], 2)
    beside = from_below_x + from_above_x + from_below_y + from_above_y
    upper = jnp.concatenate([field[1:], field[-1:]], 0)
    lower = jnp.concatenate([field[:1], field[:-1]], 0)
    return (6.0 + SCREEN) * field - beside - upper - lower


def solve_interior(field, sines_x, sines_y, cosines, spectrum):
    high = lax.Precision.HIGHEST
    depth, width, height = field.shape
    hat = jnp.dot(field.reshape(depth * width, height), sines_y, precision=high).reshape(
        depth, width, height
    )
    hat = jnp.matmul(sines_x, hat, precision=high)
    hat = jnp.dot(cosines.T, hat.reshape(depth, width * height), precision=high).reshape(
        depth, width, height
    )
    hat = hat / spectrum
    back = jnp.dot(cosines, hat.reshape(depth, width * height), precision=high).reshape(
        depth, width, height
    )
    back = jnp.matmul(sines_x, back, precision=high)
    back = jnp.dot(back.reshape(depth * width, height), sines_y, precision=high)
    return back.reshape(depth, width, height)


def norm_total(residual):
    return lax.psum(jnp.sum(residual * residual), ("gx", "gy"))


def curvature_total(direction, image):
    return lax.psum(jnp.sum(direction * image), ("gx", "gy"))


def on_device(charge, surface_charge):
    depth, width, height = charge.shape
    sines_x = sine_full(width)
    sines_y = sine_full(height)
    cosines = cosine_table(depth)
    spectrum = spectrum_table(depth, width, height)
    row_place = lax.broadcasted_iota(jnp.int32, (1, width, height), 1)
    col_place = lax.broadcasted_iota(jnp.int32, (1, width, height), 2)
    gamma = jnp.where((row_place == 0) | (col_place == 0), 1.0, 0.0).astype(jnp.float32)
    source = charge.at[0].add(surface_charge[0]).at[-1].add(surface_charge[1])
    base = solve_interior(source, sines_x, sines_y, cosines, spectrum)
    reduced = gamma * (source - apply_full(base))
    iterate = jnp.zeros_like(reduced)
    residual = reduced
    direction = reduced
    norm_now = norm_total(residual)
    for step in range(ITERS):
        lifted = -solve_interior(apply_full(direction), sines_x, sines_y, cosines, spectrum)
        image, lifted = (gamma * apply_full(direction + lifted), lifted)
        alpha = norm_now / curvature_total(direction, image)
        iterate = iterate + alpha * direction
        residual = residual - alpha * image
        if step + 1 < ITERS:
            norm_next = norm_total(residual)
            direction = residual + norm_next / norm_now * direction
            norm_now = norm_next
    correction = -solve_interior(apply_full(iterate), sines_x, sines_y, cosines, spectrum)
    potential = iterate + base + correction
    return (potential, residual)


DEPTH, WIDTH, HEIGHT = 32, 64, 128
F32, BF16 = jnp.float32, jnp.bfloat16


def halves(table):
    table = np.asarray(table, np.float64)
    high = table.astype(np.float32).astype(ml_dtypes.bfloat16)
    low = (table - high.astype(np.float64)).astype(np.float32).astype(ml_dtypes.bfloat16)
    return high, low


def sine_unit(count):
    index = np.arange(count)
    table = np.sqrt(2.0 / count) * np.sin(np.pi * np.outer(index, index) / count)
    table[0, 0] = 1.0
    return table


def host_tables():
    place, order = np.arange(DEPTH) + 0.5, np.arange(DEPTH)
    factor = np.where(order == 0, np.sqrt(1.0 / DEPTH), np.sqrt(2.0 / DEPTH))
    cosines = factor[None, :] * np.cos(np.pi * np.outer(place, order) / DEPTH)
    sin_x, sin_y = sine_unit(WIDTH), sine_unit(HEIGHT)
    vertical = 2.0 - 2.0 * np.cos(np.pi * order / DEPTH)
    across = 2.0 - 2.0 * np.cos(np.pi * np.arange(WIDTH) / WIDTH)
    along = 2.0 - 2.0 * np.cos(np.pi * np.arange(HEIGHT) / HEIGHT)
    ux = np.sqrt(2.0 / WIDTH) * np.sin(np.pi * np.arange(WIDTH) / WIDTH)
    uy = np.sqrt(2.0 / HEIGHT) * np.sin(np.pi * np.arange(HEIGHT) / HEIGHT)
    sx = np.where(np.arange(WIDTH) % 2 == 1, 1.0, -1.0)
    sy = np.where(np.arange(HEIGHT) % 2 == 1, 1.0, -1.0)
    sx[0] = sy[0] = 0.0
    ex, ey = np.eye(WIDTH)[0], np.eye(HEIGHT)[0]
    t = {}
    t["zf"] = halves(np.kron(cosines.T, np.eye(8)))
    t["zi"] = halves(np.kron(cosines, np.eye(8)))
    t["x"] = halves(np.kron(np.eye(4), sin_x))
    t["y"] = halves(sin_y)
    plane = SCREEN + across[:, None] + along[None, :]
    t["plane"] = plane.astype(np.float32)
    t["vert"] = [float(v) for v in vertical]
    t["ur"] = halves(np.concatenate([np.kron(np.eye(4), (ux + ex)[None]), np.kron(np.eye(4), (ux * sx)[None])], 0))
    uc = np.zeros((16, HEIGHT))
    uc[0], uc[1], uc[2] = uy + ey, uy * sy, ey
    t["uc"] = halves(uc)
    spec = plane[None] + vertical[:, None, None]
    inner = np.zeros((WIDTH, HEIGHT))
    inner[1:, 1:] = 1.0
    inv = inner / spec
    row_near = np.einsum("a,kab->kb", ux * ux, inv)
    row_far = np.einsum("a,kab->kb", ux * ux * sx, inv)
    col_near = np.einsum("b,kab->ka", uy * uy, inv)
    col_far = np.einsum("b,kab->ka", uy * uy * sy, inv)
    row_coef = SCREEN + vertical[:, None] + 2.0 + along[None, :] - 2.0 * row_near
    col_coef = SCREEN + vertical[:, None] + 2.0 + across[None, :] - 2.0 * col_near
    row_coef[:, 0] = SCREEN + vertical + 4.0
    col_coef[:, 0] = 0.0
    own = np.zeros((DEPTH // 2, 8, HEIGHT))
    own[:, 0], own[:, 1] = row_coef[0::2], row_coef[1::2]
    own[:, 2], own[:, 3] = row_far[0::2], row_far[1::2]
    own[:, 4] = np.concatenate([col_coef[0::2], col_coef[1::2]], 1)
    own[:, 5] = np.concatenate([col_far[0::2], col_far[1::2]], 1)
    own[:, 6], own[:, 7] = vertical[0::2, None], vertical[1::2, None]
    t["own"] = own.astype(np.float32)
    border = np.zeros((WIDTH, HEIGHT))
    border[0], border[:, 0] = uy, ux
    t["pair"] = np.stack([np.outer(ux, uy), border]).astype(np.float32)
    signs = np.zeros((8, HEIGHT))
    signs[0] = sy
    signs[1] = np.concatenate([sx, sx])
    t["signs"] = signs.astype(np.float32)
    zero = np.zeros(WIDTH)
    left = np.zeros((8, HEIGHT))
    left[0], left[1] = np.concatenate([ux + ex, zero]), np.concatenate([zero, ux + ex])
    left[2], left[3] = np.concatenate([ux * sx, zero]), np.concatenate([zero, ux * sx])
    left[6], left[7] = np.concatenate([ex, zero]), np.concatenate([zero, ex])
    right = np.zeros((8, HEIGHT))
    right[4], right[5] = uy + ey, uy * sy
    t["left"], t["right"] = left.astype(np.float32), right.astype(np.float32)
    split = np.concatenate([np.arange(0, DEPTH, 2), np.arange(1, DEPTH, 2)])
    t["cos"] = cosines[split][:, split].astype(np.float32)
    t["sy"] = sin_y.astype(np.float32)
    t["sx2"] = np.kron(np.eye(2), sin_x).astype(np.float32)
    return t


def halved(x):
    high = x.astype(BF16)
    return high, (x - high.astype(F32)).astype(BF16)


def dot(a, b, dims=((1,), (0,))):
    return lax.dot_general(a, b, (dims, ((), ())), preferred_element_type=F32)


def dot3(a, b, dims=((1,), (0,))):
    return dot(a[0], b[0], dims) + (dot(a[0], b[1], dims) + dot(a[1], b[0], dims))


def dot_exact(a, b, dims=((1,), (0,))):
    return lax.dot_general(
        a, b, (dims, ((), ())), precision=lax.Precision.HIGHEST, preferred_element_type=F32
    )


def lane_ids(shape):
    return lax.broadcasted_iota(jnp.int32, shape, len(shape) - 1)


def interior():
    row = lax.broadcasted_iota(jnp.int32, (WIDTH, HEIGHT), 0)
    return (row > 0) & (lane_ids((WIDTH, HEIGHT)) > 0)


def pair_lanes(parts):
    return jnp.concatenate(parts, 1)


def forward_kernel(vert, charge, surface, zh, zl, xh, xl, yh, yl, urh, url, uch, ucl, plane, base, msg, work):
    ztab, xtab, ytab = (zh[...], zl[...]), (xh[...], xl[...]), (yh[...], yl[...])
    for t in range(WIDTH // 16):
        sides = []
        for h in range(2):
            at = pl.ds(16 * t + 8 * h, 8)
            block = charge[:, at, :]
            block = jnp.concatenate(
                [block[:1] + surface[0:1, at, :], block[1:-1], block[-1:] + surface[1:2, at, :]], 0
            )
            sides.append(block.reshape(DEPTH * 8, HEIGHT))
        out = dot3(ztab, halved(pair_lanes(sides)))
        for h in range(2):
            side = out[:, HEIGHT * h:HEIGHT * (h + 1)]
            side = dot3(halved(side), ytab)
            work[:, 16 * t + 8 * h:16 * t + 8 * h + 8, :] = side.reshape(DEPTH, 8, HEIGHT)
    inner = interior()
    flat = plane[...]
    lane = lane_ids((8, HEIGHT))
    for t in range(DEPTH // 8):
        sides = [work[8 * t + 4 * h:8 * t + 4 * h + 4].reshape(4 * WIDTH, HEIGHT) for h in range(2)]
        out = dot3(xtab, halved(pair_lanes(sides)))
        for h in range(2):
            side = out[:, HEIGHT * h:HEIGHT * (h + 1)].reshape(4, WIDTH, HEIGHT)
            full = []
            corner = []
            for s in range(4):
                k = 8 * t + 4 * h + s
                one = jnp.where(inner, side[s] / (flat + vert[k]), side[s])
                base[k] = jnp.where(inner, one, 0.0)
                full.append(one)
                corner.append(one[0:1])
            full = jnp.concatenate(full, 0)
            parts = halved(full)
            rows = dot3((urh[...], url[...]), parts)
            own = jnp.concatenate(corner + [jnp.zeros((4, HEIGHT), F32)], 0)
            rows = jnp.where(lane == 0, own, rows)
            cols = dot3((uch[...], ucl[...]), parts, ((1,), (1,)))
            first = lane_ids((1, 4 * WIDTH)) % WIDTH == 0
            near = jnp.where(first, cols[2:3], cols[0:1])
            far = jnp.where(first, 0.0, cols[1:2])
            for g in range(2):
                at = slice(HEIGHT * g, HEIGHT * (g + 1))
                msg[4 * t + 2 * h + g] = jnp.concatenate(
                    [rows[2 * g:2 * g + 2], rows[4 + 2 * g:6 + 2 * g], near[:, at], far[:, at], jnp.zeros((2, HEIGHT), F32)],
                    0,
                )


def shift_x(n_gx, n_gy, field, by):
    cut = (by % n_gx) * n_gy
    return jnp.concatenate([field[cut:], field[:cut]], 0)


def shift_y(n_gx, n_gy, field, by):
    place = lax.broadcasted_iota(jnp.int32, field.shape, 0) % n_gy
    count = n_gx * n_gy
    ahead = by % count
    plain = jnp.concatenate([field[ahead:], field[:ahead]], 0)
    wrap = (by - n_gy if by > 0 else by + n_gy) % count
    wrapped = jnp.concatenate([field[wrap:], field[:wrap]], 0)
    edge = n_gy - 1 if by > 0 else 0
    return jnp.where(place == edge, wrapped, plain)


def turn_half(x):
    return jnp.concatenate([x[:, WIDTH:], x[:, :WIDTH]], 1)


def schur_modes(n_gx, n_gy, coef, table, row, col):
    row_coef, row_far, col_coef, col_far, row_sign, col_sign = coef
    sx = functools.partial(shift_x, n_gx, n_gy)
    sy = functools.partial(shift_y, n_gx, n_gy)
    count = n_gx * n_gy
    across = dot_exact(jnp.concatenate([col, col * col_sign], 0), table)
    along = dot_exact(jnp.concatenate([row, row * row_sign], 0), table, ((1,), (1,)))
    v = across[:count] + sx(across[count:], -1)
    w = along[:count] + sy(along[count:], -1)
    row_out = row_coef * row - row_far * (sx(row, 1) + sx(row, -1)) - v - row_sign * sy(v, 1)
    col_out = col_coef * col - col_far * (sy(col, 1) + sy(col, -1)) - w - col_sign * sx(w, 1)
    lane = lane_ids((count, HEIGHT))
    row_out = row_out - jnp.concatenate(
        [jnp.where(lane == 0, w, 0.0), jnp.where(lane == 0, turn_half(w), 0.0)], 1
    )
    col_out = jnp.where(
        lane == 0, row_out[:, :HEIGHT], jnp.where(lane == WIDTH, turn_half(row_out[:, HEIGHT:]), col_out)
    )
    return row_out, col_out


def owner_tables(own, pair, signs):
    inner = interior()
    parts = []
    for s in range(2):
        one = jnp.where(inner, pair[0] / (pair[2] + own[6 + s:7 + s]), pair[1])
        parts.append(one)
    blank = jnp.zeros((WIDTH, HEIGHT), F32)
    table = jnp.concatenate([pair_lanes([parts[0], blank]), pair_lanes([blank, parts[1]])], 0)
    coef = (
        pair_lanes([own[0:1], own[1:2]]),
        pair_lanes([own[2:3], own[3:4]]),
        own[4:5],
        own[5:6],
        pair_lanes([signs[0:1], signs[0:1]]),
        signs[1:2],
    )
    return coef, table


def start_modes(n_gx, n_gy, fields):
    sx = functools.partial(shift_x, n_gx, n_gy)
    sy = functools.partial(shift_y, n_gx, n_gy)
    row = pair_lanes([fields[0], fields[1]]) + sx(pair_lanes([fields[2], fields[3]]), -1)
    col = fields[4] + sy(fields[5], -1)
    return row, col


def inner_product(first, second):
    lane = lane_ids(first[1].shape)
    cols = jnp.where(lane % WIDTH == 0, 0.0, first[1] * second[1])
    rows = first[0] * second[0]
    return jnp.sum(rows[:, :HEIGHT] + rows[:, HEIGHT:] + cols)


def face_fields(n_gx, n_gy, pair):
    row, col = pair
    beyond = shift_x(n_gx, n_gy, row, 1)
    return [
        row[:, :HEIGHT], row[:, HEIGHT:], beyond[:, :HEIGHT], beyond[:, HEIGHT:],
        col, shift_y(n_gx, n_gy, col, 1),
    ]


def steps(sums):
    rr, rw, ww, wv = sums
    alpha = rr / rw
    after = alpha * alpha * ww - rr
    beta = after / rr
    curve = (1 + beta) * (1 + beta) * rw - 2 * (1 + beta) * alpha * ww + alpha * alpha * wv
    second = after / curve
    return alpha + second * (1 + beta), -second * alpha


def exchange_kernel(n_gx, n_gy, msg, own_ref, pair_ref, signs_ref, faces, rest, got, back, landed, sems):
    count = n_gx * n_gy
    gx, gy = lax.axis_index("gx"), lax.axis_index("gy")
    me = gx * n_gy + gy

    def partner(off):
        to = lax.rem(me + off, count)
        return to, {"gx": lax.div(to, n_gy), "gy": lax.rem(to, n_gy)}

    barrier = pltpu.get_barrier_semaphore()
    for off in range(1, count):
        pl.semaphore_signal(barrier, inc=1, device_id=partner(off)[1], device_id_type=pl.DeviceIdType.MESH)
    coef, table = owner_tables(own_ref[me], pair_ref[...], signs_ref[...])
    pl.semaphore_wait(barrier, count - 1)

    def spread(source, target, which):
        copies = []
        for off in range(1, count):
            to, device = partner(off)
            copies.append(
                pltpu.make_async_remote_copy(
                    src_ref=source.at[to],
                    dst_ref=target.at[me],
                    send_sem=sems.at[which, 0, off],
                    recv_sem=sems.at[which, 1, off],
                    device_id=device,
                    device_id_type=pl.DeviceIdType.MESH,
                )
            )
            copies[-1].start()
        target[me] = source[me]
        return copies

    first = spread(msg, got, 0)
    for copy in first:
        copy.wait_recv()
    fields = [got[:, f, :] for f in range(6)]
    r = start_modes(n_gx, n_gy, fields)
    w = schur_modes(n_gx, n_gy, coef, table, *r)
    v = schur_modes(n_gx, n_gy, coef, table, *w)
    for f, field in enumerate(face_fields(n_gx, n_gy, r)):
        back[:, f, :] = field
    for f, field in enumerate(face_fields(n_gx, n_gy, w)):
        back[:, 8 + f, :] = field
    back[:, 6, :] = v[0][:, :HEIGHT]
    back[:, 7, :] = v[0][:, HEIGHT:]
    back[:, 14, :] = v[1]
    sums = (inner_product(r, r), inner_product(r, w), inner_product(w, w), inner_product(w, v))
    lane = lane_ids((count, HEIGHT))
    back[:, 15, :] = sum(jnp.where(lane == s, value, 0.0) for s, value in enumerate(sums))
    second = spread(back, landed, 1)
    for copy in second:
        copy.wait_recv()
    for copy in first + second:
        copy.wait_send()
    faces[...], rest[...] = combine(landed[...])


def combine(landed):
    near, far = landed[:, :8], landed[:, 8:]
    total = jnp.sum(far[:, 7:8, :], 0)
    lane = lane_ids((1, HEIGHT))
    c0, c1 = steps([jnp.sum(jnp.where(lane == s, total, 0.0)) for s in range(4)])
    faces = c0 * near + c1 * far
    lead = near - c0 * far
    rest = jnp.concatenate(
        [lead[:, 0:2] - c1 * near[:, 6:8], lead[:, 4:5] - c1 * far[:, 6:7], jnp.zeros_like(near[:, :5])], 1
    )
    return faces, rest


def stacked(left, right):
    lh, ll = halved(left)
    rh, rl = halved(right)
    lhs = jnp.concatenate([lh.astype(F32), lh.astype(F32), ll.astype(F32)], 0).astype(BF16)
    rhs = jnp.concatenate([rh.astype(F32), rl.astype(F32), rh.astype(F32)], 0).astype(BF16)
    return dot(lhs, rhs, ((0,), (0,)))


def inverse_kernel(vert, base, faces, rest, left, right, zh, zl, xh, xl, yh, yl, plane, cos, sin_y, sin_x2, potential, residual, work):
    ztab, xtab, ytab = (zh[...], zl[...]), (xh[...], xl[...]), (yh[...], yl[...])
    inner = interior()
    flat = plane[...]
    lane = lane_ids((8, HEIGHT))
    sub = lax.broadcasted_iota(jnp.int32, (8, HEIGHT), 0)
    const_left, const_right = left[...], right[...]
    for t in range(DEPTH // 8):
        sides = []
        for h in range(2):
            blocks = []
            for g in range(2):
                o = 4 * t + 2 * h + g
                one = faces[o]
                lhs = jnp.where((sub >= 4) & (sub < 6) & (lane % WIDTH > 0), one, const_left)
                up = jnp.concatenate([one[2:], one[:2]], 0)
                rhs = jnp.where((sub < 4) & (lane > 0), one, const_right)
                rhs = jnp.where((sub >= 6) & (lane == 0), up, rhs)
                out = stacked(lhs, rhs)
                for s in range(2):
                    k = 2 * o + s
                    part = out[WIDTH * s:WIDTH * (s + 1)]
                    part = jnp.where(inner, part / (flat + vert[k]), part)
                    blocks.append(part + base[k])
            sides.append(jnp.concatenate(blocks, 0))
        out = dot3(xtab, halved(pair_lanes(sides)))
        for h in range(2):
            side = dot3(halved(out[:, HEIGHT * h:HEIGHT * (h + 1)]), ytab)
            work[8 * t + 4 * h:8 * t + 4 * h + 4] = side.reshape(4, WIDTH, HEIGHT)
    for t in range(WIDTH // 16):
        sides = [work[:, 16 * t + 8 * h:16 * t + 8 * h + 8, :].reshape(DEPTH * 8, HEIGHT) for h in range(2)]
        out = dot3(ztab, halved(pair_lanes(sides)))
        for h in range(2):
            side = out[:, HEIGHT * h:HEIGHT * (h + 1)]
            potential[:, 16 * t + 8 * h:16 * t + 8 * h + 8, :] = side.reshape(DEPTH, 8, HEIGHT)
    half = DEPTH // 2
    rows = jnp.concatenate([rest[:, 0, :], rest[:, 1, :]], 0)
    rows = dot_exact(cos[...], dot_exact(rows, sin_y[...]))
    cols = dot_exact(rest[:, 2, :], sin_x2[...])
    cols = dot_exact(cos[...], jnp.concatenate([cols[:, :WIDTH], cols[:, WIDTH:]], 0))
    cols = jnp.concatenate([cols[:half], cols[half:]], 1)
    cols = jnp.where(lane_ids((half, HEIGHT)) % WIDTH == 0, 0.0, cols)
    unit = jnp.where(lane == 0, 1.0, 0.0)
    mark = jnp.where(((sub == 0) & (lane == 0)) | ((sub == 1) & (lane == WIDTH)), 1.0, 0.0)
    for o in range(half):
        lhs = jnp.where(sub == 2, cols[o:o + 1], mark)
        rhs = jnp.where(sub == 0, rows[o:o + 1], jnp.where(sub == 1, rows[half + o:half + o + 1], jnp.where(sub == 2, unit, 0.0)))
        out = stacked(lhs, rhs)
        residual[2 * o] = out[:WIDTH]
        residual[2 * o + 1] = out[WIDTH:]


def on_device_modes(n_gx, n_gy, charge, surface_charge):
    t = host_tables()
    count = n_gx * n_gy
    block = jax.ShapeDtypeStruct(charge.shape, F32)
    small = jax.ShapeDtypeStruct((count, 8, HEIGHT), F32)
    params = dict(vmem_limit_bytes=48 * 1024 * 1024)
    base, msg = pl.pallas_call(
        functools.partial(forward_kernel, t["vert"]),
        out_shape=(block, small),
        scratch_shapes=[pltpu.VMEM(charge.shape, F32)],
        compiler_params=pltpu.CompilerParams(**params),
        name="forward",
    )(charge, surface_charge, *t["zf"], *t["x"], *t["y"], *t["ur"], *t["uc"], t["plane"])
    pair = np.concatenate([t["pair"], t["plane"][None]], 0)
    faces, rest = pl.pallas_call(
        functools.partial(exchange_kernel, n_gx, n_gy),
        out_shape=(small, small),
        scratch_shapes=[
            pltpu.VMEM((count, 8, HEIGHT), F32),
            pltpu.VMEM((count, 16, HEIGHT), F32),
            pltpu.VMEM((count, 16, HEIGHT), F32),
            pltpu.SemaphoreType.DMA((2, 2, count)),
        ],
        in_specs=[pl.BlockSpec(memory_space=pltpu.VMEM)] * 4,
        compiler_params=pltpu.CompilerParams(collective_id=0, has_side_effects=True, **params),
        name="exchange",
    )(msg, t["own"], pair, t["signs"])
    return pl.pallas_call(
        functools.partial(inverse_kernel, t["vert"]),
        out_shape=(block, block),
        scratch_shapes=[pltpu.VMEM(charge.shape, F32)],
        compiler_params=pltpu.CompilerParams(**params),
        name="inverse",
    )(base, faces, rest, t["left"], t["right"], *t["zi"], *t["x"], *t["y"], t["plane"], t["cos"], t["sy"], t["sx2"])


def solution(mesh):
    count = mesh.shape["gx"] * mesh.shape["gy"]
    per_device = functools.partial(on_device_modes, mesh.shape["gx"], mesh.shape["gy"])
    if 2 * count != DEPTH:
        per_device = on_device
    in_specs = (P(None, ("slab", "gx"), "gy"), P(None, ("slab", "gx"), "gy"))
    out_specs = (P(None, ("slab", "gx"), "gy"), P(None, ("slab", "gx"), "gy"))
    return jax.shard_map(
        per_device, mesh=mesh, in_specs=in_specs, out_specs=out_specs, check_vma=False
    )
```

```python
import functools

import jax
import jax.numpy as jnp
import ml_dtypes
import numpy as np
from jax import lax
from jax.experimental import pallas as pl
from jax.experimental.pallas import tpu as pltpu
from jax.sharding import PartitionSpec as P

ITERS = 2


SCREEN = 0.02


def padded(block, sides, width):
    for axis, dim in sides:
        count = lax.axis_size(axis)
        forward = [(i, i + 1) for i in range(count - 1)]
        forward.append((count - 1, 0))
        backward = [(target, source) for source, target in forward]
        low = lax.ppermute(
            lax.slice_in_dim(block, block.shape[dim] - width, None, axis=dim), axis, forward
        )
        high = lax.ppermute(lax.slice_in_dim(block, 0, width, axis=dim), axis, backward)
        block = jnp.concatenate([low, block, high], axis=dim)
    return block


def sine_full(count):
    index = jnp.arange(count).astype(jnp.float32)
    return jnp.sqrt(2.0 / count) * jnp.sin(jnp.pi * jnp.outer(index, index) / count)


def cosine_table(count):
    place = jnp.arange(count).astype(jnp.float32) + 0.5
    order = jnp.arange(count).astype(jnp.float32)
    factor = jnp.where(order == 0.0, jnp.sqrt(1.0 / count), jnp.sqrt(2.0 / count))
    return factor[None, :] * jnp.cos(jnp.pi * jnp.outer(place, order) / count)


def spectrum_table(depth, width, height):
    across = 2.0 - 2.0 * jnp.cos(jnp.pi * jnp.arange(width).astype(jnp.float32) / width)
    along = 2.0 - 2.0 * jnp.cos(jnp.pi * jnp.arange(height).astype(jnp.float32) / height)
    vertical = 2.0 - 2.0 * jnp.cos(jnp.pi * jnp.arange(depth).astype(jnp.float32) / depth)
    return SCREEN + vertical[:, None, None] + across[None, :, None] + along[None, None, :]


def apply_full(field):
    row_rims = jnp.stack([field[:, 0, :], field[:, -1, :]], 1)
    row_ext = padded(row_rims, (("gx", 1),), 1)
    col_rims = jnp.stack([field[:, :, 0], field[:, :, -1]], 0)
    col_ext = padded(col_rims, (("gy", 0),), 1)
    from_below_x = jnp.concatenate([row_ext[:, 0:1, :], field[:, :-1, :]], 1)
    from_above_x = jnp.concatenate([field[:, 1:, :], row_ext[:, 3:4, :]], 1)
    from_below_y = jnp.concatenate([col_ext[0][:, :, None], field[:, :, :-1]], 2)
    from_above_y = jnp.concatenate([field[:, :, 1:], col_ext[3][:, :, None]], 2)
    beside = from_below_x + from_above_x + from_below_y + from_above_y
    upper = jnp.concatenate([field[1:], field[-1:]], 0)
    lower = jnp.concatenate([field[:1], field[:-1]], 0)
    return (6.0 + SCREEN) * field - beside - upper - lower


def solve_interior(field, sines_x, sines_y, cosines, spectrum):
    high = lax.Precision.HIGHEST
    depth, width, height = field.shape
    hat = jnp.dot(field.reshape(depth * width, height), sines_y, precision=high).reshape(
        depth, width, height
    )
    hat = jnp.matmul(sines_x, hat, precision=high)
    hat = jnp.dot(cosines.T, hat.reshape(depth, width * height), precision=high).reshape(
        depth, width, height
    )
    hat = hat / spectrum
    back = jnp.dot(cosines, hat.reshape(depth, width * height), precision=high).reshape(
        depth, width, height
    )
    back = jnp.matmul(sines_x, back, precision=high)
    back = jnp.dot(back.reshape(depth * width, height), sines_y, precision=high)
    return back.reshape(depth, width, height)


def norm_total(residual):
    return lax.psum(jnp.sum(residual * residual), ("gx", "gy"))


def curvature_total(direction, image):
    return lax.psum(jnp.sum(direction * image), ("gx", "gy"))


def on_device(charge, surface_charge):
    depth, width, height = charge.shape
    sines_x = sine_full(width)
    sines_y = sine_full(height)
    cosines = cosine_table(depth)
    spectrum = spectrum_table(depth, width, height)
    row_place = lax.broadcasted_iota(jnp.int32, (1, width, height), 1)
    col_place = lax.broadcasted_iota(jnp.int32, (1, width, height), 2)
    gamma = jnp.where((row_place == 0) | (col_place == 0), 1.0, 0.0).astype(jnp.float32)
    source = charge.at[0].add(surface_charge[0]).at[-1].add(surface_charge[1])
    base = solve_interior(source, sines_x, sines_y, cosines, spectrum)
    reduced = gamma * (source - apply_full(base))
    iterate = jnp.zeros_like(reduced)
    residual = reduced
    direction = reduced
    norm_now = norm_total(residual)
    for step in range(ITERS):
        lifted = -solve_interior(apply_full(direction), sines_x, sines_y, cosines, spectrum)
        image, lifted = (gamma * apply_full(direction + lifted), lifted)
        alpha = norm_now / curvature_total(direction, image)
        iterate = iterate + alpha * direction
        residual = residual - alpha * image
        if step + 1 < ITERS:
            norm_next = norm_total(residual)
            direction = residual + norm_next / norm_now * direction
            norm_now = norm_next
    correction = -solve_interior(apply_full(iterate), sines_x, sines_y, cosines, spectrum)
    potential = iterate + base + correction
    return (potential, residual)


DEPTH, WIDTH, HEIGHT = 32, 64, 128
F32, BF16 = jnp.float32, jnp.bfloat16


def halves(table):
    table = np.asarray(table, np.float64)
    high = table.astype(np.float32).astype(ml_dtypes.bfloat16)
    low = (table - high.astype(np.float64)).astype(np.float32).astype(ml_dtypes.bfloat16)
    return high, low


def sine_unit(count):
    index = np.arange(count)
    table = np.sqrt(2.0 / count) * np.sin(np.pi * np.outer(index, index) / count)
    table[0, 0] = 1.0
    return table


def host_tables():
    place, order = np.arange(DEPTH) + 0.5, np.arange(DEPTH)
    factor = np.where(order == 0, np.sqrt(1.0 / DEPTH), np.sqrt(2.0 / DEPTH))
    cosines = factor[None, :] * np.cos(np.pi * np.outer(place, order) / DEPTH)
    sin_x, sin_y = sine_unit(WIDTH), sine_unit(HEIGHT)
    vertical = 2.0 - 2.0 * np.cos(np.pi * order / DEPTH)
    across = 2.0 - 2.0 * np.cos(np.pi * np.arange(WIDTH) / WIDTH)
    along = 2.0 - 2.0 * np.cos(np.pi * np.arange(HEIGHT) / HEIGHT)
    ux = np.sqrt(2.0 / WIDTH) * np.sin(np.pi * np.arange(WIDTH) / WIDTH)
    uy = np.sqrt(2.0 / HEIGHT) * np.sin(np.pi * np.arange(HEIGHT) / HEIGHT)
    sx = np.where(np.arange(WIDTH) % 2 == 1, 1.0, -1.0)
    sy = np.where(np.arange(HEIGHT) % 2 == 1, 1.0, -1.0)
    sx[0] = sy[0] = 0.0
    ex, ey = np.eye(WIDTH)[0], np.eye(HEIGHT)[0]
    t = {}
    t["zf"] = np.stack(halves(np.kron(cosines.T, np.eye(8))))
    t["zi"] = np.stack(halves(np.kron(cosines, np.eye(8))))
    t["x"] = np.stack(halves(np.kron(np.eye(4), sin_x)))
    t["y"] = np.stack(halves(sin_y))
    plane = SCREEN + across[:, None] + along[None, :]
    t["plane"] = plane.astype(np.float32)
    ur = np.concatenate([np.kron(np.eye(4), (ux + ex)[None]), np.kron(np.eye(4), (ux * sx)[None]), np.zeros((8, 4 * WIDTH))], 0)
    t["ur"] = np.stack(halves(ur))
    uc = np.zeros((16, HEIGHT))
    uc[0], uc[1], uc[2] = uy + ey, uy * sy, ey
    t["uc"] = np.stack(halves(uc))
    spec = plane[None] + vertical[:, None, None]
    inner = np.zeros((WIDTH, HEIGHT))
    inner[1:, 1:] = 1.0
    inv = inner / spec
    t["inv"] = np.where(inner > 0, inv, 1.0).astype(np.float32)
    row_near = np.einsum("a,kab->kb", ux * ux, inv)
    row_far = np.einsum("a,kab->kb", ux * ux * sx, inv)
    col_near = np.einsum("b,kab->ka", uy * uy, inv)
    col_far = np.einsum("b,kab->ka", uy * uy * sy, inv)
    row_coef = SCREEN + vertical[:, None] + 2.0 + along[None, :] - 2.0 * row_near
    col_coef = SCREEN + vertical[:, None] + 2.0 + across[None, :] - 2.0 * col_near
    row_coef[:, 0] = SCREEN + vertical + 4.0
    col_coef[:, 0] = 0.0
    own = np.zeros((DEPTH // 2, 8, HEIGHT))
    own[:, 0], own[:, 1] = row_coef[0::2], row_coef[1::2]
    own[:, 2], own[:, 3] = row_far[0::2], row_far[1::2]
    own[:, 4] = np.concatenate([col_coef[0::2], col_coef[1::2]], 1)
    own[:, 5] = np.concatenate([col_far[0::2], col_far[1::2]], 1)
    own[:, 6], own[:, 7] = vertical[0::2, None], vertical[1::2, None]
    t["own"] = own.astype(np.float32)
    border = np.zeros((WIDTH, HEIGHT))
    border[0], border[:, 0] = uy, ux
    t["pair"] = np.stack([np.outer(ux, uy), border]).astype(np.float32)
    signs = np.zeros((8, HEIGHT))
    signs[0] = sy
    signs[1] = np.concatenate([sx, sx])
    t["signs"] = signs.astype(np.float32)
    zero = np.zeros(WIDTH)
    left = np.zeros((8, HEIGHT))
    left[0], left[1] = np.concatenate([ux + ex, zero]), np.concatenate([zero, ux + ex])
    left[2], left[3] = np.concatenate([ux * sx, zero]), np.concatenate([zero, ux * sx])
    left[6], left[7] = np.concatenate([ex, zero]), np.concatenate([zero, ex])
    right = np.zeros((8, HEIGHT))
    right[4], right[5] = uy + ey, uy * sy
    t["left"], t["right"] = left.astype(np.float32), right.astype(np.float32)
    split = np.concatenate([np.arange(0, DEPTH, 2), np.arange(1, DEPTH, 2)])
    t["cos"] = cosines[split][:, split].astype(np.float32)
    t["sy"] = sin_y.astype(np.float32)
    t["sx2"] = np.kron(np.eye(2), sin_x).astype(np.float32)
    return t


def halved(x):
    high = x.astype(BF16)
    return high, (x - high.astype(F32)).astype(BF16)


def dot(a, b, dims=((1,), (0,))):
    return lax.dot_general(a, b, (dims, ((), ())), preferred_element_type=F32)


def dot3(a, b, dims=((1,), (0,))):
    return dot(a[0], b[0], dims) + (dot(a[0], b[1], dims) + dot(a[1], b[0], dims))


def dot_exact(a, b, dims=((1,), (0,))):
    return lax.dot_general(
        a, b, (dims, ((), ())), precision=lax.Precision.HIGHEST, preferred_element_type=F32
    )


def lane_ids(shape):
    return lax.broadcasted_iota(jnp.int32, shape, len(shape) - 1)


def interior():
    row = lax.broadcasted_iota(jnp.int32, (WIDTH, HEIGHT), 0)
    return (row > 0) & (lane_ids((WIDTH, HEIGHT)) > 0)


def pair_lanes(parts):
    return jnp.concatenate(parts, 1)


def forward_kernel(
    charge_hbm, surface_hbm, z_hbm, x_hbm, y_hbm, ur_hbm, uc_hbm, inv_hbm, base, msg,
    charge, surface, z, x, y, ur, uc, inv, work, sems,
):
    pairs = [(z_hbm, z), (surface_hbm, surface)]
    pairs += [(charge_hbm.at[:, pl.ds(16 * t, 16), :], charge.at[:, pl.ds(16 * t, 16), :]) for t in range(WIDTH // 16)]
    pairs += [(y_hbm, y), (x_hbm, x), (ur_hbm, ur), (uc_hbm, uc)]
    pairs += [(inv_hbm.at[pl.ds(8 * t, 8)], inv.at[pl.ds(8 * t, 8)]) for t in range(DEPTH // 8)]
    copies = [pltpu.make_async_copy(s, d, sems.at[n]) for n, (s, d) in enumerate(pairs)]
    for copy in copies:
        copy.start()
    copies[0].wait()
    copies[1].wait()
    ztab = (z[0], z[1])
    for t in range(WIDTH // 16):
        copies[2 + t].wait()
        sides = []
        for h in range(2):
            at = pl.ds(16 * t + 8 * h, 8)
            block = charge[:, at, :]
            block = jnp.concatenate(
                [block[:1] + surface[0:1, at, :], block[1:-1], block[-1:] + surface[1:2, at, :]], 0
            )
            sides.append(block.reshape(DEPTH * 8, HEIGHT))
        out = dot3(ztab, halved(pair_lanes(sides)))
        if t == 0:
            copies[6].wait()
            ytab = (y[0], y[1])
        for h in range(2):
            side = out[:, HEIGHT * h:HEIGHT * (h + 1)]
            side = dot3(halved(side), ytab)
            work[:, 16 * t + 8 * h:16 * t + 8 * h + 8, :] = side.reshape(DEPTH, 8, HEIGHT)
    for copy in copies[7:10]:
        copy.wait()
    xtab, utab, ctab = (x[0], x[1]), (ur[0], ur[1]), (uc[0], uc[1])
    inner = interior()
    lane = lane_ids((8, HEIGHT))
    for t in range(DEPTH // 8):
        copies[10 + t].wait()
        sides = [work[8 * t + 4 * h:8 * t + 4 * h + 4].reshape(4 * WIDTH, HEIGHT) for h in range(2)]
        out = dot3(xtab, halved(pair_lanes(sides)))
        for h in range(2):
            side = out[:, HEIGHT * h:HEIGHT * (h + 1)].reshape(4, WIDTH, HEIGHT)
            full = []
            corner = []
            for s in range(4):
                k = 8 * t + 4 * h + s
                one = side[s] * inv[k]
                base[k] = jnp.where(inner, one, 0.0)
                full.append(one)
                corner.append(one[0:1])
            full = jnp.concatenate(full, 0)
            parts = halved(full)
            rows = dot3(utab, parts)
            own = jnp.concatenate(corner + [jnp.zeros((4, HEIGHT), F32)], 0)
            rows = jnp.where(lane == 0, own, rows[:8])
            cols = dot3(ctab, parts, ((1,), (1,)))
            first = lane_ids((1, 4 * WIDTH)) % WIDTH == 0
            near = jnp.where(first, cols[2:3], cols[0:1])
            far = jnp.where(first, 0.0, cols[1:2])
            for g in range(2):
                at = slice(HEIGHT * g, HEIGHT * (g + 1))
                msg[4 * t + 2 * h + g] = jnp.concatenate(
                    [rows[2 * g:2 * g + 2], rows[4 + 2 * g:6 + 2 * g], near[:, at], far[:, at], jnp.zeros((2, HEIGHT), F32)],
                    0,
                )


def shift_x(n_gx, n_gy, field, by):
    cut = (by % n_gx) * n_gy
    return jnp.concatenate([field[cut:], field[:cut]], 0)


def shift_y(n_gx, n_gy, field, by):
    place = lax.broadcasted_iota(jnp.int32, field.shape, 0) % n_gy
    count = n_gx * n_gy
    ahead = by % count
    plain = jnp.concatenate([field[ahead:], field[:ahead]], 0)
    wrap = (by - n_gy if by > 0 else by + n_gy) % count
    wrapped = jnp.concatenate([field[wrap:], field[:wrap]], 0)
    edge = n_gy - 1 if by > 0 else 0
    return jnp.where(place == edge, wrapped, plain)


def turn_half(x):
    return jnp.concatenate([x[:, WIDTH:], x[:, :WIDTH]], 1)


def schur_modes(n_gx, n_gy, coef, table, row, col):
    row_coef, row_far, col_coef, col_far, row_sign, col_sign = coef
    sx = functools.partial(shift_x, n_gx, n_gy)
    sy = functools.partial(shift_y, n_gx, n_gy)
    count = n_gx * n_gy
    across = dot_exact(jnp.concatenate([col, col * col_sign], 0), table)
    along = dot_exact(jnp.concatenate([row, row * row_sign], 0), table, ((1,), (1,)))
    v = across[:count] + sx(across[count:], -1)
    w = along[:count] + sy(along[count:], -1)
    row_out = row_coef * row - row_far * (sx(row, 1) + sx(row, -1)) - v - row_sign * sy(v, 1)
    col_out = col_coef * col - col_far * (sy(col, 1) + sy(col, -1)) - w - col_sign * sx(w, 1)
    lane = lane_ids((count, HEIGHT))
    row_out = row_out - jnp.concatenate(
        [jnp.where(lane == 0, w, 0.0), jnp.where(lane == 0, turn_half(w), 0.0)], 1
    )
    col_out = jnp.where(
        lane == 0, row_out[:, :HEIGHT], jnp.where(lane == WIDTH, turn_half(row_out[:, HEIGHT:]), col_out)
    )
    return row_out, col_out


def owner_tables(own, pair, signs):
    inner = interior()
    parts = []
    for s in range(2):
        one = jnp.where(inner, pair[0] / (pair[2] + own[6 + s:7 + s]), pair[1])
        parts.append(one)
    blank = jnp.zeros((WIDTH, HEIGHT), F32)
    table = jnp.concatenate([pair_lanes([parts[0], blank]), pair_lanes([blank, parts[1]])], 0)
    coef = (
        pair_lanes([own[0:1], own[1:2]]),
        pair_lanes([own[2:3], own[3:4]]),
        own[4:5],
        own[5:6],
        pair_lanes([signs[0:1], signs[0:1]]),
        signs[1:2],
    )
    return coef, table


def start_modes(n_gx, n_gy, fields):
    sx = functools.partial(shift_x, n_gx, n_gy)
    sy = functools.partial(shift_y, n_gx, n_gy)
    row = pair_lanes([fields[0], fields[1]]) + sx(pair_lanes([fields[2], fields[3]]), -1)
    col = fields[4] + sy(fields[5], -1)
    return row, col


def inner_product(first, second):
    lane = lane_ids(first[1].shape)
    cols = jnp.where(lane % WIDTH == 0, 0.0, first[1] * second[1])
    rows = first[0] * second[0]
    return jnp.sum(rows[:, :HEIGHT] + rows[:, HEIGHT:] + cols)


def face_fields(n_gx, n_gy, pair):
    row, col = pair
    beyond = shift_x(n_gx, n_gy, row, 1)
    return [
        row[:, :HEIGHT], row[:, HEIGHT:], beyond[:, :HEIGHT], beyond[:, HEIGHT:],
        col, shift_y(n_gx, n_gy, col, 1),
    ]


def steps(sums):
    rr, rw, ww, wv = sums
    alpha = rr / rw
    after = alpha * alpha * ww - rr
    beta = after / rr
    curve = (1 + beta) * (1 + beta) * rw - 2 * (1 + beta) * alpha * ww + alpha * alpha * wv
    second = after / curve
    return alpha + second * (1 + beta), -second * alpha


def exchange_kernel(n_gx, n_gy, msg, own_ref, pair_ref, signs_ref, faces, rest, got, back_r, back_w, back_v, landed_r, landed_w, landed_v, sems):
    count = n_gx * n_gy
    gx, gy = lax.axis_index("gx"), lax.axis_index("gy")
    me = gx * n_gy + gy

    def partner(off):
        to = lax.rem(me + off, count)
        return to, {"gx": lax.div(to, n_gy), "gy": lax.rem(to, n_gy)}

    barrier = pltpu.get_barrier_semaphore()
    for off in range(1, count):
        pl.semaphore_signal(barrier, inc=1, device_id=partner(off)[1], device_id_type=pl.DeviceIdType.MESH)
    coef, table = owner_tables(own_ref[me], pair_ref[...], signs_ref[...])
    pl.semaphore_wait(barrier, count - 1)

    def spread(source, target, which):
        copies = []
        for off in range(1, count):
            to, device = partner(off)
            copies.append(
                pltpu.make_async_remote_copy(
                    src_ref=source.at[to],
                    dst_ref=target.at[me],
                    send_sem=sems.at[which, 0, off],
                    recv_sem=sems.at[which, 1, off],
                    device_id=device,
                    device_id_type=pl.DeviceIdType.MESH,
                )
            )
            copies[-1].start()
        target[me] = source[me]
        return copies

    first = spread(msg, got, 0)
    for copy in first:
        copy.wait_recv()
    fields = [got[:, f, :] for f in range(6)]
    r = start_modes(n_gx, n_gy, fields)
    for f, field in enumerate(face_fields(n_gx, n_gy, r)):
        back_r[:, f, :] = field
    second = spread(back_r, landed_r, 1)
    w = schur_modes(n_gx, n_gy, coef, table, *r)
    for f, field in enumerate(face_fields(n_gx, n_gy, w)):
        back_w[:, f, :] = field
    second += spread(back_w, landed_w, 2)
    v = schur_modes(n_gx, n_gy, coef, table, *w)
    back_v[:, 0, :] = v[0][:, :HEIGHT]
    back_v[:, 1, :] = v[0][:, HEIGHT:]
    back_v[:, 2, :] = v[1]
    sums = (inner_product(r, r), inner_product(r, w), inner_product(w, w), inner_product(w, v))
    lane = lane_ids((count, HEIGHT))
    back_v[:, 3, :] = sum(jnp.where(lane == s, value, 0.0) for s, value in enumerate(sums))
    second += spread(back_v, landed_v, 3)
    for copy in second:
        copy.wait_recv()
    for copy in first + second:
        copy.wait_send()
    faces[...], rest[...] = combine(landed_r[...], landed_w[...], landed_v[...])


def combine(r, w, v):
    total = jnp.sum(v[:, 3:4, :], 0)
    lane = lane_ids((1, HEIGHT))
    c0, c1 = steps([jnp.sum(jnp.where(lane == s, total, 0.0)) for s in range(4)])
    sub = lax.broadcasted_iota(jnp.int32, r.shape, 1)
    r = jnp.where(sub < 6, r, 0.0)
    w = jnp.where(sub < 6, w, 0.0)
    lead = r - c0 * w
    rest = jnp.concatenate(
        [lead[:, 0:2] - c1 * v[:, 0:2], lead[:, 4:5] - c1 * v[:, 2:3], jnp.zeros_like(r[:, :5])], 1
    )
    return c0 * r + c1 * w, rest


def stacked(left, right):
    lh, ll = halved(left)
    rh, rl = halved(right)
    lhs = jnp.concatenate([lh.astype(F32), lh.astype(F32), ll.astype(F32)], 0).astype(BF16)
    rhs = jnp.concatenate([rh.astype(F32), rl.astype(F32), rh.astype(F32)], 0).astype(BF16)
    return dot(lhs, rhs, ((0,), (0,)))


def inverse_kernel(base, faces, rest, left, right, z, x, y, inv, cos, sin_y, sin_x2, potential, residual, work):
    ztab, xtab, ytab = (z[0], z[1]), (x[0], x[1]), (y[0], y[1])
    lane = lane_ids((8, HEIGHT))
    sub = lax.broadcasted_iota(jnp.int32, (8, HEIGHT), 0)
    const_left, const_right = left[...], right[...]
    for t in range(DEPTH // 8):
        sides = []
        for h in range(2):
            blocks = []
            for g in range(2):
                o = 4 * t + 2 * h + g
                one = faces[o]
                lhs = jnp.where((sub >= 4) & (sub < 6) & (lane % WIDTH > 0), one, const_left)
                up = jnp.concatenate([one[2:], one[:2]], 0)
                rhs = jnp.where((sub < 4) & (lane > 0), one, const_right)
                rhs = jnp.where((sub >= 6) & (lane == 0), up, rhs)
                out = stacked(lhs, rhs)
                for s in range(2):
                    k = 2 * o + s
                    blocks.append(out[WIDTH * s:WIDTH * (s + 1)] * inv[k] + base[k])
            sides.append(jnp.concatenate(blocks, 0))
        out = dot3(xtab, halved(pair_lanes(sides)))
        for h in range(2):
            side = dot3(halved(out[:, HEIGHT * h:HEIGHT * (h + 1)]), ytab)
            work[8 * t + 4 * h:8 * t + 4 * h + 4] = side.reshape(4, WIDTH, HEIGHT)
    for t in range(WIDTH // 16):
        sides = [work[:, 16 * t + 8 * h:16 * t + 8 * h + 8, :].reshape(DEPTH * 8, HEIGHT) for h in range(2)]
        out = dot3(ztab, halved(pair_lanes(sides)))
        for h in range(2):
            side = out[:, HEIGHT * h:HEIGHT * (h + 1)]
            potential[:, 16 * t + 8 * h:16 * t + 8 * h + 8, :] = side.reshape(DEPTH, 8, HEIGHT)
    half = DEPTH // 2
    rows = jnp.concatenate([rest[:, 0, :], rest[:, 1, :]], 0)
    rows = dot_exact(cos[...], dot_exact(rows, sin_y[...]))
    cols = dot_exact(rest[:, 2, :], sin_x2[...])
    cols = dot_exact(cos[...], jnp.concatenate([cols[:, :WIDTH], cols[:, WIDTH:]], 0))
    cols = jnp.concatenate([cols[:half], cols[half:]], 1)
    cols = jnp.where(lane_ids((half, HEIGHT)) % WIDTH == 0, 0.0, cols)
    unit = jnp.where(lane == 0, 1.0, 0.0)
    mark = jnp.where(((sub == 0) & (lane == 0)) | ((sub == 1) & (lane == WIDTH)), 1.0, 0.0)
    for o in range(half):
        lhs = jnp.where(sub == 2, cols[o:o + 1], mark)
        rhs = jnp.where(sub == 0, rows[o:o + 1], jnp.where(sub == 1, rows[half + o:half + o + 1], jnp.where(sub == 2, unit, 0.0)))
        out = stacked(lhs, rhs)
        residual[2 * o] = out[:WIDTH]
        residual[2 * o + 1] = out[WIDTH:]


def on_device_modes(n_gx, n_gy, charge, surface_charge):
    t = host_tables()
    count = n_gx * n_gy
    block = jax.ShapeDtypeStruct(charge.shape, F32)
    small = jax.ShapeDtypeStruct((count, 8, HEIGHT), F32)
    params = dict(vmem_limit_bytes=48 * 1024 * 1024)
    hbm = pl.BlockSpec(memory_space=pltpu.HBM)
    base, msg = pl.pallas_call(
        forward_kernel,
        out_shape=(block, small),
        in_specs=[hbm] * 8,
        scratch_shapes=[
            pltpu.VMEM(charge.shape, F32),
            pltpu.VMEM(surface_charge.shape, F32),
            pltpu.VMEM(t["zf"].shape, BF16),
            pltpu.VMEM(t["x"].shape, BF16),
            pltpu.VMEM(t["y"].shape, BF16),
            pltpu.VMEM(t["ur"].shape, BF16),
            pltpu.VMEM(t["uc"].shape, BF16),
            pltpu.VMEM(charge.shape, F32),
            pltpu.VMEM(charge.shape, F32),
            pltpu.SemaphoreType.DMA((14,)),
        ],
        compiler_params=pltpu.CompilerParams(**params),
        name="forward",
    )(charge, surface_charge, t["zf"], t["x"], t["y"], t["ur"], t["uc"], t["inv"])
    pair = np.concatenate([t["pair"], t["plane"][None]], 0)
    eight, four = (count, 8, HEIGHT), (count, 4, HEIGHT)
    faces, rest = pl.pallas_call(
        functools.partial(exchange_kernel, n_gx, n_gy),
        out_shape=(small, small),
        scratch_shapes=[pltpu.VMEM(shape, F32) for shape in (eight, eight, eight, four, eight, eight, four)]
        + [pltpu.SemaphoreType.DMA((4, 2, count))],
        in_specs=[pl.BlockSpec(memory_space=pltpu.VMEM)] * 4,
        compiler_params=pltpu.CompilerParams(collective_id=0, has_side_effects=True, **params),
        name="exchange",
    )(msg, t["own"], pair, t["signs"])
    return pl.pallas_call(
        inverse_kernel,
        out_shape=(block, block),
        scratch_shapes=[pltpu.VMEM(charge.shape, F32)],
        compiler_params=pltpu.CompilerParams(**params),
        name="inverse",
    )(base, faces, rest, t["left"], t["right"], t["zi"], t["x"], t["y"], t["inv"], t["cos"], t["sy"], t["sx2"])


def solution(mesh):
    count = mesh.shape["gx"] * mesh.shape["gy"]
    per_device = functools.partial(on_device_modes, mesh.shape["gx"], mesh.shape["gy"])
    if 2 * count != DEPTH:
        per_device = on_device
    in_specs = (P(None, ("slab", "gx"), "gy"), P(None, ("slab", "gx"), "gy"))
    out_specs = (P(None, ("slab", "gx"), "gy"), P(None, ("slab", "gx"), "gy"))
    return jax.shard_map(
        per_device, mesh=mesh, in_specs=in_specs, out_specs=out_specs, check_vma=False
    )
```

```python
import functools

import jax
import jax.numpy as jnp
import ml_dtypes
import numpy as np
from jax import lax
from jax.experimental import pallas as pl
from jax.experimental.pallas import tpu as pltpu
from jax.sharding import PartitionSpec as P

ITERS = 2


SCREEN = 0.02


def padded(block, sides, width):
    for axis, dim in sides:
        count = lax.axis_size(axis)
        forward = [(i, i + 1) for i in range(count - 1)]
        forward.append((count - 1, 0))
        backward = [(target, source) for source, target in forward]
        low = lax.ppermute(
            lax.slice_in_dim(block, block.shape[dim] - width, None, axis=dim), axis, forward
        )
        high = lax.ppermute(lax.slice_in_dim(block, 0, width, axis=dim), axis, backward)
        block = jnp.concatenate([low, block, high], axis=dim)
    return block


def sine_full(count):
    index = jnp.arange(count).astype(jnp.float32)
    return jnp.sqrt(2.0 / count) * jnp.sin(jnp.pi * jnp.outer(index, index) / count)


def cosine_table(count):
    place = jnp.arange(count).astype(jnp.float32) + 0.5
    order = jnp.arange(count).astype(jnp.float32)
    factor = jnp.where(order == 0.0, jnp.sqrt(1.0 / count), jnp.sqrt(2.0 / count))
    return factor[None, :] * jnp.cos(jnp.pi * jnp.outer(place, order) / count)


def spectrum_table(depth, width, height):
    across = 2.0 - 2.0 * jnp.cos(jnp.pi * jnp.arange(width).astype(jnp.float32) / width)
    along = 2.0 - 2.0 * jnp.cos(jnp.pi * jnp.arange(height).astype(jnp.float32) / height)
    vertical = 2.0 - 2.0 * jnp.cos(jnp.pi * jnp.arange(depth).astype(jnp.float32) / depth)
    return SCREEN + vertical[:, None, None] + across[None, :, None] + along[None, None, :]


def apply_full(field):
    row_rims = jnp.stack([field[:, 0, :], field[:, -1, :]], 1)
    row_ext = padded(row_rims, (("gx", 1),), 1)
    col_rims = jnp.stack([field[:, :, 0], field[:, :, -1]], 0)
    col_ext = padded(col_rims, (("gy", 0),), 1)
    from_below_x = jnp.concatenate([row_ext[:, 0:1, :], field[:, :-1, :]], 1)
    from_above_x = jnp.concatenate([field[:, 1:, :], row_ext[:, 3:4, :]], 1)
    from_below_y = jnp.concatenate([col_ext[0][:, :, None], field[:, :, :-1]], 2)
    from_above_y = jnp.concatenate([field[:, :, 1:], col_ext[3][:, :, None]], 2)
    beside = from_below_x + from_above_x + from_below_y + from_above_y
    upper = jnp.concatenate([field[1:], field[-1:]], 0)
    lower = jnp.concatenate([field[:1], field[:-1]], 0)
    return (6.0 + SCREEN) * field - beside - upper - lower


def solve_interior(field, sines_x, sines_y, cosines, spectrum):
    high = lax.Precision.HIGHEST
    depth, width, height = field.shape
    hat = jnp.dot(field.reshape(depth * width, height), sines_y, precision=high).reshape(
        depth, width, height
    )
    hat = jnp.matmul(sines_x, hat, precision=high)
    hat = jnp.dot(cosines.T, hat.reshape(depth, width * height), precision=high).reshape(
        depth, width, height
    )
    hat = hat / spectrum
    back = jnp.dot(cosines, hat.reshape(depth, width * height), precision=high).reshape(
        depth, width, height
    )
    back = jnp.matmul(sines_x, back, precision=high)
    back = jnp.dot(back.reshape(depth * width, height), sines_y, precision=high)
    return back.reshape(depth, width, height)


def norm_total(residual):
    return lax.psum(jnp.sum(residual * residual), ("gx", "gy"))


def curvature_total(direction, image):
    return lax.psum(jnp.sum(direction * image), ("gx", "gy"))


def on_device(charge, surface_charge):
    depth, width, height = charge.shape
    sines_x = sine_full(width)
    sines_y = sine_full(height)
    cosines = cosine_table(depth)
    spectrum = spectrum_table(depth, width, height)
    row_place = lax.broadcasted_iota(jnp.int32, (1, width, height), 1)
    col_place = lax.broadcasted_iota(jnp.int32, (1, width, height), 2)
    gamma = jnp.where((row_place == 0) | (col_place == 0), 1.0, 0.0).astype(jnp.float32)
    source = charge.at[0].add(surface_charge[0]).at[-1].add(surface_charge[1])
    base = solve_interior(source, sines_x, sines_y, cosines, spectrum)
    reduced = gamma * (source - apply_full(base))
    iterate = jnp.zeros_like(reduced)
    residual = reduced
    direction = reduced
    norm_now = norm_total(residual)
    for step in range(ITERS):
        lifted = -solve_interior(apply_full(direction), sines_x, sines_y, cosines, spectrum)
        image, lifted = (gamma * apply_full(direction + lifted), lifted)
        alpha = norm_now / curvature_total(direction, image)
        iterate = iterate + alpha * direction
        residual = residual - alpha * image
        if step + 1 < ITERS:
            norm_next = norm_total(residual)
            direction = residual + norm_next / norm_now * direction
            norm_now = norm_next
    correction = -solve_interior(apply_full(iterate), sines_x, sines_y, cosines, spectrum)
    potential = iterate + base + correction
    return (potential, residual)


DEPTH, WIDTH, HEIGHT = 32, 64, 128
F32, BF16 = jnp.float32, jnp.bfloat16


def halves(table):
    table = np.asarray(table, np.float64)
    high = table.astype(np.float32).astype(ml_dtypes.bfloat16)
    low = (table - high.astype(np.float64)).astype(np.float32).astype(ml_dtypes.bfloat16)
    return high, low


def sine_unit(count):
    index = np.arange(count)
    table = np.sqrt(2.0 / count) * np.sin(np.pi * np.outer(index, index) / count)
    table[0, 0] = 1.0
    return table


def host_tables():
    place, order = np.arange(DEPTH) + 0.5, np.arange(DEPTH)
    factor = np.where(order == 0, np.sqrt(1.0 / DEPTH), np.sqrt(2.0 / DEPTH))
    cosines = factor[None, :] * np.cos(np.pi * np.outer(place, order) / DEPTH)
    sin_x, sin_y = sine_unit(WIDTH), sine_unit(HEIGHT)
    vertical = 2.0 - 2.0 * np.cos(np.pi * order / DEPTH)
    across = 2.0 - 2.0 * np.cos(np.pi * np.arange(WIDTH) / WIDTH)
    along = 2.0 - 2.0 * np.cos(np.pi * np.arange(HEIGHT) / HEIGHT)
    ux = np.sqrt(2.0 / WIDTH) * np.sin(np.pi * np.arange(WIDTH) / WIDTH)
    uy = np.sqrt(2.0 / HEIGHT) * np.sin(np.pi * np.arange(HEIGHT) / HEIGHT)
    sx = np.where(np.arange(WIDTH) % 2 == 1, 1.0, -1.0)
    sy = np.where(np.arange(HEIGHT) % 2 == 1, 1.0, -1.0)
    sx[0] = sy[0] = 0.0
    ex, ey = np.eye(WIDTH)[0], np.eye(HEIGHT)[0]
    t = {}
    t["zf"] = np.stack(halves(np.kron(cosines.T, np.eye(8))))
    t["zi"] = np.stack(halves(np.kron(cosines, np.eye(8))))
    t["x"] = np.stack(halves(np.kron(np.eye(4), sin_x)))
    t["y"] = np.stack(halves(sin_y))
    plane = SCREEN + across[:, None] + along[None, :]
    t["plane"] = plane.astype(np.float32)
    ur = np.concatenate([np.kron(np.eye(4), (ux + ex)[None]), np.kron(np.eye(4), (ux * sx)[None]), np.zeros((8, 4 * WIDTH))], 0)
    t["ur"] = np.stack(halves(ur))
    uc = np.zeros((16, HEIGHT))
    uc[0], uc[1], uc[2] = uy + ey, uy * sy, ey
    t["uc"] = np.stack(halves(uc))
    spec = plane[None] + vertical[:, None, None]
    inner = np.zeros((WIDTH, HEIGHT))
    inner[1:, 1:] = 1.0
    inv = inner / spec
    t["inv"] = np.where(inner > 0, inv, 1.0).astype(np.float32)
    row_near = np.einsum("a,kab->kb", ux * ux, inv)
    row_far = np.einsum("a,kab->kb", ux * ux * sx, inv)
    col_near = np.einsum("b,kab->ka", uy * uy, inv)
    col_far = np.einsum("b,kab->ka", uy * uy * sy, inv)
    row_coef = SCREEN + vertical[:, None] + 2.0 + along[None, :] - 2.0 * row_near
    col_coef = SCREEN + vertical[:, None] + 2.0 + across[None, :] - 2.0 * col_near
    row_coef[:, 0] = SCREEN + vertical + 4.0
    col_coef[:, 0] = 0.0
    own = np.zeros((DEPTH // 2, 8, HEIGHT))
    own[:, 0], own[:, 1] = row_coef[0::2], row_coef[1::2]
    own[:, 2], own[:, 3] = row_far[0::2], row_far[1::2]
    own[:, 4] = np.concatenate([col_coef[0::2], col_coef[1::2]], 1)
    own[:, 5] = np.concatenate([col_far[0::2], col_far[1::2]], 1)
    own[:, 6], own[:, 7] = vertical[0::2, None], vertical[1::2, None]
    t["own"] = own.astype(np.float32)
    border = np.zeros((WIDTH, HEIGHT))
    border[0], border[:, 0] = uy, ux
    t["pair"] = np.stack([np.outer(ux, uy), border]).astype(np.float32)
    signs = np.zeros((8, HEIGHT))
    signs[0] = sy
    signs[1] = np.concatenate([sx, sx])
    t["signs"] = signs.astype(np.float32)
    zero = np.zeros(WIDTH)
    left = np.zeros((8, HEIGHT))
    left[0], left[1] = np.concatenate([ux + ex, zero]), np.concatenate([zero, ux + ex])
    left[2], left[3] = np.concatenate([ux * sx, zero]), np.concatenate([zero, ux * sx])
    left[6], left[7] = np.concatenate([ex, zero]), np.concatenate([zero, ex])
    right = np.zeros((8, HEIGHT))
    right[4], right[5] = uy + ey, uy * sy
    t["left"], t["right"] = left.astype(np.float32), right.astype(np.float32)
    split = np.concatenate([np.arange(0, DEPTH, 2), np.arange(1, DEPTH, 2)])
    t["cos"] = cosines[split][:, split].astype(np.float32)
    t["sy"] = sin_y.astype(np.float32)
    t["sx2"] = np.kron(np.eye(2), sin_x).astype(np.float32)
    return t


def halved(x):
    high = x.astype(BF16)
    return high, (x - high.astype(F32)).astype(BF16)


def dot(a, b, dims=((1,), (0,))):
    return lax.dot_general(a, b, (dims, ((), ())), preferred_element_type=F32)


def dot3(a, b, dims=((1,), (0,))):
    return dot(a[0], b[0], dims) + (dot(a[0], b[1], dims) + dot(a[1], b[0], dims))


def dot_exact(a, b, dims=((1,), (0,))):
    return lax.dot_general(
        a, b, (dims, ((), ())), precision=lax.Precision.HIGHEST, preferred_element_type=F32
    )


def lane_ids(shape):
    return lax.broadcasted_iota(jnp.int32, shape, len(shape) - 1)


def interior():
    row = lax.broadcasted_iota(jnp.int32, (WIDTH, HEIGHT), 0)
    return (row > 0) & (lane_ids((WIDTH, HEIGHT)) > 0)


def pair_lanes(parts):
    return jnp.concatenate(parts, 1)


def shift_x(n_gx, n_gy, field, by):
    cut = (by % n_gx) * n_gy
    return jnp.concatenate([field[cut:], field[:cut]], 0)


def shift_y(n_gx, n_gy, field, by):
    place = lax.broadcasted_iota(jnp.int32, field.shape, 0) % n_gy
    count = n_gx * n_gy
    ahead = by % count
    plain = jnp.concatenate([field[ahead:], field[:ahead]], 0)
    wrap = (by - n_gy if by > 0 else by + n_gy) % count
    wrapped = jnp.concatenate([field[wrap:], field[:wrap]], 0)
    edge = n_gy - 1 if by > 0 else 0
    return jnp.where(place == edge, wrapped, plain)


def turn_half(x):
    return jnp.concatenate([x[:, WIDTH:], x[:, :WIDTH]], 1)


def schur_modes(n_gx, n_gy, coef, table, row, col):
    row_coef, row_far, col_coef, col_far, row_sign, col_sign = coef
    sx = functools.partial(shift_x, n_gx, n_gy)
    sy = functools.partial(shift_y, n_gx, n_gy)
    count = n_gx * n_gy
    across = dot_exact(jnp.concatenate([col, col * col_sign], 0), table)
    along = dot_exact(jnp.concatenate([row, row * row_sign], 0), table, ((1,), (1,)))
    v = across[:count] + sx(across[count:], -1)
    w = along[:count] + sy(along[count:], -1)
    row_out = row_coef * row - row_far * (sx(row, 1) + sx(row, -1)) - v - row_sign * sy(v, 1)
    col_out = col_coef * col - col_far * (sy(col, 1) + sy(col, -1)) - w - col_sign * sx(w, 1)
    lane = lane_ids((count, HEIGHT))
    row_out = row_out - jnp.concatenate(
        [jnp.where(lane == 0, w, 0.0), jnp.where(lane == 0, turn_half(w), 0.0)], 1
    )
    col_out = jnp.where(
        lane == 0, row_out[:, :HEIGHT], jnp.where(lane == WIDTH, turn_half(row_out[:, HEIGHT:]), col_out)
    )
    return row_out, col_out


def owner_tables(own, pair, signs):
    inner = interior()
    parts = []
    for s in range(2):
        one = jnp.where(inner, pair[0] / (pair[2] + own[6 + s:7 + s]), pair[1])
        parts.append(one)
    blank = jnp.zeros((WIDTH, HEIGHT), F32)
    table = jnp.concatenate([pair_lanes([parts[0], blank]), pair_lanes([blank, parts[1]])], 0)
    coef = (
        pair_lanes([own[0:1], own[1:2]]),
        pair_lanes([own[2:3], own[3:4]]),
        own[4:5],
        own[5:6],
        pair_lanes([signs[0:1], signs[0:1]]),
        signs[1:2],
    )
    return coef, table


def start_modes(n_gx, n_gy, fields):
    sx = functools.partial(shift_x, n_gx, n_gy)
    sy = functools.partial(shift_y, n_gx, n_gy)
    row = pair_lanes([fields[0], fields[1]]) + sx(pair_lanes([fields[2], fields[3]]), -1)
    col = fields[4] + sy(fields[5], -1)
    return row, col


def inner_product(first, second):
    lane = lane_ids(first[1].shape)
    cols = jnp.where(lane % WIDTH == 0, 0.0, first[1] * second[1])
    rows = first[0] * second[0]
    return jnp.sum(rows[:, :HEIGHT] + rows[:, HEIGHT:] + cols)


def face_fields(n_gx, n_gy, pair):
    row, col = pair
    beyond = shift_x(n_gx, n_gy, row, 1)
    return [
        row[:, :HEIGHT], row[:, HEIGHT:], beyond[:, :HEIGHT], beyond[:, HEIGHT:],
        col, shift_y(n_gx, n_gy, col, 1),
    ]


def steps(sums):
    rr, rw, ww, wv = sums
    alpha = rr / rw
    after = alpha * alpha * ww - rr
    beta = after / rr
    curve = (1 + beta) * (1 + beta) * rw - 2 * (1 + beta) * alpha * ww + alpha * alpha * wv
    second = after / curve
    return alpha + second * (1 + beta), -second * alpha


def face_kernel(
    n_gx, n_gy,
    charge_hbm, surface_hbm, z_hbm, x_hbm, y_hbm, ur_hbm, uc_hbm, inv_hbm, own_hbm, pair_hbm, signs_hbm,
    base_hbm, faces,
    charge, surface, z, x, y, ur, uc, inv, own_ref, pair_ref, signs_ref,
    work, base, msg, got, back, landed, load_sems, store_sems, sems,
):
    count = n_gx * n_gy
    gx, gy = lax.axis_index("gx"), lax.axis_index("gy")
    me = gx * n_gy + gy
    pairs = [(z_hbm, z), (surface_hbm, surface)]
    pairs += [(charge_hbm.at[:, pl.ds(16 * t, 16), :], charge.at[:, pl.ds(16 * t, 16), :]) for t in range(WIDTH // 16)]
    pairs += [(y_hbm, y), (x_hbm, x), (ur_hbm, ur), (uc_hbm, uc)]
    pairs += [(inv_hbm.at[pl.ds(8 * t, 8)], inv.at[pl.ds(8 * t, 8)]) for t in range(DEPTH // 8)]
    pairs += [(own_hbm, own_ref), (pair_hbm, pair_ref), (signs_hbm, signs_ref)]
    copies = [pltpu.make_async_copy(s, d, load_sems.at[n]) for n, (s, d) in enumerate(pairs)]
    for copy in copies:
        copy.start()

    def partner(off):
        to = lax.rem(me + off, count)
        return to, {"gx": lax.div(to, n_gy), "gy": lax.rem(to, n_gy)}

    barrier = pltpu.get_barrier_semaphore()
    for off in range(1, count):
        pl.semaphore_signal(barrier, inc=1, device_id=partner(off)[1], device_id_type=pl.DeviceIdType.MESH)
    copies[0].wait()
    copies[1].wait()
    ztab = (z[0], z[1])
    for t in range(WIDTH // 16):
        copies[2 + t].wait()
        sides = []
        for h in range(2):
            at = pl.ds(16 * t + 8 * h, 8)
            block = charge[:, at, :]
            block = jnp.concatenate(
                [block[:1] + surface[0:1, at, :], block[1:-1], block[-1:] + surface[1:2, at, :]], 0
            )
            sides.append(block.reshape(DEPTH * 8, HEIGHT))
        out = dot3(ztab, halved(pair_lanes(sides)))
        if t == 0:
            copies[6].wait()
            ytab = (y[0], y[1])
        for h in range(2):
            side = out[:, HEIGHT * h:HEIGHT * (h + 1)]
            side = dot3(halved(side), ytab)
            work[:, 16 * t + 8 * h:16 * t + 8 * h + 8, :] = side.reshape(DEPTH, 8, HEIGHT)
    for copy in copies[7:10]:
        copy.wait()
    xtab, utab, ctab = (x[0], x[1]), (ur[0], ur[1]), (uc[0], uc[1])
    inner = interior()
    lane = lane_ids((8, HEIGHT))
    pl.semaphore_wait(barrier, count - 1)
    stores = []
    first = [
        pltpu.make_async_remote_copy(
            src_ref=msg.at[to],
            dst_ref=got.at[me],
            send_sem=sems.at[0, 0, to],
            recv_sem=sems.at[0, 1, me],
            device_id={"gx": to // n_gy, "gy": to % n_gy},
            device_id_type=pl.DeviceIdType.MESH,
        )
        for to in range(count)
    ]
    for t in range(DEPTH // 8):
        copies[10 + t].wait()
        sides = [work[8 * t + 4 * h:8 * t + 4 * h + 4].reshape(4 * WIDTH, HEIGHT) for h in range(2)]
        out = dot3(xtab, halved(pair_lanes(sides)))
        for h in range(2):
            side = out[:, HEIGHT * h:HEIGHT * (h + 1)].reshape(4, WIDTH, HEIGHT)
            full = []
            corner = []
            for s in range(4):
                k = 8 * t + 4 * h + s
                one = side[s] * inv[k]
                base[k] = jnp.where(inner, one, 0.0)
                full.append(one)
                corner.append(one[0:1])
            full = jnp.concatenate(full, 0)
            parts = halved(full)
            rows = dot3(utab, parts)
            own = jnp.concatenate(corner + [jnp.zeros((4, HEIGHT), F32)], 0)
            rows = jnp.where(lane == 0, own, rows[:8])
            cols = dot3(ctab, parts, ((1,), (1,)))
            edge = lane_ids((1, 4 * WIDTH)) % WIDTH == 0
            near = jnp.where(edge, cols[2:3], cols[0:1])
            far = jnp.where(edge, 0.0, cols[1:2])
            for g in range(2):
                at = slice(HEIGHT * g, HEIGHT * (g + 1))
                msg[4 * t + 2 * h + g] = jnp.concatenate(
                    [rows[2 * g:2 * g + 2], rows[4 + 2 * g:6 + 2 * g], near[:, at], far[:, at], jnp.zeros((2, HEIGHT), F32)],
                    0,
                )
        stores.append(
            pltpu.make_async_copy(base.at[pl.ds(8 * t, 8)], base_hbm.at[pl.ds(8 * t, 8)], store_sems.at[t])
        )
        stores[-1].start()
        for to in range(4 * t, 4 * t + 4):
            pl.when(me != to)(first[to].start)
    for copy in copies[14:]:
        copy.wait()
    coef, table = owner_tables(own_ref[me], pair_ref[...], signs_ref[...])
    got[me] = msg[me]
    for source in range(count):
        arrival = pltpu.make_async_remote_copy(
            src_ref=msg.at[source],
            dst_ref=got.at[source],
            send_sem=sems.at[0, 0, source],
            recv_sem=sems.at[0, 1, source],
            device_id={"gx": source // n_gy, "gy": source % n_gy},
            device_id_type=pl.DeviceIdType.MESH,
        )
        pl.when(me != source)(arrival.wait_recv)
    r = start_modes(n_gx, n_gy, [got[:, f, :] for f in range(6)])
    w = schur_modes(n_gx, n_gy, coef, table, *r)
    v = schur_modes(n_gx, n_gy, coef, table, *w)
    for f, field in enumerate(face_fields(n_gx, n_gy, r)):
        back[:, f, :] = field
    for f, field in enumerate(face_fields(n_gx, n_gy, w)):
        back[:, 8 + f, :] = field
    back[:, 6, :] = v[0][:, :HEIGHT]
    back[:, 7, :] = v[0][:, HEIGHT:]
    back[:, 14, :] = v[1]
    sums = (inner_product(r, r), inner_product(r, w), inner_product(w, w), inner_product(w, v))
    lanes = lane_ids((count, HEIGHT))
    back[:, 15, :] = sum(jnp.where(lanes == s, value, 0.0) for s, value in enumerate(sums))
    second = []
    for off in range(1, count):
        to, device = partner(off)
        second.append(
            pltpu.make_async_remote_copy(
                src_ref=back.at[to],
                dst_ref=landed.at[me],
                send_sem=sems.at[1, 0, off],
                recv_sem=sems.at[1, 1, off],
                device_id=device,
                device_id_type=pl.DeviceIdType.MESH,
            )
        )
        second[-1].start()
    landed[me] = back[me]
    for copy in stores:
        copy.wait()
    for to in range(count):
        pl.when(me != to)(first[to].wait_send)
    for copy in second:
        copy.wait_recv()
    faces[...] = combine(landed[...])
    for copy in second:
        copy.wait_send()


def combine(landed):
    near, far = landed[:, :8], landed[:, 8:]
    total = jnp.sum(far[:, 7:8, :], 0)
    lane = lane_ids((1, HEIGHT))
    c0, c1 = steps([jnp.sum(jnp.where(lane == s, total, 0.0)) for s in range(4)])
    lead = near - c0 * far
    rest = [lead[:, 0:2] - c1 * near[:, 6:8], lead[:, 4:5] - c1 * far[:, 6:7], jnp.zeros_like(near[:, :5])]
    return jnp.concatenate([c0 * near + c1 * far] + rest, 1)


def stacked(left, right):
    lh, ll = halved(left)
    rh, rl = halved(right)
    lhs = jnp.concatenate([lh.astype(F32), lh.astype(F32), ll.astype(F32)], 0).astype(BF16)
    rhs = jnp.concatenate([rh.astype(F32), rl.astype(F32), rh.astype(F32)], 0).astype(BF16)
    return dot(lhs, rhs, ((0,), (0,)))


def inverse_kernel(
    faces_hbm, base_hbm, x_hbm, y_hbm, z_hbm, inv_hbm, small_hbm, square_hbm, potential_hbm, residual_hbm,
    faces, base, x, y, z, inv, small, square, potential, residual, work, load_sems, store_sems,
):
    pairs = [(faces_hbm, faces), (small_hbm, small), (x_hbm, x), (y_hbm, y)]
    for t in range(DEPTH // 8):
        at = pl.ds(8 * t, 8)
        pairs += [(inv_hbm.at[at], inv.at[at]), (base_hbm.at[at], base.at[at])]
    pairs += [(square_hbm, square), (z_hbm, z)]
    copies = [pltpu.make_async_copy(s, d, load_sems.at[n]) for n, (s, d) in enumerate(pairs)]
    for copy in copies:
        copy.start()
    for copy in copies[:4]:
        copy.wait()
    xtab, ytab = (x[0], x[1]), (y[0], y[1])
    lane = lane_ids((8, HEIGHT))
    sub = lax.broadcasted_iota(jnp.int32, (8, HEIGHT), 0)
    const_left, const_right = small[0:8], small[8:16]
    for t in range(DEPTH // 8):
        copies[4 + 2 * t].wait()
        copies[5 + 2 * t].wait()
        sides = []
        for h in range(2):
            blocks = []
            for g in range(2):
                o = 4 * t + 2 * h + g
                one = faces[o, :8]
                lhs = jnp.where((sub >= 4) & (sub < 6) & (lane % WIDTH > 0), one, const_left)
                up = jnp.concatenate([one[2:], one[:2]], 0)
                rhs = jnp.where((sub < 4) & (lane > 0), one, const_right)
                rhs = jnp.where((sub >= 6) & (lane == 0), up, rhs)
                out = stacked(lhs, rhs)
                for s in range(2):
                    k = 2 * o + s
                    blocks.append(out[WIDTH * s:WIDTH * (s + 1)] * inv[k] + base[k])
            sides.append(jnp.concatenate(blocks, 0))
        out = dot3(xtab, halved(pair_lanes(sides)))
        for h in range(2):
            side = dot3(halved(out[:, HEIGHT * h:HEIGHT * (h + 1)]), ytab)
            work[8 * t + 4 * h:8 * t + 4 * h + 4] = side.reshape(4, WIDTH, HEIGHT)
    copies[12].wait()
    cosines = square[2, :DEPTH, :DEPTH]
    half = DEPTH // 2
    rows = jnp.concatenate([faces[:, 8, :], faces[:, 9, :]], 0)
    rows = dot_exact(cosines, dot_exact(rows, square[0]))
    cols = dot_exact(faces[:, 10, :], square[1])
    cols = dot_exact(cosines, jnp.concatenate([cols[:, :WIDTH], cols[:, WIDTH:]], 0))
    cols = jnp.concatenate([cols[:half], cols[half:]], 1)
    cols = jnp.where(lane_ids((half, HEIGHT)) % WIDTH == 0, 0.0, cols)
    unit = jnp.where(lane == 0, 1.0, 0.0)
    mark = jnp.where(((sub == 0) & (lane == 0)) | ((sub == 1) & (lane == WIDTH)), 1.0, 0.0)
    for o in range(half):
        lhs = jnp.where(sub == 2, cols[o:o + 1], mark)
        rhs = jnp.where(sub == 0, rows[o:o + 1], jnp.where(sub == 1, rows[half + o:half + o + 1], jnp.where(sub == 2, unit, 0.0)))
        out = stacked(lhs, rhs)
        residual[2 * o] = out[:WIDTH]
        residual[2 * o + 1] = out[WIDTH:]
    stores = [pltpu.make_async_copy(residual, residual_hbm, store_sems.at[WIDTH // 16])]
    stores[0].start()
    copies[13].wait()
    ztab = (z[0], z[1])
    for t in range(WIDTH // 16):
        sides = [work[:, 16 * t + 8 * h:16 * t + 8 * h + 8, :].reshape(DEPTH * 8, HEIGHT) for h in range(2)]
        out = dot3(ztab, halved(pair_lanes(sides)))
        for h in range(2):
            side = out[:, HEIGHT * h:HEIGHT * (h + 1)]
            potential[:, 16 * t + 8 * h:16 * t + 8 * h + 8, :] = side.reshape(DEPTH, 8, HEIGHT)
        at = pl.ds(16 * t, 16)
        stores.append(pltpu.make_async_copy(potential.at[:, at, :], potential_hbm.at[:, at, :], store_sems.at[t]))
        stores[-1].start()
    for copy in stores:
        copy.wait()


def on_device_modes(n_gx, n_gy, charge, surface_charge):
    t = host_tables()
    count = n_gx * n_gy
    block = jax.ShapeDtypeStruct(charge.shape, F32)
    hbm = pl.BlockSpec(memory_space=pl.ANY)
    vmem = pl.BlockSpec(memory_space=pltpu.VMEM)

    def held(values):
        return [pltpu.VMEM(value.shape, value.dtype) for value in values]

    pair = np.concatenate([t["pair"], t["plane"][None]], 0)
    args = [charge, surface_charge, t["zf"], t["x"], t["y"], t["ur"], t["uc"], t["inv"], t["own"], pair, t["signs"]]
    eight, sixteen = (count, 8, HEIGHT), (count, 16, HEIGHT)
    base, faces = pl.pallas_call(
        functools.partial(face_kernel, n_gx, n_gy),
        out_shape=(block, jax.ShapeDtypeStruct(sixteen, F32)),
        in_specs=[hbm] * len(args),
        out_specs=(hbm, vmem),
        scratch_shapes=held(args)
        + [pltpu.VMEM(shape, F32) for shape in (charge.shape, charge.shape, eight, eight, sixteen, sixteen)]
        + [
            pltpu.SemaphoreType.DMA((17,)),
            pltpu.SemaphoreType.DMA((DEPTH // 8,)),
            pltpu.SemaphoreType.DMA((2, 2, count)),
        ],
        compiler_params=pltpu.CompilerParams(collective_id=0, has_side_effects=True),
        name="faces",
    )(*args)
    small = np.concatenate([t["left"], t["right"]], 0)
    square = np.zeros((3, HEIGHT, HEIGHT), np.float32)
    square[0], square[1], square[2, :DEPTH, :DEPTH] = t["sy"], t["sx2"], t["cos"]
    args = [faces, base, t["x"], t["y"], t["zi"], t["inv"], small, square]
    return pl.pallas_call(
        inverse_kernel,
        out_shape=(block, block),
        in_specs=[hbm] * len(args),
        out_specs=(hbm, hbm),
        scratch_shapes=held(args)
        + [pltpu.VMEM(charge.shape, F32)] * 3
        + [pltpu.SemaphoreType.DMA((14,)), pltpu.SemaphoreType.DMA((WIDTH // 16 + 1,))],
        name="inverse",
    )(*args)


def solution(mesh):
    count = mesh.shape["gx"] * mesh.shape["gy"]
    per_device = functools.partial(on_device_modes, mesh.shape["gx"], mesh.shape["gy"])
    if 2 * count != DEPTH:
        per_device = on_device
    in_specs = (P(None, ("slab", "gx"), "gy"), P(None, ("slab", "gx"), "gy"))
    out_specs = (P(None, ("slab", "gx"), "gy"), P(None, ("slab", "gx"), "gy"))
    return jax.shard_map(
        per_device, mesh=mesh, in_specs=in_specs, out_specs=out_specs, check_vma=False
    )
```

```python
import functools

import jax
import jax.numpy as jnp
import ml_dtypes
import numpy as np
from jax import lax
from jax.experimental import pallas as pl
from jax.experimental.pallas import tpu as pltpu
from jax.sharding import PartitionSpec as P

ITERS = 2


SCREEN = 0.02


def padded(block, sides, width):
    for axis, dim in sides:
        count = lax.axis_size(axis)
        forward = [(i, i + 1) for i in range(count - 1)]
        forward.append((count - 1, 0))
        backward = [(target, source) for source, target in forward]
        low = lax.ppermute(
            lax.slice_in_dim(block, block.shape[dim] - width, None, axis=dim), axis, forward
        )
        high = lax.ppermute(lax.slice_in_dim(block, 0, width, axis=dim), axis, backward)
        block = jnp.concatenate([low, block, high], axis=dim)
    return block


def sine_full(count):
    index = jnp.arange(count).astype(jnp.float32)
    return jnp.sqrt(2.0 / count) * jnp.sin(jnp.pi * jnp.outer(index, index) / count)


def cosine_table(count):
    place = jnp.arange(count).astype(jnp.float32) + 0.5
    order = jnp.arange(count).astype(jnp.float32)
    factor = jnp.where(order == 0.0, jnp.sqrt(1.0 / count), jnp.sqrt(2.0 / count))
    return factor[None, :] * jnp.cos(jnp.pi * jnp.outer(place, order) / count)


def spectrum_table(depth, width, height):
    across = 2.0 - 2.0 * jnp.cos(jnp.pi * jnp.arange(width).astype(jnp.float32) / width)
    along = 2.0 - 2.0 * jnp.cos(jnp.pi * jnp.arange(height).astype(jnp.float32) / height)
    vertical = 2.0 - 2.0 * jnp.cos(jnp.pi * jnp.arange(depth).astype(jnp.float32) / depth)
    return SCREEN + vertical[:, None, None] + across[None, :, None] + along[None, None, :]


def apply_full(field):
    row_rims = jnp.stack([field[:, 0, :], field[:, -1, :]], 1)
    row_ext = padded(row_rims, (("gx", 1),), 1)
    col_rims = jnp.stack([field[:, :, 0], field[:, :, -1]], 0)
    col_ext = padded(col_rims, (("gy", 0),), 1)
    from_below_x = jnp.concatenate([row_ext[:, 0:1, :], field[:, :-1, :]], 1)
    from_above_x = jnp.concatenate([field[:, 1:, :], row_ext[:, 3:4, :]], 1)
    from_below_y = jnp.concatenate([col_ext[0][:, :, None], field[:, :, :-1]], 2)
    from_above_y = jnp.concatenate([field[:, :, 1:], col_ext[3][:, :, None]], 2)
    beside = from_below_x + from_above_x + from_below_y + from_above_y
    upper = jnp.concatenate([field[1:], field[-1:]], 0)
    lower = jnp.concatenate([field[:1], field[:-1]], 0)
    return (6.0 + SCREEN) * field - beside - upper - lower


def solve_interior(field, sines_x, sines_y, cosines, spectrum):
    high = lax.Precision.HIGHEST
    depth, width, height = field.shape
    hat = jnp.dot(field.reshape(depth * width, height), sines_y, precision=high).reshape(
        depth, width, height
    )
    hat = jnp.matmul(sines_x, hat, precision=high)
    hat = jnp.dot(cosines.T, hat.reshape(depth, width * height), precision=high).reshape(
        depth, width, height
    )
    hat = hat / spectrum
    back = jnp.dot(cosines, hat.reshape(depth, width * height), precision=high).reshape(
        depth, width, height
    )
    back = jnp.matmul(sines_x, back, precision=high)
    back = jnp.dot(back.reshape(depth * width, height), sines_y, precision=high)
    return back.reshape(depth, width, height)


def norm_total(residual):
    return lax.psum(jnp.sum(residual * residual), ("gx", "gy"))


def curvature_total(direction, image):
    return lax.psum(jnp.sum(direction * image), ("gx", "gy"))


def on_device(charge, surface_charge):
    depth, width, height = charge.shape
    sines_x = sine_full(width)
    sines_y = sine_full(height)
    cosines = cosine_table(depth)
    spectrum = spectrum_table(depth, width, height)
    row_place = lax.broadcasted_iota(jnp.int32, (1, width, height), 1)
    col_place = lax.broadcasted_iota(jnp.int32, (1, width, height), 2)
    gamma = jnp.where((row_place == 0) | (col_place == 0), 1.0, 0.0).astype(jnp.float32)
    source = charge.at[0].add(surface_charge[0]).at[-1].add(surface_charge[1])
    base = solve_interior(source, sines_x, sines_y, cosines, spectrum)
    reduced = gamma * (source - apply_full(base))
    iterate = jnp.zeros_like(reduced)
    residual = reduced
    direction = reduced
    norm_now = norm_total(residual)
    for step in range(ITERS):
        lifted = -solve_interior(apply_full(direction), sines_x, sines_y, cosines, spectrum)
        image, lifted = (gamma * apply_full(direction + lifted), lifted)
        alpha = norm_now / curvature_total(direction, image)
        iterate = iterate + alpha * direction
        residual = residual - alpha * image
        if step + 1 < ITERS:
            norm_next = norm_total(residual)
            direction = residual + norm_next / norm_now * direction
            norm_now = norm_next
    correction = -solve_interior(apply_full(iterate), sines_x, sines_y, cosines, spectrum)
    potential = iterate + base + correction
    return (potential, residual)


DEPTH, WIDTH, HEIGHT = 32, 64, 128
F32, BF16 = jnp.float32, jnp.bfloat16


def halves(table):
    table = np.asarray(table, np.float64)
    high = table.astype(np.float32).astype(ml_dtypes.bfloat16)
    low = (table - high.astype(np.float64)).astype(np.float32).astype(ml_dtypes.bfloat16)
    return high, low


def sine_unit(count):
    index = np.arange(count)
    table = np.sqrt(2.0 / count) * np.sin(np.pi * np.outer(index, index) / count)
    table[0, 0] = 1.0
    return table


def host_tables():
    place, order = np.arange(DEPTH) + 0.5, np.arange(DEPTH)
    factor = np.where(order == 0, np.sqrt(1.0 / DEPTH), np.sqrt(2.0 / DEPTH))
    cosines = factor[None, :] * np.cos(np.pi * np.outer(place, order) / DEPTH)
    sin_x, sin_y = sine_unit(WIDTH), sine_unit(HEIGHT)
    vertical = 2.0 - 2.0 * np.cos(np.pi * order / DEPTH)
    across = 2.0 - 2.0 * np.cos(np.pi * np.arange(WIDTH) / WIDTH)
    along = 2.0 - 2.0 * np.cos(np.pi * np.arange(HEIGHT) / HEIGHT)
    ux = np.sqrt(2.0 / WIDTH) * np.sin(np.pi * np.arange(WIDTH) / WIDTH)
    uy = np.sqrt(2.0 / HEIGHT) * np.sin(np.pi * np.arange(HEIGHT) / HEIGHT)
    sx = np.where(np.arange(WIDTH) % 2 == 1, 1.0, -1.0)
    sy = np.where(np.arange(HEIGHT) % 2 == 1, 1.0, -1.0)
    sx[0] = sy[0] = 0.0
    ex, ey = np.eye(WIDTH)[0], np.eye(HEIGHT)[0]
    t = {}
    t["zf"] = np.concatenate(halves(np.kron(cosines.T, np.eye(8))))
    t["zi"] = np.concatenate(halves(np.kron(cosines, np.eye(8))))
    t["x"] = np.concatenate(halves(np.kron(np.eye(4), sin_x)))
    y_both = np.concatenate(halves(sin_y), 1)
    t["y"] = np.concatenate([y_both, y_both], 0)
    plane = SCREEN + across[:, None] + along[None, :]
    t["plane"] = plane.astype(np.float32)
    ur = np.concatenate([np.kron(np.eye(4), (ux + ex)[None]), np.kron(np.eye(4), (ux * sx)[None]), np.zeros((8, 4 * WIDTH))], 0)
    t["ur"] = np.concatenate(halves(ur))
    uc = np.zeros((16, HEIGHT))
    uc[0], uc[1], uc[2] = uy + ey, uy * sy, ey
    t["uc"] = np.concatenate(halves(uc))
    spec = plane[None] + vertical[:, None, None]
    inner = np.zeros((WIDTH, HEIGHT))
    inner[1:, 1:] = 1.0
    inv = inner / spec
    t["inv"] = np.where(inner > 0, inv, 1.0).astype(np.float32)
    row_near = np.einsum("a,kab->kb", ux * ux, inv)
    row_far = np.einsum("a,kab->kb", ux * ux * sx, inv)
    col_near = np.einsum("b,kab->ka", uy * uy, inv)
    col_far = np.einsum("b,kab->ka", uy * uy * sy, inv)
    row_coef = SCREEN + vertical[:, None] + 2.0 + along[None, :] - 2.0 * row_near
    col_coef = SCREEN + vertical[:, None] + 2.0 + across[None, :] - 2.0 * col_near
    row_coef[:, 0] = SCREEN + vertical + 4.0
    col_coef[:, 0] = 0.0
    own = np.zeros((DEPTH // 2, 8, HEIGHT))
    own[:, 0], own[:, 1] = row_coef[0::2], row_coef[1::2]
    own[:, 2], own[:, 3] = row_far[0::2], row_far[1::2]
    own[:, 4] = np.concatenate([col_coef[0::2], col_coef[1::2]], 1)
    own[:, 5] = np.concatenate([col_far[0::2], col_far[1::2]], 1)
    own[:, 6], own[:, 7] = vertical[0::2, None], vertical[1::2, None]
    t["own"] = own.astype(np.float32)
    border = np.zeros((WIDTH, HEIGHT))
    border[0], border[:, 0] = uy, ux
    t["pair"] = np.stack([np.outer(ux, uy), border]).astype(np.float32)
    signs = np.zeros((8, HEIGHT))
    signs[0] = sy
    signs[1] = np.concatenate([sx, sx])
    t["signs"] = signs.astype(np.float32)
    zero = np.zeros(WIDTH)
    left = np.zeros((8, HEIGHT))
    left[0], left[1] = np.concatenate([ux + ex, zero]), np.concatenate([zero, ux + ex])
    left[2], left[3] = np.concatenate([ux * sx, zero]), np.concatenate([zero, ux * sx])
    left[6], left[7] = np.concatenate([ex, zero]), np.concatenate([zero, ex])
    right = np.zeros((8, HEIGHT))
    right[4], right[5] = uy + ey, uy * sy
    t["left"], t["right"] = left.astype(np.float32), right.astype(np.float32)
    split = np.concatenate([np.arange(0, DEPTH, 2), np.arange(1, DEPTH, 2)])
    t["cos"] = cosines[split][:, split].astype(np.float32)
    t["sy"] = sin_y.astype(np.float32)
    t["sx2"] = np.kron(np.eye(2), sin_x).astype(np.float32)
    return t


def halved(x):
    high = x.astype(BF16)
    return high, (x - high.astype(F32)).astype(BF16)


def dot(a, b, dims=((1,), (0,))):
    return lax.dot_general(a, b, (dims, ((), ())), preferred_element_type=F32)


def dot_table(table, b, dims=((1,), (0,))):
    count = table.shape[0] // 2
    both = dot(table, b[0], dims)
    return both[:count] + (both[count:] + dot(table[:count], b[1], dims))


def dot_packed(x, table):
    out = dot(jnp.concatenate(halved(x), 1), table)
    half = out.shape[1] // 2
    return out[:, :half] + out[:, half:]


def dot_exact(a, b, dims=((1,), (0,))):
    return lax.dot_general(
        a, b, (dims, ((), ())), precision=lax.Precision.HIGHEST, preferred_element_type=F32
    )


def lane_ids(shape):
    return lax.broadcasted_iota(jnp.int32, shape, len(shape) - 1)


def interior():
    row = lax.broadcasted_iota(jnp.int32, (WIDTH, HEIGHT), 0)
    return (row > 0) & (lane_ids((WIDTH, HEIGHT)) > 0)


def pair_lanes(parts):
    return jnp.concatenate(parts, 1)


def shift_x(n_gx, n_gy, field, by):
    cut = (by % n_gx) * n_gy
    return jnp.concatenate([field[cut:], field[:cut]], 0)


def shift_y(n_gx, n_gy, field, by):
    place = lax.broadcasted_iota(jnp.int32, field.shape, 0) % n_gy
    count = n_gx * n_gy
    ahead = by % count
    plain = jnp.concatenate([field[ahead:], field[:ahead]], 0)
    wrap = (by - n_gy if by > 0 else by + n_gy) % count
    wrapped = jnp.concatenate([field[wrap:], field[:wrap]], 0)
    edge = n_gy - 1 if by > 0 else 0
    return jnp.where(place == edge, wrapped, plain)


def turn_half(x):
    return jnp.concatenate([x[:, WIDTH:], x[:, :WIDTH]], 1)


def schur_modes(n_gx, n_gy, coef, table, row, col):
    row_coef, row_far, col_coef, col_far, row_sign, col_sign = coef
    sx = functools.partial(shift_x, n_gx, n_gy)
    sy = functools.partial(shift_y, n_gx, n_gy)
    count = n_gx * n_gy
    across = jnp.concatenate(halved(jnp.concatenate([col, col * col_sign], 0)), 1)
    across = dot(across, table[0]) + dot(across, table[1])
    along = dot(jnp.concatenate(halved(jnp.concatenate([row, row * row_sign], 0)), 0), table[2])
    along = along[:2 * count] + along[2 * count:]
    along = along[:, :HEIGHT] + along[:, HEIGHT:]
    v = across[:count] + sx(across[count:], -1)
    w = along[:count] + sy(along[count:], -1)
    row_out = row_coef * row - row_far * (sx(row, 1) + sx(row, -1)) - v - row_sign * sy(v, 1)
    col_out = col_coef * col - col_far * (sy(col, 1) + sy(col, -1)) - w - col_sign * sx(w, 1)
    lane = lane_ids((count, HEIGHT))
    row_out = row_out - jnp.concatenate(
        [jnp.where(lane == 0, w, 0.0), jnp.where(lane == 0, turn_half(w), 0.0)], 1
    )
    col_out = jnp.where(
        lane == 0, row_out[:, :HEIGHT], jnp.where(lane == WIDTH, turn_half(row_out[:, HEIGHT:]), col_out)
    )
    return row_out, col_out


def owner_tables(own, pair, turned, signs):
    inner = interior()
    blank = jnp.zeros((WIDTH, HEIGHT), F32)
    lane = lane_ids((HEIGHT, HEIGHT))
    inside = (lane % WIDTH > 0) & (lax.broadcasted_iota(jnp.int32, (HEIGHT, HEIGHT), 0) > 0)
    parts, other = [], []
    for s in range(2):
        vert = own[6 + s:7 + s]
        parts.append(jnp.where(inner, pair[0] / (pair[2] + vert), pair[1]))
        one = jnp.where(inside, turned[0] / (turned[2] + vert), turned[1])
        other.append(jnp.where((lane < WIDTH) == (s == 0), one, 0.0))
    high, low = halved(jnp.concatenate([pair_lanes([parts[0], blank]), pair_lanes([blank, parts[1]])], 0))
    table = (
        jnp.concatenate([high, high], 0),
        jnp.concatenate([low, low], 0),
        jnp.concatenate(halved(jnp.concatenate(other, 0)), 1),
    )
    coef = (
        pair_lanes([own[0:1], own[1:2]]),
        pair_lanes([own[2:3], own[3:4]]),
        own[4:5],
        own[5:6],
        pair_lanes([signs[0:1], signs[0:1]]),
        signs[1:2],
    )
    return coef, table


def start_modes(n_gx, n_gy, fields):
    sx = functools.partial(shift_x, n_gx, n_gy)
    sy = functools.partial(shift_y, n_gx, n_gy)
    row = pair_lanes([fields[0], fields[1]]) + sx(pair_lanes([fields[2], fields[3]]), -1)
    col = fields[4] + sy(fields[5], -1)
    return row, col


def inner_product(first, second):
    lane = lane_ids(first[1].shape)
    cols = jnp.where(lane % WIDTH == 0, 0.0, first[1] * second[1])
    rows = first[0] * second[0]
    down = jnp.sum(rows[:, :HEIGHT] + rows[:, HEIGHT:] + cols, 0, keepdims=True)
    return jnp.sum(down, 1, keepdims=True)


def face_fields(n_gx, n_gy, pair):
    row, col = pair
    beyond = shift_x(n_gx, n_gy, row, 1)
    return [
        row[:, :HEIGHT], row[:, HEIGHT:], beyond[:, :HEIGHT], beyond[:, HEIGHT:],
        col, shift_y(n_gx, n_gy, col, 1),
    ]


def steps(sums):
    rr, rw, ww, wv = sums
    alpha = rr / rw
    after = alpha * alpha * ww - rr
    beta = after / rr
    curve = (1 + beta) * (1 + beta) * rw - 2 * (1 + beta) * alpha * ww + alpha * alpha * wv
    second = after / curve
    return alpha + second * (1 + beta), -second * alpha


def face_kernel(
    n_gx, n_gy,
    charge_hbm, surface_hbm, z_hbm, x_hbm, y_hbm, ur_hbm, uc_hbm, inv_hbm, own_hbm, pair_hbm, turned_hbm, signs_hbm,
    base_hbm, faces,
    charge, surface, z, x, y, ur, uc, inv, own_ref, pair_ref, turned_ref, signs_ref,
    work, base, msg, got, back, landed, load_sems, store_sems, sems,
):
    count = n_gx * n_gy
    gx, gy = lax.axis_index("gx"), lax.axis_index("gy")
    me = gx * n_gy + gy
    pairs = [(z_hbm, z), (surface_hbm, surface)]
    pairs += [(charge_hbm.at[:, pl.ds(16 * t, 16), :], charge.at[:, pl.ds(16 * t, 16), :]) for t in range(WIDTH // 16)]
    pairs += [(y_hbm, y), (x_hbm, x), (ur_hbm, ur), (uc_hbm, uc)]
    pairs += [(inv_hbm.at[pl.ds(8 * t, 8)], inv.at[pl.ds(8 * t, 8)]) for t in range(DEPTH // 8)]
    pairs += [(own_hbm, own_ref), (pair_hbm, pair_ref), (turned_hbm, turned_ref), (signs_hbm, signs_ref)]
    copies = [pltpu.make_async_copy(s, d, load_sems.at[n]) for n, (s, d) in enumerate(pairs)]
    for copy in copies:
        copy.start()

    def partner(off):
        to_x, to_y = gx + off // n_gy, gy + off % n_gy
        to_x = jnp.where(to_x >= n_gx, to_x - n_gx, to_x)
        to_y = jnp.where(to_y >= n_gy, to_y - n_gy, to_y)
        return to_x * n_gy + to_y, {"gx": to_x, "gy": to_y}

    barrier = pltpu.get_barrier_semaphore()
    for off in range(1, count):
        pl.semaphore_signal(barrier, inc=1, device_id=partner(off)[1], device_id_type=pl.DeviceIdType.MESH)
    copies[0].wait()
    copies[1].wait()
    ztab = z[...]
    for t in range(WIDTH // 16):
        copies[2 + t].wait()
        sides = []
        for h in range(2):
            at = pl.ds(16 * t + 8 * h, 8)
            block = charge[:, at, :]
            block = jnp.concatenate(
                [block[:1] + surface[0:1, at, :], block[1:-1], block[-1:] + surface[1:2, at, :]], 0
            )
            sides.append(block.reshape(DEPTH * 8, HEIGHT))
        out = dot_table(ztab, halved(pair_lanes(sides)))
        if t == 0:
            copies[6].wait()
            ytab = y[...]
        for h in range(2):
            side = out[:, HEIGHT * h:HEIGHT * (h + 1)]
            side = dot_packed(side, ytab)
            work[:, 16 * t + 8 * h:16 * t + 8 * h + 8, :] = side.reshape(DEPTH, 8, HEIGHT)
    for copy in copies[7:10]:
        copy.wait()
    xtab, utab, ctab = x[...], ur[...], uc[...]
    inner = interior()
    lane = lane_ids((8, HEIGHT))
    pl.semaphore_wait(barrier, count - 1)
    stores = []
    first = [
        pltpu.make_async_remote_copy(
            src_ref=msg.at[to],
            dst_ref=got.at[me],
            send_sem=sems.at[0, 0, to],
            recv_sem=sems.at[0, 1, me],
            device_id={"gx": to // n_gy, "gy": to % n_gy},
            device_id_type=pl.DeviceIdType.MESH,
        )
        for to in range(count)
    ]
    for t in range(DEPTH // 8):
        copies[10 + t].wait()
        sides = [work[8 * t + 4 * h:8 * t + 4 * h + 4].reshape(4 * WIDTH, HEIGHT) for h in range(2)]
        out = dot_table(xtab, halved(pair_lanes(sides)))
        for h in range(2):
            side = out[:, HEIGHT * h:HEIGHT * (h + 1)].reshape(4, WIDTH, HEIGHT)
            full = []
            corner = []
            for s in range(4):
                k = 8 * t + 4 * h + s
                one = side[s] * inv[k]
                base[k] = jnp.where(inner, one, 0.0)
                full.append(one)
                corner.append(one[0:1])
            full = jnp.concatenate(full, 0)
            parts = halved(full)
            rows = dot_table(utab, parts)
            own = jnp.concatenate(corner + [jnp.zeros((4, HEIGHT), F32)], 0)
            rows = jnp.where(lane == 0, own, rows[:8])
            cols = dot_table(ctab, parts, ((1,), (1,)))
            edge = lane_ids((1, 4 * WIDTH)) % WIDTH == 0
            near = jnp.where(edge, cols[2:3], cols[0:1])
            far = jnp.where(edge, 0.0, cols[1:2])
            for g in range(2):
                at = slice(HEIGHT * g, HEIGHT * (g + 1))
                msg[4 * t + 2 * h + g] = jnp.concatenate(
                    [rows[2 * g:2 * g + 2], rows[4 + 2 * g:6 + 2 * g], near[:, at], far[:, at], jnp.zeros((2, HEIGHT), F32)],
                    0,
                )
        stores.append(
            pltpu.make_async_copy(base.at[pl.ds(8 * t, 8)], base_hbm.at[pl.ds(8 * t, 8)], store_sems.at[t])
        )
        stores[-1].start()
        for to in range(4 * t, 4 * t + 4):
            pl.when(me != to)(first[to].start)
    for copy in copies[14:]:
        copy.wait()
    coef, table = owner_tables(own_ref[me], pair_ref[...], turned_ref[...], signs_ref[...])
    got[me] = msg[me]
    for source in range(count):
        arrival = pltpu.make_async_remote_copy(
            src_ref=msg.at[source],
            dst_ref=got.at[source],
            send_sem=sems.at[0, 0, source],
            recv_sem=sems.at[0, 1, source],
            device_id={"gx": source // n_gy, "gy": source % n_gy},
            device_id_type=pl.DeviceIdType.MESH,
        )
        pl.when(me != source)(arrival.wait_recv)
    r = start_modes(n_gx, n_gy, [got[:, f, :] for f in range(6)])
    w = schur_modes(n_gx, n_gy, coef, table, *r)
    v = schur_modes(n_gx, n_gy, coef, table, *w)
    for f, field in enumerate(face_fields(n_gx, n_gy, r)):
        back[:, f, :] = field
    for f, field in enumerate(face_fields(n_gx, n_gy, w)):
        back[:, 8 + f, :] = field
    back[:, 6, :] = v[0][:, :HEIGHT]
    back[:, 7, :] = v[0][:, HEIGHT:]
    back[:, 14, :] = v[1]
    sums = (inner_product(r, r), inner_product(r, w), inner_product(w, w), inner_product(w, v))
    lanes = lane_ids((count, HEIGHT))
    back[:, 15, :] = sum(jnp.where(lanes == s, value, 0.0) for s, value in enumerate(sums))
    second = []
    for off in range(1, count):
        to, device = partner(off)
        second.append(
            pltpu.make_async_remote_copy(
                src_ref=back.at[to],
                dst_ref=landed.at[me],
                send_sem=sems.at[1, 0, off],
                recv_sem=sems.at[1, 1, off],
                device_id=device,
                device_id_type=pl.DeviceIdType.MESH,
            )
        )
        second[-1].start()
    landed[me] = back[me]
    for copy in stores:
        copy.wait()
    for to in range(count):
        pl.when(me != to)(first[to].wait_send)
    for copy in second:
        copy.wait_recv()
    faces[...] = combine(landed[...])
    for copy in second:
        copy.wait_send()


def combine(landed):
    near, far = landed[:, :8], landed[:, 8:]
    total = jnp.sum(far[:, 7:8, :], 0)
    lane = lane_ids((1, HEIGHT))
    c0, c1 = steps([jnp.sum(jnp.where(lane == s, total, 0.0), 1, keepdims=True) for s in range(4)])
    c0, c1 = c0[None], c1[None]
    lead = near - c0 * far
    rest = [lead[:, 0:2] - c1 * near[:, 6:8], lead[:, 4:5] - c1 * far[:, 6:7], jnp.zeros_like(near[:, :5])]
    return jnp.concatenate([c0 * near + c1 * far] + rest, 1)


def stacked(left, right):
    lh, ll = halved(left)
    rh, rl = halved(right)
    lhs = jnp.concatenate([lh.astype(F32), lh.astype(F32), ll.astype(F32)], 0).astype(BF16)
    rhs = jnp.concatenate([rh.astype(F32), rl.astype(F32), rh.astype(F32)], 0).astype(BF16)
    return dot(lhs, rhs, ((0,), (0,)))


def inverse_kernel(
    faces_hbm, base_hbm, x_hbm, y_hbm, z_hbm, inv_hbm, small_hbm, square_hbm, potential_hbm, residual_hbm,
    faces, base, x, y, z, inv, small, square, potential, residual, work, load_sems, store_sems,
):
    pairs = [(faces_hbm, faces), (small_hbm, small), (square_hbm, square), (x_hbm, x), (y_hbm, y)]
    for t in range(DEPTH // 8):
        at = pl.ds(8 * t, 8)
        pairs += [(inv_hbm.at[at], inv.at[at]), (base_hbm.at[at], base.at[at])]
    pairs += [(z_hbm, z)]
    copies = [pltpu.make_async_copy(s, d, load_sems.at[n]) for n, (s, d) in enumerate(pairs)]
    for copy in copies:
        copy.start()
    for copy in copies[:3]:
        copy.wait()
    lane = lane_ids((8, HEIGHT))
    sub = lax.broadcasted_iota(jnp.int32, (8, HEIGHT), 0)
    const_left, const_right = small[0:8], small[8:16]
    cosines = square[2, :DEPTH, :DEPTH]
    half = DEPTH // 2
    rows = jnp.concatenate([faces[:, 8, :], faces[:, 9, :]], 0)
    rows = dot_exact(cosines, dot_exact(rows, square[0]))
    cols = dot_exact(faces[:, 10, :], square[1])
    cols = dot_exact(cosines, jnp.concatenate([cols[:, :WIDTH], cols[:, WIDTH:]], 0))
    cols = jnp.concatenate([cols[:half], cols[half:]], 1)
    cols = jnp.where(lane_ids((half, HEIGHT)) % WIDTH == 0, 0.0, cols)
    unit = jnp.where(lane == 0, 1.0, 0.0)
    mark = jnp.where(((sub == 0) & (lane == 0)) | ((sub == 1) & (lane == WIDTH)), 1.0, 0.0)
    for o in range(half):
        lhs = jnp.where(sub == 2, cols[o:o + 1], mark)
        rhs = jnp.where(sub == 0, rows[o:o + 1], jnp.where(sub == 1, rows[half + o:half + o + 1], jnp.where(sub == 2, unit, 0.0)))
        out = stacked(lhs, rhs)
        residual[2 * o] = out[:WIDTH]
        residual[2 * o + 1] = out[WIDTH:]
    stores = [pltpu.make_async_copy(residual, residual_hbm, store_sems.at[WIDTH // 16])]
    stores[0].start()
    copies[3].wait()
    copies[4].wait()
    xtab, ytab = x[...], y[...]
    for t in range(DEPTH // 8):
        copies[5 + 2 * t].wait()
        copies[6 + 2 * t].wait()
        sides = []
        for h in range(2):
            blocks = []
            for g in range(2):
                o = 4 * t + 2 * h + g
                one = faces[o, :8]
                lhs = jnp.where((sub >= 4) & (sub < 6) & (lane % WIDTH > 0), one, const_left)
                up = jnp.concatenate([one[2:], one[:2]], 0)
                rhs = jnp.where((sub < 4) & (lane > 0), one, const_right)
                rhs = jnp.where((sub >= 6) & (lane == 0), up, rhs)
                out = stacked(lhs, rhs)
                for s in range(2):
                    k = 2 * o + s
                    blocks.append(out[WIDTH * s:WIDTH * (s + 1)] * inv[k] + base[k])
            sides.append(jnp.concatenate(blocks, 0))
        out = dot_table(xtab, halved(pair_lanes(sides)))
        for h in range(2):
            side = dot_packed(out[:, HEIGHT * h:HEIGHT * (h + 1)], ytab)
            work[8 * t + 4 * h:8 * t + 4 * h + 4] = side.reshape(4, WIDTH, HEIGHT)
    copies[13].wait()
    ztab = z[...]
    for t in range(WIDTH // 16):
        sides = [work[:, 16 * t + 8 * h:16 * t + 8 * h + 8, :].reshape(DEPTH * 8, HEIGHT) for h in range(2)]
        out = dot_table(ztab, halved(pair_lanes(sides)))
        for h in range(2):
            side = out[:, HEIGHT * h:HEIGHT * (h + 1)]
            potential[:, 16 * t + 8 * h:16 * t + 8 * h + 8, :] = side.reshape(DEPTH, 8, HEIGHT)
        at = pl.ds(16 * t, 16)
        stores.append(pltpu.make_async_copy(potential.at[:, at, :], potential_hbm.at[:, at, :], store_sems.at[t]))
        stores[-1].start()
    for copy in stores:
        copy.wait()


def on_device_modes(n_gx, n_gy, charge, surface_charge):
    t = host_tables()
    count = n_gx * n_gy
    block = jax.ShapeDtypeStruct(charge.shape, F32)
    hbm = pl.BlockSpec(memory_space=pl.ANY)
    vmem = pl.BlockSpec(memory_space=pltpu.VMEM)

    def held(values):
        return [pltpu.VMEM(value.shape, value.dtype) for value in values]

    pair = np.concatenate([t["pair"], t["plane"][None]], 0)
    turned = np.concatenate([np.swapaxes(pair, 1, 2)] * 2, 2)
    args = [charge, surface_charge, t["zf"], t["x"], t["y"], t["ur"], t["uc"], t["inv"], t["own"], pair, turned, t["signs"]]
    eight, sixteen = (count, 8, HEIGHT), (count, 16, HEIGHT)
    base, faces = pl.pallas_call(
        functools.partial(face_kernel, n_gx, n_gy),
        out_shape=(block, jax.ShapeDtypeStruct(sixteen, F32)),
        in_specs=[hbm] * len(args),
        out_specs=(hbm, vmem),
        scratch_shapes=held(args)
        + [pltpu.VMEM(shape, F32) for shape in (charge.shape, charge.shape, eight, eight, sixteen, sixteen)]
        + [
            pltpu.SemaphoreType.DMA((18,)),
            pltpu.SemaphoreType.DMA((DEPTH // 8,)),
            pltpu.SemaphoreType.DMA((2, 2, count)),
        ],
        compiler_params=pltpu.CompilerParams(collective_id=0, has_side_effects=True),
        name="faces",
    )(*args)
    small = np.concatenate([t["left"], t["right"]], 0)
    square = np.zeros((3, HEIGHT, HEIGHT), np.float32)
    square[0], square[1], square[2, :DEPTH, :DEPTH] = t["sy"], t["sx2"], t["cos"]
    args = [faces, base, t["x"], t["y"], t["zi"], t["inv"], small, square]
    return pl.pallas_call(
        inverse_kernel,
        out_shape=(block, block),
        in_specs=[hbm] * len(args),
        out_specs=(hbm, hbm),
        scratch_shapes=held(args)
        + [pltpu.VMEM(charge.shape, F32)] * 3
        + [pltpu.SemaphoreType.DMA((14,)), pltpu.SemaphoreType.DMA((WIDTH // 16 + 1,))],
        name="inverse",
    )(*args)


def solution(mesh):
    count = mesh.shape["gx"] * mesh.shape["gy"]
    per_device = functools.partial(on_device_modes, mesh.shape["gx"], mesh.shape["gy"])
    if 2 * count != DEPTH:
        per_device = on_device
    in_specs = (P(None, ("slab", "gx"), "gy"), P(None, ("slab", "gx"), "gy"))
    out_specs = (P(None, ("slab", "gx"), "gy"), P(None, ("slab", "gx"), "gy"))
    return jax.shard_map(
        per_device, mesh=mesh, in_specs=in_specs, out_specs=out_specs, check_vma=False
    )
```

```python
import functools

import jax
import jax.numpy as jnp
import ml_dtypes
import numpy as np
from jax import lax
from jax.experimental import pallas as pl
from jax.experimental.pallas import tpu as pltpu
from jax.sharding import PartitionSpec as P

ITERS = 2


SCREEN = 0.02


def padded(block, sides, width):
    for axis, dim in sides:
        count = lax.axis_size(axis)
        forward = [(i, i + 1) for i in range(count - 1)]
        forward.append((count - 1, 0))
        backward = [(target, source) for source, target in forward]
        low = lax.ppermute(
            lax.slice_in_dim(block, block.shape[dim] - width, None, axis=dim), axis, forward
        )
        high = lax.ppermute(lax.slice_in_dim(block, 0, width, axis=dim), axis, backward)
        block = jnp.concatenate([low, block, high], axis=dim)
    return block


def sine_full(count):
    index = jnp.arange(count).astype(jnp.float32)
    return jnp.sqrt(2.0 / count) * jnp.sin(jnp.pi * jnp.outer(index, index) / count)


def cosine_table(count):
    place = jnp.arange(count).astype(jnp.float32) + 0.5
    order = jnp.arange(count).astype(jnp.float32)
    factor = jnp.where(order == 0.0, jnp.sqrt(1.0 / count), jnp.sqrt(2.0 / count))
    return factor[None, :] * jnp.cos(jnp.pi * jnp.outer(place, order) / count)


def spectrum_table(depth, width, height):
    across = 2.0 - 2.0 * jnp.cos(jnp.pi * jnp.arange(width).astype(jnp.float32) / width)
    along = 2.0 - 2.0 * jnp.cos(jnp.pi * jnp.arange(height).astype(jnp.float32) / height)
    vertical = 2.0 - 2.0 * jnp.cos(jnp.pi * jnp.arange(depth).astype(jnp.float32) / depth)
    return SCREEN + vertical[:, None, None] + across[None, :, None] + along[None, None, :]


def apply_full(field):
    row_rims = jnp.stack([field[:, 0, :], field[:, -1, :]], 1)
    row_ext = padded(row_rims, (("gx", 1),), 1)
    col_rims = jnp.stack([field[:, :, 0], field[:, :, -1]], 0)
    col_ext = padded(col_rims, (("gy", 0),), 1)
    from_below_x = jnp.concatenate([row_ext[:, 0:1, :], field[:, :-1, :]], 1)
    from_above_x = jnp.concatenate([field[:, 1:, :], row_ext[:, 3:4, :]], 1)
    from_below_y = jnp.concatenate([col_ext[0][:, :, None], field[:, :, :-1]], 2)
    from_above_y = jnp.concatenate([field[:, :, 1:], col_ext[3][:, :, None]], 2)
    beside = from_below_x + from_above_x + from_below_y + from_above_y
    upper = jnp.concatenate([field[1:], field[-1:]], 0)
    lower = jnp.concatenate([field[:1], field[:-1]], 0)
    return (6.0 + SCREEN) * field - beside - upper - lower


def solve_interior(field, sines_x, sines_y, cosines, spectrum):
    high = lax.Precision.HIGHEST
    depth, width, height = field.shape
    hat = jnp.dot(field.reshape(depth * width, height), sines_y, precision=high).reshape(
        depth, width, height
    )
    hat = jnp.matmul(sines_x, hat, precision=high)
    hat = jnp.dot(cosines.T, hat.reshape(depth, width * height), precision=high).reshape(
        depth, width, height
    )
    hat = hat / spectrum
    back = jnp.dot(cosines, hat.reshape(depth, width * height), precision=high).reshape(
        depth, width, height
    )
    back = jnp.matmul(sines_x, back, precision=high)
    back = jnp.dot(back.reshape(depth * width, height), sines_y, precision=high)
    return back.reshape(depth, width, height)


def norm_total(residual):
    return lax.psum(jnp.sum(residual * residual), ("gx", "gy"))


def curvature_total(direction, image):
    return lax.psum(jnp.sum(direction * image), ("gx", "gy"))


def on_device(charge, surface_charge):
    depth, width, height = charge.shape
    sines_x = sine_full(width)
    sines_y = sine_full(height)
    cosines = cosine_table(depth)
    spectrum = spectrum_table(depth, width, height)
    row_place = lax.broadcasted_iota(jnp.int32, (1, width, height), 1)
    col_place = lax.broadcasted_iota(jnp.int32, (1, width, height), 2)
    gamma = jnp.where((row_place == 0) | (col_place == 0), 1.0, 0.0).astype(jnp.float32)
    source = charge.at[0].add(surface_charge[0]).at[-1].add(surface_charge[1])
    base = solve_interior(source, sines_x, sines_y, cosines, spectrum)
    reduced = gamma * (source - apply_full(base))
    iterate = jnp.zeros_like(reduced)
    residual = reduced
    direction = reduced
    norm_now = norm_total(residual)
    for step in range(ITERS):
        lifted = -solve_interior(apply_full(direction), sines_x, sines_y, cosines, spectrum)
        image, lifted = (gamma * apply_full(direction + lifted), lifted)
        alpha = norm_now / curvature_total(direction, image)
        iterate = iterate + alpha * direction
        residual = residual - alpha * image
        if step + 1 < ITERS:
            norm_next = norm_total(residual)
            direction = residual + norm_next / norm_now * direction
            norm_now = norm_next
    correction = -solve_interior(apply_full(iterate), sines_x, sines_y, cosines, spectrum)
    potential = iterate + base + correction
    return (potential, residual)


DEPTH, WIDTH, HEIGHT = 32, 64, 128
F32, BF16 = jnp.float32, jnp.bfloat16


def halves(table):
    table = np.asarray(table, np.float64)
    high = table.astype(np.float32).astype(ml_dtypes.bfloat16)
    low = (table - high.astype(np.float64)).astype(np.float32).astype(ml_dtypes.bfloat16)
    return high, low


def sine_unit(count):
    index = np.arange(count)
    table = np.sqrt(2.0 / count) * np.sin(np.pi * np.outer(index, index) / count)
    table[0, 0] = 1.0
    return table


def host_tables():
    place, order = np.arange(DEPTH) + 0.5, np.arange(DEPTH)
    factor = np.where(order == 0, np.sqrt(1.0 / DEPTH), np.sqrt(2.0 / DEPTH))
    cosines = factor[None, :] * np.cos(np.pi * np.outer(place, order) / DEPTH)
    sin_x, sin_y = sine_unit(WIDTH), sine_unit(HEIGHT)
    vertical = 2.0 - 2.0 * np.cos(np.pi * order / DEPTH)
    across = 2.0 - 2.0 * np.cos(np.pi * np.arange(WIDTH) / WIDTH)
    along = 2.0 - 2.0 * np.cos(np.pi * np.arange(HEIGHT) / HEIGHT)
    ux = np.sqrt(2.0 / WIDTH) * np.sin(np.pi * np.arange(WIDTH) / WIDTH)
    uy = np.sqrt(2.0 / HEIGHT) * np.sin(np.pi * np.arange(HEIGHT) / HEIGHT)
    sx = np.where(np.arange(WIDTH) % 2 == 1, 1.0, -1.0)
    sy = np.where(np.arange(HEIGHT) % 2 == 1, 1.0, -1.0)
    sx[0] = sy[0] = 0.0
    ex, ey = np.eye(WIDTH)[0], np.eye(HEIGHT)[0]
    t = {}
    t["zf"] = np.concatenate(halves(np.kron(cosines.T, np.eye(8))))
    t["zi"] = np.concatenate(halves(np.kron(cosines, np.eye(8))))
    t["x"] = np.concatenate(halves(np.kron(np.eye(4), sin_x)))
    y_both = np.concatenate(halves(sin_y), 1)
    t["y"] = np.concatenate([y_both, y_both], 0)
    plane = SCREEN + across[:, None] + along[None, :]
    t["plane"] = plane.astype(np.float32)
    ur = np.concatenate([np.kron(np.eye(4), (ux + ex)[None]), np.kron(np.eye(4), (ux * sx)[None]), np.zeros((8, 4 * WIDTH))], 0)
    t["ur"] = np.concatenate(halves(ur))
    uc = np.zeros((16, HEIGHT))
    uc[0], uc[1], uc[2] = uy + ey, uy * sy, ey
    t["uc"] = np.concatenate(halves(uc))
    spec = plane[None] + vertical[:, None, None]
    inner = np.zeros((WIDTH, HEIGHT))
    inner[1:, 1:] = 1.0
    inv = inner / spec
    t["inv"] = np.where(inner > 0, inv, 1.0).astype(np.float32)
    row_near = np.einsum("a,kab->kb", ux * ux, inv)
    row_far = np.einsum("a,kab->kb", ux * ux * sx, inv)
    col_near = np.einsum("b,kab->ka", uy * uy, inv)
    col_far = np.einsum("b,kab->ka", uy * uy * sy, inv)
    row_coef = SCREEN + vertical[:, None] + 2.0 + along[None, :] - 2.0 * row_near
    col_coef = SCREEN + vertical[:, None] + 2.0 + across[None, :] - 2.0 * col_near
    row_coef[:, 0] = SCREEN + vertical + 4.0
    col_coef[:, 0] = 0.0
    own = np.zeros((DEPTH // 2, 8, HEIGHT))
    own[:, 0], own[:, 1] = row_coef[0::2], row_coef[1::2]
    own[:, 2], own[:, 3] = row_far[0::2], row_far[1::2]
    own[:, 4] = np.concatenate([col_coef[0::2], col_coef[1::2]], 1)
    own[:, 5] = np.concatenate([col_far[0::2], col_far[1::2]], 1)
    own[:, 6], own[:, 7] = vertical[0::2, None], vertical[1::2, None]
    t["own"] = own.astype(np.float32)
    border = np.zeros((WIDTH, HEIGHT))
    border[0], border[:, 0] = uy, ux
    t["pair"] = np.stack([np.outer(ux, uy), border]).astype(np.float32)
    signs = np.zeros((8, HEIGHT))
    signs[0] = sy
    signs[1] = np.concatenate([sx, sx])
    t["signs"] = signs.astype(np.float32)
    zero = np.zeros(WIDTH)
    left = np.zeros((8, HEIGHT))
    left[0], left[1] = np.concatenate([ux + ex, zero]), np.concatenate([zero, ux + ex])
    left[2], left[3] = np.concatenate([ux * sx, zero]), np.concatenate([zero, ux * sx])
    left[6], left[7] = np.concatenate([ex, zero]), np.concatenate([zero, ex])
    right = np.zeros((8, HEIGHT))
    right[4], right[5] = uy + ey, uy * sy
    t["left"], t["right"] = left.astype(np.float32), right.astype(np.float32)
    split = np.concatenate([np.arange(0, DEPTH, 2), np.arange(1, DEPTH, 2)])
    t["cos"] = cosines[split][:, split].astype(np.float32)
    t["sy"] = sin_y.astype(np.float32)
    t["sx2"] = np.kron(np.eye(2), sin_x).astype(np.float32)
    return t


def halved(x):
    high = x.astype(BF16)
    return high, (x - high.astype(F32)).astype(BF16)


def dot(a, b, dims=((1,), (0,))):
    return lax.dot_general(a, b, (dims, ((), ())), preferred_element_type=F32)


def dot_table(table, b, dims=((1,), (0,))):
    count = table.shape[0] // 2
    both = dot(table, b[0], dims)
    return both[:count] + (both[count:] + dot(table[:count], b[1], dims))


def dot_packed(x, table):
    out = dot(jnp.concatenate(halved(x), 1), table)
    half = out.shape[1] // 2
    return out[:, :half] + out[:, half:]


def dot_exact(a, b, dims=((1,), (0,))):
    return lax.dot_general(
        a, b, (dims, ((), ())), precision=lax.Precision.HIGHEST, preferred_element_type=F32
    )


def lane_ids(shape):
    return lax.broadcasted_iota(jnp.int32, shape, len(shape) - 1)


def interior():
    row = lax.broadcasted_iota(jnp.int32, (WIDTH, HEIGHT), 0)
    return (row > 0) & (lane_ids((WIDTH, HEIGHT)) > 0)


def pair_lanes(parts):
    return jnp.concatenate(parts, 1)


def shift_x(n_gx, n_gy, field, by):
    cut = (by % n_gx) * n_gy
    return jnp.concatenate([field[cut:], field[:cut]], 0)


def shift_y(n_gx, n_gy, field, by):
    place = lax.broadcasted_iota(jnp.int32, field.shape, 0) % n_gy
    count = n_gx * n_gy
    ahead = by % count
    plain = jnp.concatenate([field[ahead:], field[:ahead]], 0)
    wrap = (by - n_gy if by > 0 else by + n_gy) % count
    wrapped = jnp.concatenate([field[wrap:], field[:wrap]], 0)
    edge = n_gy - 1 if by > 0 else 0
    return jnp.where(place == edge, wrapped, plain)


def turn_half(x):
    return jnp.concatenate([x[:, WIDTH:], x[:, :WIDTH]], 1)


def schur_modes(n_gx, n_gy, coef, table, row, col):
    row_coef, row_far, col_coef, col_far, row_sign, col_sign = coef
    sx = functools.partial(shift_x, n_gx, n_gy)
    sy = functools.partial(shift_y, n_gx, n_gy)
    count = n_gx * n_gy
    across = jnp.concatenate(halved(jnp.concatenate([col, col * col_sign], 0)), 1)
    across = dot(across, table[0]) + dot(across, table[1])
    along = dot(jnp.concatenate(halved(jnp.concatenate([row, row * row_sign], 0)), 0), table[2])
    along = along[:2 * count] + along[2 * count:]
    along = along[:, :HEIGHT] + along[:, HEIGHT:]
    v = across[:count] + sx(across[count:], -1)
    w = along[:count] + sy(along[count:], -1)
    row_out = row_coef * row - row_far * (sx(row, 1) + sx(row, -1)) - v - row_sign * sy(v, 1)
    col_out = col_coef * col - col_far * (sy(col, 1) + sy(col, -1)) - w - col_sign * sx(w, 1)
    lane = lane_ids((count, HEIGHT))
    row_out = row_out - jnp.concatenate(
        [jnp.where(lane == 0, w, 0.0), jnp.where(lane == 0, turn_half(w), 0.0)], 1
    )
    col_out = jnp.where(
        lane == 0, row_out[:, :HEIGHT], jnp.where(lane == WIDTH, turn_half(row_out[:, HEIGHT:]), col_out)
    )
    return row_out, col_out


def owner_tables(own, pair, turned, signs):
    inner = interior()
    blank = jnp.zeros((WIDTH, HEIGHT), F32)
    lane = lane_ids((HEIGHT, HEIGHT))
    inside = (lane % WIDTH > 0) & (lax.broadcasted_iota(jnp.int32, (HEIGHT, HEIGHT), 0) > 0)
    parts, other = [], []
    for s in range(2):
        vert = own[6 + s:7 + s]
        parts.append(jnp.where(inner, pair[0] / (pair[2] + vert), pair[1]))
        one = jnp.where(inside, turned[0] / (turned[2] + vert), turned[1])
        other.append(jnp.where((lane < WIDTH) == (s == 0), one, 0.0))
    high, low = halved(jnp.concatenate([pair_lanes([parts[0], blank]), pair_lanes([blank, parts[1]])], 0))
    table = (
        jnp.concatenate([high, high], 0),
        jnp.concatenate([low, low], 0),
        jnp.concatenate(halved(jnp.concatenate(other, 0)), 1),
    )
    coef = (
        pair_lanes([own[0:1], own[1:2]]),
        pair_lanes([own[2:3], own[3:4]]),
        own[4:5],
        own[5:6],
        pair_lanes([signs[0:1], signs[0:1]]),
        signs[1:2],
    )
    return coef, table


def start_modes(n_gx, n_gy, fields):
    sx = functools.partial(shift_x, n_gx, n_gy)
    sy = functools.partial(shift_y, n_gx, n_gy)
    row = pair_lanes([fields[0], fields[1]]) + sx(pair_lanes([fields[2], fields[3]]), -1)
    col = fields[4] + sy(fields[5], -1)
    return row, col


def inner_product(first, second):
    lane = lane_ids(first[1].shape)
    cols = jnp.where(lane % WIDTH == 0, 0.0, first[1] * second[1])
    rows = first[0] * second[0]
    down = jnp.sum(rows[:, :HEIGHT] + rows[:, HEIGHT:] + cols, 0, keepdims=True)
    return jnp.sum(down, 1, keepdims=True)


def face_fields(n_gx, n_gy, pair):
    row, col = pair
    beyond = shift_x(n_gx, n_gy, row, 1)
    return [
        row[:, :HEIGHT], row[:, HEIGHT:], beyond[:, :HEIGHT], beyond[:, HEIGHT:],
        col, shift_y(n_gx, n_gy, col, 1),
    ]


def steps(sums):
    rr, rw, ww, wv = sums
    alpha = rr / rw
    after = alpha * alpha * ww - rr
    beta = after / rr
    curve = (1 + beta) * (1 + beta) * rw - 2 * (1 + beta) * alpha * ww + alpha * alpha * wv
    second = after / curve
    return alpha + second * (1 + beta), -second * alpha


def face_kernel(
    n_gx, n_gy,
    charge_hbm, surface_hbm, z_hbm, x_hbm, y_hbm, ur_hbm, uc_hbm, inv_hbm, own_hbm, pair_hbm, turned_hbm, signs_hbm,
    base_hbm, faces,
    charge, surface, z, x, y, ur, uc, inv, own_ref, pair_ref, turned_ref, signs_ref,
    work, base, msg, got, back, landed, load_sems, store_sems, sems,
):
    count = n_gx * n_gy
    gx, gy = lax.axis_index("gx"), lax.axis_index("gy")
    me = gx * n_gy + gy
    pairs = [(z_hbm, z), (surface_hbm, surface)]
    pairs += [(charge_hbm.at[:, pl.ds(16 * t, 16), :], charge.at[:, pl.ds(16 * t, 16), :]) for t in range(WIDTH // 16)]
    pairs += [(y_hbm, y), (x_hbm, x), (ur_hbm, ur), (uc_hbm, uc)]
    pairs += [(inv_hbm.at[pl.ds(8 * t, 8)], inv.at[pl.ds(8 * t, 8)]) for t in range(DEPTH // 8)]
    pairs += [(own_hbm, own_ref), (pair_hbm, pair_ref), (turned_hbm, turned_ref), (signs_hbm, signs_ref)]
    copies = [pltpu.make_async_copy(s, d, load_sems.at[n]) for n, (s, d) in enumerate(pairs)]
    for copy in copies:
        copy.start()

    def partner(off):
        to_x, to_y = gx + off // n_gy, gy + off % n_gy
        to_x = jnp.where(to_x >= n_gx, to_x - n_gx, to_x)
        to_y = jnp.where(to_y >= n_gy, to_y - n_gy, to_y)
        return to_x * n_gy + to_y, {"gx": to_x, "gy": to_y}

    def send(source, target, which, off):
        to, device = partner(off)
        copy = pltpu.make_async_remote_copy(
            src_ref=source.at[to],
            dst_ref=target.at[me],
            send_sem=sems.at[which, 0],
            recv_sem=sems.at[which, 1],
            device_id=device,
            device_id_type=pl.DeviceIdType.MESH,
        )
        copy.start()

    def all_done(buffer, sem):
        whole = buffer.at[pl.ds(0, count - 1)]
        pltpu.make_async_copy(whole, whole, sem).wait()

    barrier = pltpu.get_barrier_semaphore()
    for off in range(1, count):
        pl.semaphore_signal(barrier, inc=1, device_id=partner(off)[1], device_id_type=pl.DeviceIdType.MESH)
    copies[0].wait()
    copies[1].wait()
    ztab = z[...]
    for t in range(WIDTH // 16):
        copies[2 + t].wait()
        sides = []
        for h in range(2):
            at = pl.ds(16 * t + 8 * h, 8)
            block = charge[:, at, :]
            block = jnp.concatenate(
                [block[:1] + surface[0:1, at, :], block[1:-1], block[-1:] + surface[1:2, at, :]], 0
            )
            sides.append(block.reshape(DEPTH * 8, HEIGHT))
        out = dot_table(ztab, halved(pair_lanes(sides)))
        if t == 0:
            copies[6].wait()
            ytab = y[...]
        for h in range(2):
            side = out[:, HEIGHT * h:HEIGHT * (h + 1)]
            side = dot_packed(side, ytab)
            work[:, 16 * t + 8 * h:16 * t + 8 * h + 8, :] = side.reshape(DEPTH, 8, HEIGHT)
    for copy in copies[7:10]:
        copy.wait()
    xtab, utab, ctab = x[...], ur[...], uc[...]
    inner = interior()
    lane = lane_ids((8, HEIGHT))
    pl.semaphore_wait(barrier, count - 1)
    for copy in copies[10:14]:
        copy.wait()
    stores = []
    for step in range(1, n_gx + 1):
        t = partner(n_gy * (step % n_gx))[1]["gx"]
        sides = [work[pl.ds(8 * t + 4 * h, 4)].reshape(4 * WIDTH, HEIGHT) for h in range(2)]
        out = dot_table(xtab, halved(pair_lanes(sides)))
        for h in range(2):
            side = out[:, HEIGHT * h:HEIGHT * (h + 1)].reshape(4, WIDTH, HEIGHT)
            full = []
            corner = []
            for s in range(4):
                k = 8 * t + 4 * h + s
                one = side[s] * inv[k]
                base[k] = jnp.where(inner, one, 0.0)
                full.append(one)
                corner.append(one[0:1])
            full = jnp.concatenate(full, 0)
            parts = halved(full)
            rows = dot_table(utab, parts)
            own = jnp.concatenate(corner + [jnp.zeros((4, HEIGHT), F32)], 0)
            rows = jnp.where(lane == 0, own, rows[:8])
            cols = dot_table(ctab, parts, ((1,), (1,)))
            edge = lane_ids((1, 4 * WIDTH)) % WIDTH == 0
            near = jnp.where(edge, cols[2:3], cols[0:1])
            far = jnp.where(edge, 0.0, cols[1:2])
            for g in range(2):
                at = slice(HEIGHT * g, HEIGHT * (g + 1))
                msg[4 * t + 2 * h + g] = jnp.concatenate(
                    [rows[2 * g:2 * g + 2], rows[4 + 2 * g:6 + 2 * g], near[:, at], far[:, at]],
                    0,
                )
        part = pl.ds(8 * t, 8)
        stores.append(pltpu.make_async_copy(base.at[part], base_hbm.at[part], store_sems.at[step - 1]))
        stores[-1].start()
        for ahead in range(1 if step == n_gx else 0, n_gy):
            send(msg, got, 0, n_gy * (step % n_gx) + ahead)
    for copy in copies[14:]:
        copy.wait()
    coef, table = owner_tables(own_ref[me], pair_ref[...], turned_ref[...], signs_ref[...])
    got[me] = msg[me]
    all_done(got, sems.at[0, 1])
    r = start_modes(n_gx, n_gy, [got[:, f, :] for f in range(6)])
    w = schur_modes(n_gx, n_gy, coef, table, *r)
    v = schur_modes(n_gx, n_gy, coef, table, *w)
    for f, field in enumerate(face_fields(n_gx, n_gy, r)):
        back[:, f, :] = field
    for f, field in enumerate(face_fields(n_gx, n_gy, w)):
        back[:, 8 + f, :] = field
    back[:, 6, :] = v[0][:, :HEIGHT]
    back[:, 7, :] = v[0][:, HEIGHT:]
    back[:, 14, :] = v[1]
    sums = (inner_product(r, r), inner_product(r, w), inner_product(w, w), inner_product(w, v))
    lanes = lane_ids((count, HEIGHT))
    back[:, 15, :] = sum(jnp.where(lanes == s, value, 0.0) for s, value in enumerate(sums))
    for off in range(1, count):
        send(back, landed, 1, off)
    landed[me] = back[me]
    for copy in stores:
        copy.wait()
    all_done(msg, sems.at[0, 0])
    all_done(landed, sems.at[1, 1])
    faces[...] = combine(landed[...])
    all_done(back, sems.at[1, 0])


def combine(landed):
    near, far = landed[:, :8], landed[:, 8:]
    total = jnp.sum(far[:, 7:8, :], 0)
    lane = lane_ids((1, HEIGHT))
    c0, c1 = steps([jnp.sum(jnp.where(lane == s, total, 0.0), 1, keepdims=True) for s in range(4)])
    c0, c1 = c0[None], c1[None]
    lead = near - c0 * far
    rest = [lead[:, 0:2] - c1 * near[:, 6:8], lead[:, 4:5] - c1 * far[:, 6:7], jnp.zeros_like(near[:, :5])]
    return jnp.concatenate([c0 * near + c1 * far] + rest, 1)


def stacked(left, right):
    lh, ll = halved(left)
    rh, rl = halved(right)
    lhs = jnp.concatenate([lh.astype(F32), lh.astype(F32), ll.astype(F32)], 0).astype(BF16)
    rhs = jnp.concatenate([rh.astype(F32), rl.astype(F32), rh.astype(F32)], 0).astype(BF16)
    return dot(lhs, rhs, ((0,), (0,)))


def inverse_kernel(
    faces_hbm, base_hbm, x_hbm, y_hbm, z_hbm, inv_hbm, small_hbm, square_hbm, potential_hbm, residual_hbm,
    faces, base, x, y, z, inv, small, square, potential, residual, work, load_sems, store_sems,
):
    pairs = [(faces_hbm, faces), (small_hbm, small), (square_hbm, square), (x_hbm, x), (y_hbm, y)]
    for t in range(DEPTH // 8):
        at = pl.ds(8 * t, 8)
        pairs += [(inv_hbm.at[at], inv.at[at]), (base_hbm.at[at], base.at[at])]
    pairs += [(z_hbm, z)]
    copies = [pltpu.make_async_copy(s, d, load_sems.at[n]) for n, (s, d) in enumerate(pairs)]
    for copy in copies:
        copy.start()
    for copy in copies[:3]:
        copy.wait()
    lane = lane_ids((8, HEIGHT))
    sub = lax.broadcasted_iota(jnp.int32, (8, HEIGHT), 0)
    const_left, const_right = small[0:8], small[8:16]
    cosines = square[2, :DEPTH, :DEPTH]
    half = DEPTH // 2
    rows = jnp.concatenate([faces[:, 8, :], faces[:, 9, :]], 0)
    rows = dot_exact(cosines, dot_exact(rows, square[0]))
    cols = dot_exact(faces[:, 10, :], square[1])
    cols = dot_exact(cosines, jnp.concatenate([cols[:, :WIDTH], cols[:, WIDTH:]], 0))
    cols = jnp.concatenate([cols[:half], cols[half:]], 1)
    cols = jnp.where(lane_ids((half, HEIGHT)) % WIDTH == 0, 0.0, cols)
    unit = jnp.where(lane == 0, 1.0, 0.0)
    mark = jnp.where(((sub == 0) & (lane == 0)) | ((sub == 1) & (lane == WIDTH)), 1.0, 0.0)
    for o in range(half):
        lhs = jnp.where(sub == 2, cols[o:o + 1], mark)
        rhs = jnp.where(sub == 0, rows[o:o + 1], jnp.where(sub == 1, rows[half + o:half + o + 1], jnp.where(sub == 2, unit, 0.0)))
        out = stacked(lhs, rhs)
        residual[2 * o] = out[:WIDTH]
        residual[2 * o + 1] = out[WIDTH:]
    stores = [pltpu.make_async_copy(residual, residual_hbm, store_sems.at[WIDTH // 16])]
    stores[0].start()
    copies[3].wait()
    copies[4].wait()
    xtab, ytab = x[...], y[...]
    for t in range(DEPTH // 8):
        copies[5 + 2 * t].wait()
        copies[6 + 2 * t].wait()
        sides = []
        for h in range(2):
            blocks = []
            for g in range(2):
                o = 4 * t + 2 * h + g
                one = faces[o, :8]
                lhs = jnp.where((sub >= 4) & (sub < 6) & (lane % WIDTH > 0), one, const_left)
                up = jnp.concatenate([one[2:], one[:2]], 0)
                rhs = jnp.where((sub < 4) & (lane > 0), one, const_right)
                rhs = jnp.where((sub >= 6) & (lane == 0), up, rhs)
                out = stacked(lhs, rhs)
                for s in range(2):
                    k = 2 * o + s
                    blocks.append(out[WIDTH * s:WIDTH * (s + 1)] * inv[k] + base[k])
            sides.append(jnp.concatenate(blocks, 0))
        out = dot_table(xtab, halved(pair_lanes(sides)))
        for h in range(2):
            side = dot_packed(out[:, HEIGHT * h:HEIGHT * (h + 1)], ytab)
            work[8 * t + 4 * h:8 * t + 4 * h + 4] = side.reshape(4, WIDTH, HEIGHT)
    copies[13].wait()
    ztab = z[...]
    for t in range(WIDTH // 16):
        sides = [work[:, 16 * t + 8 * h:16 * t + 8 * h + 8, :].reshape(DEPTH * 8, HEIGHT) for h in range(2)]
        out = dot_table(ztab, halved(pair_lanes(sides)))
        for h in range(2):
            side = out[:, HEIGHT * h:HEIGHT * (h + 1)]
            potential[:, 16 * t + 8 * h:16 * t + 8 * h + 8, :] = side.reshape(DEPTH, 8, HEIGHT)
        at = pl.ds(16 * t, 16)
        stores.append(pltpu.make_async_copy(potential.at[:, at, :], potential_hbm.at[:, at, :], store_sems.at[t]))
        stores[-1].start()
    for copy in stores:
        copy.wait()


def on_device_modes(n_gx, n_gy, charge, surface_charge):
    t = host_tables()
    count = n_gx * n_gy
    block = jax.ShapeDtypeStruct(charge.shape, F32)
    hbm = pl.BlockSpec(memory_space=pl.ANY)
    vmem = pl.BlockSpec(memory_space=pltpu.VMEM)

    def held(values):
        return [pltpu.VMEM(value.shape, value.dtype) for value in values]

    pair = np.concatenate([t["pair"], t["plane"][None]], 0)
    turned = np.concatenate([np.swapaxes(pair, 1, 2)] * 2, 2)
    args = [charge, surface_charge, t["zf"], t["x"], t["y"], t["ur"], t["uc"], t["inv"], t["own"], pair, turned, t["signs"]]
    six, sixteen = (count, 6, HEIGHT), (count, 16, HEIGHT)
    base, faces = pl.pallas_call(
        functools.partial(face_kernel, n_gx, n_gy),
        out_shape=(block, jax.ShapeDtypeStruct(sixteen, F32)),
        in_specs=[hbm] * len(args),
        out_specs=(hbm, vmem),
        scratch_shapes=held(args)
        + [pltpu.VMEM(shape, F32) for shape in (charge.shape, charge.shape, six, six, sixteen, sixteen)]
        + [
            pltpu.SemaphoreType.DMA((18,)),
            pltpu.SemaphoreType.DMA((DEPTH // 8,)),
            pltpu.SemaphoreType.DMA((2, 2)),
        ],
        compiler_params=pltpu.CompilerParams(collective_id=0, has_side_effects=True),
        name="faces",
    )(*args)
    small = np.concatenate([t["left"], t["right"]], 0)
    square = np.zeros((3, HEIGHT, HEIGHT), np.float32)
    square[0], square[1], square[2, :DEPTH, :DEPTH] = t["sy"], t["sx2"], t["cos"]
    args = [faces, base, t["x"], t["y"], t["zi"], t["inv"], small, square]
    return pl.pallas_call(
        inverse_kernel,
        out_shape=(block, block),
        in_specs=[hbm] * len(args),
        out_specs=(hbm, hbm),
        scratch_shapes=held(args)
        + [pltpu.VMEM(charge.shape, F32)] * 3
        + [pltpu.SemaphoreType.DMA((14,)), pltpu.SemaphoreType.DMA((WIDTH // 16 + 1,))],
        name="inverse",
    )(*args)


def solution(mesh):
    per_device = functools.partial(on_device_modes, mesh.shape["gx"], mesh.shape["gy"])
    if (mesh.shape["gx"], mesh.shape["gy"]) != (4, 4):
        per_device = on_device
    in_specs = (P(None, ("slab", "gx"), "gy"), P(None, ("slab", "gx"), "gy"))
    out_specs = (P(None, ("slab", "gx"), "gy"), P(None, ("slab", "gx"), "gy"))
    return jax.shard_map(
        per_device, mesh=mesh, in_specs=in_specs, out_specs=out_specs, check_vma=False
    )
```

```python
import functools

import jax
import jax.numpy as jnp
import ml_dtypes
import numpy as np
from jax import lax
from jax.experimental import pallas as pl
from jax.experimental.pallas import tpu as pltpu
from jax.sharding import PartitionSpec as P

ITERS = 2


SCREEN = 0.02


def padded(block, sides, width):
    for axis, dim in sides:
        count = lax.axis_size(axis)
        forward = [(i, i + 1) for i in range(count - 1)]
        forward.append((count - 1, 0))
        backward = [(target, source) for source, target in forward]
        low = lax.ppermute(
            lax.slice_in_dim(block, block.shape[dim] - width, None, axis=dim), axis, forward
        )
        high = lax.ppermute(lax.slice_in_dim(block, 0, width, axis=dim), axis, backward)
        block = jnp.concatenate([low, block, high], axis=dim)
    return block


def sine_full(count):
    index = jnp.arange(count).astype(jnp.float32)
    return jnp.sqrt(2.0 / count) * jnp.sin(jnp.pi * jnp.outer(index, index) / count)


def cosine_table(count):
    place = jnp.arange(count).astype(jnp.float32) + 0.5
    order = jnp.arange(count).astype(jnp.float32)
    factor = jnp.where(order == 0.0, jnp.sqrt(1.0 / count), jnp.sqrt(2.0 / count))
    return factor[None, :] * jnp.cos(jnp.pi * jnp.outer(place, order) / count)


def spectrum_table(depth, width, height):
    across = 2.0 - 2.0 * jnp.cos(jnp.pi * jnp.arange(width).astype(jnp.float32) / width)
    along = 2.0 - 2.0 * jnp.cos(jnp.pi * jnp.arange(height).astype(jnp.float32) / height)
    vertical = 2.0 - 2.0 * jnp.cos(jnp.pi * jnp.arange(depth).astype(jnp.float32) / depth)
    return SCREEN + vertical[:, None, None] + across[None, :, None] + along[None, None, :]


def apply_full(field):
    row_rims = jnp.stack([field[:, 0, :], field[:, -1, :]], 1)
    row_ext = padded(row_rims, (("gx", 1),), 1)
    col_rims = jnp.stack([field[:, :, 0], field[:, :, -1]], 0)
    col_ext = padded(col_rims, (("gy", 0),), 1)
    from_below_x = jnp.concatenate([row_ext[:, 0:1, :], field[:, :-1, :]], 1)
    from_above_x = jnp.concatenate([field[:, 1:, :], row_ext[:, 3:4, :]], 1)
    from_below_y = jnp.concatenate([col_ext[0][:, :, None], field[:, :, :-1]], 2)
    from_above_y = jnp.concatenate([field[:, :, 1:], col_ext[3][:, :, None]], 2)
    beside = from_below_x + from_above_x + from_below_y + from_above_y
    upper = jnp.concatenate([field[1:], field[-1:]], 0)
    lower = jnp.concatenate([field[:1], field[:-1]], 0)
    return (6.0 + SCREEN) * field - beside - upper - lower


def solve_interior(field, sines_x, sines_y, cosines, spectrum):
    high = lax.Precision.HIGHEST
    depth, width, height = field.shape
    hat = jnp.dot(field.reshape(depth * width, height), sines_y, precision=high).reshape(
        depth, width, height
    )
    hat = jnp.matmul(sines_x, hat, precision=high)
    hat = jnp.dot(cosines.T, hat.reshape(depth, width * height), precision=high).reshape(
        depth, width, height
    )
    hat = hat / spectrum
    back = jnp.dot(cosines, hat.reshape(depth, width * height), precision=high).reshape(
        depth, width, height
    )
    back = jnp.matmul(sines_x, back, precision=high)
    back = jnp.dot(back.reshape(depth * width, height), sines_y, precision=high)
    return back.reshape(depth, width, height)


def norm_total(residual):
    return lax.psum(jnp.sum(residual * residual), ("gx", "gy"))


def curvature_total(direction, image):
    return lax.psum(jnp.sum(direction * image), ("gx", "gy"))


def on_device(charge, surface_charge):
    depth, width, height = charge.shape
    sines_x = sine_full(width)
    sines_y = sine_full(height)
    cosines = cosine_table(depth)
    spectrum = spectrum_table(depth, width, height)
    row_place = lax.broadcasted_iota(jnp.int32, (1, width, height), 1)
    col_place = lax.broadcasted_iota(jnp.int32, (1, width, height), 2)
    gamma = jnp.where((row_place == 0) | (col_place == 0), 1.0, 0.0).astype(jnp.float32)
    source = charge.at[0].add(surface_charge[0]).at[-1].add(surface_charge[1])
    base = solve_interior(source, sines_x, sines_y, cosines, spectrum)
    reduced = gamma * (source - apply_full(base))
    iterate = jnp.zeros_like(reduced)
    residual = reduced
    direction = reduced
    norm_now = norm_total(residual)
    for step in range(ITERS):
        lifted = -solve_interior(apply_full(direction), sines_x, sines_y, cosines, spectrum)
        image, lifted = (gamma * apply_full(direction + lifted), lifted)
        alpha = norm_now / curvature_total(direction, image)
        iterate = iterate + alpha * direction
        residual = residual - alpha * image
        if step + 1 < ITERS:
            norm_next = norm_total(residual)
            direction = residual + norm_next / norm_now * direction
            norm_now = norm_next
    correction = -solve_interior(apply_full(iterate), sines_x, sines_y, cosines, spectrum)
    potential = iterate + base + correction
    return (potential, residual)


DEPTH, WIDTH, HEIGHT = 32, 64, 128
F32, BF16 = jnp.float32, jnp.bfloat16


def halves(table):
    table = np.asarray(table, np.float64)
    high = table.astype(np.float32).astype(ml_dtypes.bfloat16)
    low = (table - high.astype(np.float64)).astype(np.float32).astype(ml_dtypes.bfloat16)
    return high, low


def sine_unit(count):
    index = np.arange(count)
    table = np.sqrt(2.0 / count) * np.sin(np.pi * np.outer(index, index) / count)
    table[0, 0] = 1.0
    return table


def host_tables():
    place, order = np.arange(DEPTH) + 0.5, np.arange(DEPTH)
    factor = np.where(order == 0, np.sqrt(1.0 / DEPTH), np.sqrt(2.0 / DEPTH))
    cosines = factor[None, :] * np.cos(np.pi * np.outer(place, order) / DEPTH)
    sin_x, sin_y = sine_unit(WIDTH), sine_unit(HEIGHT)
    vertical = 2.0 - 2.0 * np.cos(np.pi * order / DEPTH)
    across = 2.0 - 2.0 * np.cos(np.pi * np.arange(WIDTH) / WIDTH)
    along = 2.0 - 2.0 * np.cos(np.pi * np.arange(HEIGHT) / HEIGHT)
    ux = np.sqrt(2.0 / WIDTH) * np.sin(np.pi * np.arange(WIDTH) / WIDTH)
    uy = np.sqrt(2.0 / HEIGHT) * np.sin(np.pi * np.arange(HEIGHT) / HEIGHT)
    sx = np.where(np.arange(WIDTH) % 2 == 1, 1.0, -1.0)
    sy = np.where(np.arange(HEIGHT) % 2 == 1, 1.0, -1.0)
    sx[0] = sy[0] = 0.0
    ex, ey = np.eye(WIDTH)[0], np.eye(HEIGHT)[0]
    t = {}
    t["zf"] = np.concatenate(halves(np.kron(cosines.T, np.eye(8))))
    t["zi"] = np.concatenate(halves(np.kron(cosines, np.eye(8))))
    t["x"] = np.concatenate(halves(np.kron(np.eye(4), sin_x)))
    y_both = np.concatenate(halves(sin_y), 1)
    t["y"] = np.concatenate([y_both, y_both], 0)
    plane = SCREEN + across[:, None] + along[None, :]
    t["plane"] = plane.astype(np.float32)
    ur = np.concatenate([np.kron(np.eye(4), (ux + ex)[None]), np.kron(np.eye(4), (ux * sx)[None]), np.zeros((8, 4 * WIDTH))], 0)
    t["ur"] = np.concatenate(halves(ur))
    uc = np.zeros((16, HEIGHT))
    uc[0], uc[1], uc[2] = uy + ey, uy * sy, ey
    t["uc"] = np.concatenate(halves(uc))
    spec = plane[None] + vertical[:, None, None]
    inner = np.zeros((WIDTH, HEIGHT))
    inner[1:, 1:] = 1.0
    inv = inner / spec
    t["inv"] = np.where(inner > 0, inv, 1.0).astype(np.float32)
    row_near = np.einsum("a,kab->kb", ux * ux, inv)
    row_far = np.einsum("a,kab->kb", ux * ux * sx, inv)
    col_near = np.einsum("b,kab->ka", uy * uy, inv)
    col_far = np.einsum("b,kab->ka", uy * uy * sy, inv)
    row_coef = SCREEN + vertical[:, None] + 2.0 + along[None, :] - 2.0 * row_near
    col_coef = SCREEN + vertical[:, None] + 2.0 + across[None, :] - 2.0 * col_near
    row_coef[:, 0] = SCREEN + vertical + 4.0
    col_coef[:, 0] = 0.0
    own = np.zeros((DEPTH // 2, 8, HEIGHT))
    own[:, 0], own[:, 1] = row_coef[0::2], row_coef[1::2]
    own[:, 2], own[:, 3] = row_far[0::2], row_far[1::2]
    own[:, 4] = np.concatenate([col_coef[0::2], col_coef[1::2]], 1)
    own[:, 5] = np.concatenate([col_far[0::2], col_far[1::2]], 1)
    own[:, 6], own[:, 7] = vertical[0::2, None], vertical[1::2, None]
    t["own"] = own.astype(np.float32)
    border = np.zeros((WIDTH, HEIGHT))
    border[0], border[:, 0] = uy, ux
    t["pair"] = np.stack([np.outer(ux, uy), border]).astype(np.float32)
    signs = np.zeros((8, HEIGHT))
    signs[0] = sy
    signs[1] = np.concatenate([sx, sx])
    t["signs"] = signs.astype(np.float32)
    zero = np.zeros(WIDTH)
    left = np.zeros((8, HEIGHT))
    left[0], left[1] = np.concatenate([ux + ex, zero]), np.concatenate([zero, ux + ex])
    left[2], left[3] = np.concatenate([ux * sx, zero]), np.concatenate([zero, ux * sx])
    left[6], left[7] = np.concatenate([ex, zero]), np.concatenate([zero, ex])
    right = np.zeros((8, HEIGHT))
    right[4], right[5] = uy + ey, uy * sy
    t["left"], t["right"] = left.astype(np.float32), right.astype(np.float32)
    split = np.concatenate([np.arange(0, DEPTH, 2), np.arange(1, DEPTH, 2)])
    pair_x = np.concatenate(halves(np.kron(np.eye(2), sin_x)), 1)
    wide = np.zeros((DEPTH, 2 * HEIGHT))
    wide[:, :DEPTH] = cosines[split][:, split]
    t["square"] = np.concatenate([pair_x, pair_x] + list(halves(wide)), 0)
    return t


def halved(x):
    high = x.astype(BF16)
    return high, (x - high.astype(F32)).astype(BF16)


def dot(a, b, dims=((1,), (0,))):
    return lax.dot_general(a, b, (dims, ((), ())), preferred_element_type=F32)


def dot_table(table, b, dims=((1,), (0,))):
    count = table.shape[0] // 2
    both = dot(table, b[0], dims)
    return both[:count] + (both[count:] + dot(table[:count], b[1], dims))


def dot_packed(x, table):
    out = dot(jnp.concatenate(halved(x), 1), table)
    half = out.shape[1] // 2
    return out[:, :half] + out[:, half:]


def dot_exact(a, b, dims=((1,), (0,))):
    return lax.dot_general(
        a, b, (dims, ((), ())), precision=lax.Precision.HIGHEST, preferred_element_type=F32
    )


def lane_ids(shape):
    return lax.broadcasted_iota(jnp.int32, shape, len(shape) - 1)


def interior():
    row = lax.broadcasted_iota(jnp.int32, (WIDTH, HEIGHT), 0)
    return (row > 0) & (lane_ids((WIDTH, HEIGHT)) > 0)


def pair_lanes(parts):
    return jnp.concatenate(parts, 1)


def shift_x(n_gx, n_gy, field, by):
    cut = (by % n_gx) * n_gy
    return jnp.concatenate([field[cut:], field[:cut]], 0)


def shift_y(n_gx, n_gy, field, by):
    place = lax.broadcasted_iota(jnp.int32, field.shape, 0) % n_gy
    count = n_gx * n_gy
    ahead = by % count
    plain = jnp.concatenate([field[ahead:], field[:ahead]], 0)
    wrap = (by - n_gy if by > 0 else by + n_gy) % count
    wrapped = jnp.concatenate([field[wrap:], field[:wrap]], 0)
    edge = n_gy - 1 if by > 0 else 0
    return jnp.where(place == edge, wrapped, plain)


def turn_half(x):
    return jnp.concatenate([x[:, WIDTH:], x[:, :WIDTH]], 1)


def schur_modes(n_gx, n_gy, coef, table, row, col):
    row_coef, row_far, col_coef, col_far, row_sign, col_sign = coef
    sx = functools.partial(shift_x, n_gx, n_gy)
    sy = functools.partial(shift_y, n_gx, n_gy)
    count = n_gx * n_gy
    across = jnp.concatenate(halved(jnp.concatenate([col, col * col_sign], 0)), 1)
    across = dot(across, table[0]) + dot(across, table[1])
    along = dot(jnp.concatenate(halved(jnp.concatenate([row, row * row_sign], 0)), 0), table[2])
    along = along[:2 * count] + along[2 * count:]
    along = along[:, :HEIGHT] + along[:, HEIGHT:]
    v = across[:count] + sx(across[count:], -1)
    w = along[:count] + sy(along[count:], -1)
    row_out = row_coef * row - row_far * (sx(row, 1) + sx(row, -1)) - v - row_sign * sy(v, 1)
    col_out = col_coef * col - col_far * (sy(col, 1) + sy(col, -1)) - w - col_sign * sx(w, 1)
    lane = lane_ids((count, HEIGHT))
    row_out = row_out - jnp.concatenate(
        [jnp.where(lane == 0, w, 0.0), jnp.where(lane == 0, turn_half(w), 0.0)], 1
    )
    col_out = jnp.where(
        lane == 0, row_out[:, :HEIGHT], jnp.where(lane == WIDTH, turn_half(row_out[:, HEIGHT:]), col_out)
    )
    return row_out, col_out


def owner_tables(own, pair, turned, signs):
    inner = interior()
    blank = jnp.zeros((WIDTH, HEIGHT), F32)
    lane = lane_ids((HEIGHT, HEIGHT))
    inside = (lane % WIDTH > 0) & (lax.broadcasted_iota(jnp.int32, (HEIGHT, HEIGHT), 0) > 0)
    parts, other = [], []
    for s in range(2):
        vert = own[6 + s:7 + s]
        parts.append(jnp.where(inner, pair[0] / (pair[2] + vert), pair[1]))
        one = jnp.where(inside, turned[0] / (turned[2] + vert), turned[1])
        other.append(jnp.where((lane < WIDTH) == (s == 0), one, 0.0))
    high, low = halved(jnp.concatenate([pair_lanes([parts[0], blank]), pair_lanes([blank, parts[1]])], 0))
    table = (
        jnp.concatenate([high, high], 0),
        jnp.concatenate([low, low], 0),
        jnp.concatenate(halved(jnp.concatenate(other, 0)), 1),
    )
    coef = (
        pair_lanes([own[0:1], own[1:2]]),
        pair_lanes([own[2:3], own[3:4]]),
        own[4:5],
        own[5:6],
        pair_lanes([signs[0:1], signs[0:1]]),
        signs[1:2],
    )
    return coef, table


def start_modes(n_gx, n_gy, fields):
    sx = functools.partial(shift_x, n_gx, n_gy)
    sy = functools.partial(shift_y, n_gx, n_gy)
    row = pair_lanes([fields[0], fields[1]]) + sx(pair_lanes([fields[2], fields[3]]), -1)
    col = fields[4] + sy(fields[5], -1)
    return row, col


def inner_product(first, second):
    lane = lane_ids(first[1].shape)
    cols = jnp.where(lane % WIDTH == 0, 0.0, first[1] * second[1])
    rows = first[0] * second[0]
    down = jnp.sum(rows[:, :HEIGHT] + rows[:, HEIGHT:] + cols, 0, keepdims=True)
    return jnp.sum(down, 1, keepdims=True)


def face_fields(n_gx, n_gy, pair):
    row, col = pair
    beyond = shift_x(n_gx, n_gy, row, 1)
    return [
        row[:, :HEIGHT], row[:, HEIGHT:], beyond[:, :HEIGHT], beyond[:, HEIGHT:],
        col, shift_y(n_gx, n_gy, col, 1),
    ]


def steps(sums):
    rr, rw, ww, wv = sums
    alpha = rr / rw
    after = alpha * alpha * ww - rr
    beta = after / rr
    curve = (1 + beta) * (1 + beta) * rw - 2 * (1 + beta) * alpha * ww + alpha * alpha * wv
    second = after / curve
    return alpha + second * (1 + beta), -second * alpha


def face_kernel(
    n_gx, n_gy,
    charge_hbm, surface_hbm, z_hbm, x_hbm, y_hbm, ur_hbm, uc_hbm, inv_hbm, own_hbm, pair_hbm, turned_hbm, signs_hbm,
    base_hbm, faces,
    charge, surface, z, x, y, ur, uc, inv, own_ref, pair_ref, turned_ref, signs_ref,
    work, base, msg, got, back, landed, load_sems, store_sems, sems,
):
    count = n_gx * n_gy
    gx, gy = lax.axis_index("gx"), lax.axis_index("gy")
    me = gx * n_gy + gy
    pairs = [(z_hbm, z), (surface_hbm, surface)]
    pairs += [(charge_hbm.at[:, pl.ds(16 * t, 16), :], charge.at[:, pl.ds(16 * t, 16), :]) for t in range(WIDTH // 16)]
    pairs += [(y_hbm, y), (x_hbm, x), (ur_hbm, ur), (uc_hbm, uc)]
    pairs += [(inv_hbm.at[pl.ds(8 * t, 8)], inv.at[pl.ds(8 * t, 8)]) for t in range(DEPTH // 8)]
    pairs += [(own_hbm, own_ref), (pair_hbm, pair_ref), (turned_hbm, turned_ref), (signs_hbm, signs_ref)]
    copies = [pltpu.make_async_copy(s, d, load_sems.at[n]) for n, (s, d) in enumerate(pairs)]
    for copy in copies:
        copy.start()

    def partner(off):
        to_x, to_y = gx + off // n_gy, gy + off % n_gy
        to_x = jnp.where(to_x >= n_gx, to_x - n_gx, to_x)
        to_y = jnp.where(to_y >= n_gy, to_y - n_gy, to_y)
        return to_x * n_gy + to_y, {"gx": to_x, "gy": to_y}

    def send(source, target, which, off):
        to, device = partner(off)
        copy = pltpu.make_async_remote_copy(
            src_ref=source.at[to],
            dst_ref=target.at[me],
            send_sem=sems.at[which, 0],
            recv_sem=sems.at[which, 1],
            device_id=device,
            device_id_type=pl.DeviceIdType.MESH,
        )
        copy.start()

    def all_done(buffer, sem):
        whole = buffer.at[pl.ds(0, count - 1)]
        pltpu.make_async_copy(whole, whole, sem).wait()

    barrier = pltpu.get_barrier_semaphore()
    for off in range(1, count):
        pl.semaphore_signal(barrier, inc=1, device_id=partner(off)[1], device_id_type=pl.DeviceIdType.MESH)
    copies[0].wait()
    copies[1].wait()
    ztab = z[...]
    for t in range(WIDTH // 16):
        copies[2 + t].wait()
        sides = []
        for h in range(2):
            at = pl.ds(16 * t + 8 * h, 8)
            block = charge[:, at, :]
            block = jnp.concatenate(
                [block[:1] + surface[0:1, at, :], block[1:-1], block[-1:] + surface[1:2, at, :]], 0
            )
            sides.append(block.reshape(DEPTH * 8, HEIGHT))
        out = dot_table(ztab, halved(pair_lanes(sides)))
        if t == 0:
            copies[6].wait()
            ytab = y[...]
        for h in range(2):
            side = out[:, HEIGHT * h:HEIGHT * (h + 1)]
            side = dot_packed(side, ytab)
            work[:, 16 * t + 8 * h:16 * t + 8 * h + 8, :] = side.reshape(DEPTH, 8, HEIGHT)
    for copy in copies[7:10]:
        copy.wait()
    xtab, utab, ctab = x[...], ur[...], uc[...]
    inner = interior()
    lane = lane_ids((8, HEIGHT))
    pl.semaphore_wait(barrier, count - 1)
    for copy in copies[10:14]:
        copy.wait()
    stores = []
    for step in range(1, n_gx + 1):
        t = partner(n_gy * (step % n_gx))[1]["gx"]
        sides = [work[pl.ds(8 * t + 4 * h, 4)].reshape(4 * WIDTH, HEIGHT) for h in range(2)]
        out = dot_table(xtab, halved(pair_lanes(sides)))
        for h in range(2):
            side = out[:, HEIGHT * h:HEIGHT * (h + 1)].reshape(4, WIDTH, HEIGHT)
            full = []
            corner = []
            for s in range(4):
                k = 8 * t + 4 * h + s
                one = side[s] * inv[k]
                base[k] = jnp.where(inner, one, 0.0)
                full.append(one)
                corner.append(one[0:1])
            full = jnp.concatenate(full, 0)
            parts = halved(full)
            rows = dot_table(utab, parts)
            own = jnp.concatenate(corner + [jnp.zeros((4, HEIGHT), F32)], 0)
            rows = jnp.where(lane == 0, own, rows[:8])
            cols = dot_table(ctab, parts, ((1,), (1,)))
            edge = lane_ids((1, 4 * WIDTH)) % WIDTH == 0
            near = jnp.where(edge, cols[2:3], cols[0:1])
            far = jnp.where(edge, 0.0, cols[1:2])
            for g in range(2):
                at = slice(HEIGHT * g, HEIGHT * (g + 1))
                msg[4 * t + 2 * h + g] = jnp.concatenate(
                    [rows[2 * g:2 * g + 2], rows[4 + 2 * g:6 + 2 * g], near[:, at], far[:, at]],
                    0,
                )
        part = pl.ds(8 * t, 8)
        stores.append(pltpu.make_async_copy(base.at[part], base_hbm.at[part], store_sems.at[step - 1]))
        stores[-1].start()
        for ahead in range(1 if step == n_gx else 0, n_gy):
            send(msg, got, 0, n_gy * (step % n_gx) + ahead)
    for copy in copies[14:]:
        copy.wait()
    coef, table = owner_tables(own_ref[me], pair_ref[...], turned_ref[...], signs_ref[...])
    got[me] = msg[me]
    all_done(got, sems.at[0, 1])
    r = start_modes(n_gx, n_gy, [got[:, f, :] for f in range(6)])
    w = schur_modes(n_gx, n_gy, coef, table, *r)
    v = schur_modes(n_gx, n_gy, coef, table, *w)
    for f, field in enumerate(face_fields(n_gx, n_gy, r)):
        back[:, f, :] = field
    for f, field in enumerate(face_fields(n_gx, n_gy, w)):
        back[:, 8 + f, :] = field
    back[:, 6, :] = v[0][:, :HEIGHT]
    back[:, 7, :] = v[0][:, HEIGHT:]
    back[:, 14, :] = v[1]
    sums = (inner_product(r, r), inner_product(r, w), inner_product(w, w), inner_product(w, v))
    lanes = lane_ids((count, HEIGHT))
    back[:, 15, :] = sum(jnp.where(lanes == s, value, 0.0) for s, value in enumerate(sums))
    for off in range(1, count):
        send(back, landed, 1, off)
    landed[me] = back[me]
    for copy in stores:
        copy.wait()
    all_done(msg, sems.at[0, 0])
    all_done(landed, sems.at[1, 1])
    faces[...] = combine(landed[...])
    all_done(back, sems.at[1, 0])


def combine(landed):
    near, far = landed[:, :8], landed[:, 8:]
    total = jnp.sum(far[:, 7:8, :], 0)
    lane = lane_ids((1, HEIGHT))
    c0, c1 = steps([jnp.sum(jnp.where(lane == s, total, 0.0), 1, keepdims=True) for s in range(4)])
    c0, c1 = c0[None], c1[None]
    lead = near - c0 * far
    rest = [lead[:, 0:2] - c1 * near[:, 6:8], lead[:, 4:5] - c1 * far[:, 6:7], jnp.zeros_like(near[:, :5])]
    return jnp.concatenate([c0 * near + c1 * far] + rest, 1)


def stacked(left, right):
    lh, ll = halved(left)
    rh, rl = halved(right)
    lhs = jnp.concatenate([lh.astype(F32), lh.astype(F32), ll.astype(F32)], 0).astype(BF16)
    rhs = jnp.concatenate([rh.astype(F32), rl.astype(F32), rh.astype(F32)], 0).astype(BF16)
    return dot(lhs, rhs, ((0,), (0,)))


def inverse_kernel(
    faces_hbm, base_hbm, x_hbm, y_hbm, z_hbm, inv_hbm, small_hbm, square_hbm, potential_hbm, residual_hbm,
    faces, base, x, y, z, inv, small, square, potential, residual, work, load_sems, store_sems,
):
    pairs = [(faces_hbm, faces), (small_hbm, small), (square_hbm, square), (x_hbm, x), (y_hbm, y)]
    for t in range(DEPTH // 8):
        at = pl.ds(8 * t, 8)
        pairs += [(inv_hbm.at[at], inv.at[at]), (base_hbm.at[at], base.at[at])]
    pairs += [(z_hbm, z)]
    copies = [pltpu.make_async_copy(s, d, load_sems.at[n]) for n, (s, d) in enumerate(pairs)]
    for copy in copies:
        copy.start()
    for copy in copies[:5]:
        copy.wait()
    lane = lane_ids((8, HEIGHT))
    sub = lax.broadcasted_iota(jnp.int32, (8, HEIGHT), 0)
    const_left, const_right = small[0:8], small[8:16]
    xtab, ytab = x[...], y[...]
    copies[5].wait()
    copies[6].wait()
    half = DEPTH // 2
    rows = dot_packed(jnp.concatenate([faces[:, 8, :], faces[:, 9, :]], 0), ytab)
    cols = dot_packed(faces[:, 10, :], square[0:2 * HEIGHT])
    cols = jnp.concatenate([cols[:, :WIDTH], cols[:, WIDTH:]], 0)
    both = jnp.concatenate([rows, cols, jnp.zeros_like(cols)], 1)
    both = dot_table(square[2 * HEIGHT:, :DEPTH], halved(both))
    rows, cols = both[:, :HEIGHT], both[:, HEIGHT:HEIGHT + WIDTH]
    cols = jnp.concatenate([cols[:half], cols[half:]], 1)
    cols = jnp.where(lane_ids((half, HEIGHT)) % WIDTH == 0, 0.0, cols)
    unit = jnp.where(lane == 0, 1.0, 0.0)
    mark = jnp.where(((sub == 0) & (lane == 0)) | ((sub == 1) & (lane == WIDTH)), 1.0, 0.0)
    for o in range(half):
        lhs = jnp.where(sub == 2, cols[o:o + 1], mark)
        rhs = jnp.where(sub == 0, rows[o:o + 1], jnp.where(sub == 1, rows[half + o:half + o + 1], jnp.where(sub == 2, unit, 0.0)))
        out = stacked(lhs, rhs)
        residual[2 * o] = out[:WIDTH]
        residual[2 * o + 1] = out[WIDTH:]
    for t in range(DEPTH // 8):
        if t > 0:
            copies[5 + 2 * t].wait()
            copies[6 + 2 * t].wait()
        sides = []
        for h in range(2):
            blocks = []
            for g in range(2):
                o = 4 * t + 2 * h + g
                one = faces[o, :8]
                lhs = jnp.where((sub >= 4) & (sub < 6) & (lane % WIDTH > 0), one, const_left)
                up = jnp.concatenate([one[2:], one[:2]], 0)
                rhs = jnp.where((sub < 4) & (lane > 0), one, const_right)
                rhs = jnp.where((sub >= 6) & (lane == 0), up, rhs)
                out = stacked(lhs, rhs)
                for s in range(2):
                    k = 2 * o + s
                    blocks.append(out[WIDTH * s:WIDTH * (s + 1)] * inv[k] + base[k])
            sides.append(jnp.concatenate(blocks, 0))
        out = dot_table(xtab, halved(pair_lanes(sides)))
        for h in range(2):
            side = dot_packed(out[:, HEIGHT * h:HEIGHT * (h + 1)], ytab)
            work[8 * t + 4 * h:8 * t + 4 * h + 4] = side.reshape(4, WIDTH, HEIGHT)
        if t == 0:
            stores = [pltpu.make_async_copy(residual, residual_hbm, store_sems.at[WIDTH // 16])]
            stores[0].start()
    copies[13].wait()
    ztab = z[...]
    for t in range(WIDTH // 16):
        sides = [work[:, 16 * t + 8 * h:16 * t + 8 * h + 8, :].reshape(DEPTH * 8, HEIGHT) for h in range(2)]
        out = dot_table(ztab, halved(pair_lanes(sides)))
        for h in range(2):
            side = out[:, HEIGHT * h:HEIGHT * (h + 1)]
            potential[:, 16 * t + 8 * h:16 * t + 8 * h + 8, :] = side.reshape(DEPTH, 8, HEIGHT)
        at = pl.ds(16 * t, 16)
        stores.append(pltpu.make_async_copy(potential.at[:, at, :], potential_hbm.at[:, at, :], store_sems.at[t]))
        stores[-1].start()
    for copy in stores:
        copy.wait()


def on_device_modes(n_gx, n_gy, charge, surface_charge):
    t = host_tables()
    count = n_gx * n_gy
    block = jax.ShapeDtypeStruct(charge.shape, F32)
    hbm = pl.BlockSpec(memory_space=pl.ANY)
    vmem = pl.BlockSpec(memory_space=pltpu.VMEM)

    def held(values):
        return [pltpu.VMEM(value.shape, value.dtype) for value in values]

    pair = np.concatenate([t["pair"], t["plane"][None]], 0)
    turned = np.concatenate([np.swapaxes(pair, 1, 2)] * 2, 2)
    args = [charge, surface_charge, t["zf"], t["x"], t["y"], t["ur"], t["uc"], t["inv"], t["own"], pair, turned, t["signs"]]
    six, sixteen = (count, 6, HEIGHT), (count, 16, HEIGHT)
    base, faces = pl.pallas_call(
        functools.partial(face_kernel, n_gx, n_gy),
        out_shape=(block, jax.ShapeDtypeStruct(sixteen, F32)),
        in_specs=[hbm] * len(args),
        out_specs=(hbm, vmem),
        scratch_shapes=held(args)
        + [pltpu.VMEM(shape, F32) for shape in (charge.shape, charge.shape, six, six, sixteen, sixteen)]
        + [
            pltpu.SemaphoreType.DMA((18,)),
            pltpu.SemaphoreType.DMA((DEPTH // 8,)),
            pltpu.SemaphoreType.DMA((2, 2)),
        ],
        compiler_params=pltpu.CompilerParams(collective_id=0, has_side_effects=True),
        name="faces",
    )(*args)
    small = np.concatenate([t["left"], t["right"]], 0)
    args = [faces, base, t["x"], t["y"], t["zi"], t["inv"], small, t["square"]]
    return pl.pallas_call(
        inverse_kernel,
        out_shape=(block, block),
        in_specs=[hbm] * len(args),
        out_specs=(hbm, hbm),
        scratch_shapes=held(args)
        + [pltpu.VMEM(charge.shape, F32)] * 3
        + [pltpu.SemaphoreType.DMA((14,)), pltpu.SemaphoreType.DMA((WIDTH // 16 + 1,))],
        name="inverse",
    )(*args)


def solution(mesh):
    per_device = functools.partial(on_device_modes, mesh.shape["gx"], mesh.shape["gy"])
    if (mesh.shape["gx"], mesh.shape["gy"]) != (4, 4):
        per_device = on_device
    in_specs = (P(None, ("slab", "gx"), "gy"), P(None, ("slab", "gx"), "gy"))
    out_specs = (P(None, ("slab", "gx"), "gy"), P(None, ("slab", "gx"), "gy"))
    return jax.shard_map(
        per_device, mesh=mesh, in_specs=in_specs, out_specs=out_specs, check_vma=False
    )
```

```python
import functools

import jax
import jax.numpy as jnp
import ml_dtypes
import numpy as np
from jax import lax
from jax.experimental import pallas as pl
from jax.experimental.pallas import tpu as pltpu
from jax.sharding import PartitionSpec as P

ITERS = 2


SCREEN = 0.02


def padded(block, sides, width):
    for axis, dim in sides:
        count = lax.axis_size(axis)
        forward = [(i, i + 1) for i in range(count - 1)]
        forward.append((count - 1, 0))
        backward = [(target, source) for source, target in forward]
        low = lax.ppermute(
            lax.slice_in_dim(block, block.shape[dim] - width, None, axis=dim), axis, forward
        )
        high = lax.ppermute(lax.slice_in_dim(block, 0, width, axis=dim), axis, backward)
        block = jnp.concatenate([low, block, high], axis=dim)
    return block


def sine_full(count):
    index = jnp.arange(count).astype(jnp.float32)
    return jnp.sqrt(2.0 / count) * jnp.sin(jnp.pi * jnp.outer(index, index) / count)


def cosine_table(count):
    place = jnp.arange(count).astype(jnp.float32) + 0.5
    order = jnp.arange(count).astype(jnp.float32)
    factor = jnp.where(order == 0.0, jnp.sqrt(1.0 / count), jnp.sqrt(2.0 / count))
    return factor[None, :] * jnp.cos(jnp.pi * jnp.outer(place, order) / count)


def spectrum_table(depth, width, height):
    across = 2.0 - 2.0 * jnp.cos(jnp.pi * jnp.arange(width).astype(jnp.float32) / width)
    along = 2.0 - 2.0 * jnp.cos(jnp.pi * jnp.arange(height).astype(jnp.float32) / height)
    vertical = 2.0 - 2.0 * jnp.cos(jnp.pi * jnp.arange(depth).astype(jnp.float32) / depth)
    return SCREEN + vertical[:, None, None] + across[None, :, None] + along[None, None, :]


def apply_full(field):
    row_rims = jnp.stack([field[:, 0, :], field[:, -1, :]], 1)
    row_ext = padded(row_rims, (("gx", 1),), 1)
    col_rims = jnp.stack([field[:, :, 0], field[:, :, -1]], 0)
    col_ext = padded(col_rims, (("gy", 0),), 1)
    from_below_x = jnp.concatenate([row_ext[:, 0:1, :], field[:, :-1, :]], 1)
    from_above_x = jnp.concatenate([field[:, 1:, :], row_ext[:, 3:4, :]], 1)
    from_below_y = jnp.concatenate([col_ext[0][:, :, None], field[:, :, :-1]], 2)
    from_above_y = jnp.concatenate([field[:, :, 1:], col_ext[3][:, :, None]], 2)
    beside = from_below_x + from_above_x + from_below_y + from_above_y
    upper = jnp.concatenate([field[1:], field[-1:]], 0)
    lower = jnp.concatenate([field[:1], field[:-1]], 0)
    return (6.0 + SCREEN) * field - beside - upper - lower


def solve_interior(field, sines_x, sines_y, cosines, spectrum):
    high = lax.Precision.HIGHEST
    depth, width, height = field.shape
    hat = jnp.dot(field.reshape(depth * width, height), sines_y, precision=high).reshape(
        depth, width, height
    )
    hat = jnp.matmul(sines_x, hat, precision=high)
    hat = jnp.dot(cosines.T, hat.reshape(depth, width * height), precision=high).reshape(
        depth, width, height
    )
    hat = hat / spectrum
    back = jnp.dot(cosines, hat.reshape(depth, width * height), precision=high).reshape(
        depth, width, height
    )
    back = jnp.matmul(sines_x, back, precision=high)
    back = jnp.dot(back.reshape(depth * width, height), sines_y, precision=high)
    return back.reshape(depth, width, height)


def norm_total(residual):
    return lax.psum(jnp.sum(residual * residual), ("gx", "gy"))


def curvature_total(direction, image):
    return lax.psum(jnp.sum(direction * image), ("gx", "gy"))


def on_device(charge, surface_charge):
    depth, width, height = charge.shape
    sines_x = sine_full(width)
    sines_y = sine_full(height)
    cosines = cosine_table(depth)
    spectrum = spectrum_table(depth, width, height)
    row_place = lax.broadcasted_iota(jnp.int32, (1, width, height), 1)
    col_place = lax.broadcasted_iota(jnp.int32, (1, width, height), 2)
    gamma = jnp.where((row_place == 0) | (col_place == 0), 1.0, 0.0).astype(jnp.float32)
    source = charge.at[0].add(surface_charge[0]).at[-1].add(surface_charge[1])
    base = solve_interior(source, sines_x, sines_y, cosines, spectrum)
    reduced = gamma * (source - apply_full(base))
    iterate = jnp.zeros_like(reduced)
    residual = reduced
    direction = reduced
    norm_now = norm_total(residual)
    for step in range(ITERS):
        lifted = -solve_interior(apply_full(direction), sines_x, sines_y, cosines, spectrum)
        image, lifted = (gamma * apply_full(direction + lifted), lifted)
        alpha = norm_now / curvature_total(direction, image)
        iterate = iterate + alpha * direction
        residual = residual - alpha * image
        if step + 1 < ITERS:
            norm_next = norm_total(residual)
            direction = residual + norm_next / norm_now * direction
            norm_now = norm_next
    correction = -solve_interior(apply_full(iterate), sines_x, sines_y, cosines, spectrum)
    potential = iterate + base + correction
    return (potential, residual)


DEPTH, WIDTH, HEIGHT = 32, 64, 128
F32, BF16 = jnp.float32, jnp.bfloat16


def halves(table):
    table = np.asarray(table, np.float64)
    high = table.astype(np.float32).astype(ml_dtypes.bfloat16)
    low = (table - high.astype(np.float64)).astype(np.float32).astype(ml_dtypes.bfloat16)
    return high, low


def sine_unit(count):
    index = np.arange(count)
    table = np.sqrt(2.0 / count) * np.sin(np.pi * np.outer(index, index) / count)
    table[0, 0] = 1.0
    return table


def host_tables():
    place, order = np.arange(DEPTH) + 0.5, np.arange(DEPTH)
    factor = np.where(order == 0, np.sqrt(1.0 / DEPTH), np.sqrt(2.0 / DEPTH))
    cosines = factor[None, :] * np.cos(np.pi * np.outer(place, order) / DEPTH)
    sin_x, sin_y = sine_unit(WIDTH), sine_unit(HEIGHT)
    vertical = 2.0 - 2.0 * np.cos(np.pi * order / DEPTH)
    across = 2.0 - 2.0 * np.cos(np.pi * np.arange(WIDTH) / WIDTH)
    along = 2.0 - 2.0 * np.cos(np.pi * np.arange(HEIGHT) / HEIGHT)
    ux = np.sqrt(2.0 / WIDTH) * np.sin(np.pi * np.arange(WIDTH) / WIDTH)
    uy = np.sqrt(2.0 / HEIGHT) * np.sin(np.pi * np.arange(HEIGHT) / HEIGHT)
    sx = np.where(np.arange(WIDTH) % 2 == 1, 1.0, -1.0)
    sy = np.where(np.arange(HEIGHT) % 2 == 1, 1.0, -1.0)
    sx[0] = sy[0] = 0.0
    ex, ey = np.eye(WIDTH)[0], np.eye(HEIGHT)[0]
    t = {}
    t["zf"] = np.concatenate(halves(np.kron(cosines.T, np.eye(8))))
    t["zi"] = np.concatenate(halves(np.kron(cosines, np.eye(8))))
    t["x"] = np.concatenate(halves(np.kron(np.eye(4), sin_x)))
    y_both = np.concatenate(halves(sin_y), 1)
    t["y"] = np.concatenate([y_both, y_both], 0)
    plane = SCREEN + across[:, None] + along[None, :]
    t["plane"] = plane.astype(np.float32)
    ur = np.concatenate([np.kron(np.eye(4), (ux + ex)[None]), np.kron(np.eye(4), (ux * sx)[None]), np.zeros((8, 4 * WIDTH))], 0)
    t["ur"] = np.concatenate(halves(ur))
    uc = np.zeros((16, HEIGHT))
    uc[0], uc[1], uc[2] = uy + ey, uy * sy, ey
    t["uc"] = np.concatenate(halves(uc))
    spec = plane[None] + vertical[:, None, None]
    inner = np.zeros((WIDTH, HEIGHT))
    inner[1:, 1:] = 1.0
    inv = inner / spec
    t["inv"] = np.where(inner > 0, inv, 1.0).astype(np.float32)
    row_near = np.einsum("a,kab->kb", ux * ux, inv)
    row_far = np.einsum("a,kab->kb", ux * ux * sx, inv)
    col_near = np.einsum("b,kab->ka", uy * uy, inv)
    col_far = np.einsum("b,kab->ka", uy * uy * sy, inv)
    row_coef = SCREEN + vertical[:, None] + 2.0 + along[None, :] - 2.0 * row_near
    col_coef = SCREEN + vertical[:, None] + 2.0 + across[None, :] - 2.0 * col_near
    row_coef[:, 0] = SCREEN + vertical + 4.0
    col_coef[:, 0] = 0.0
    own = np.zeros((DEPTH // 2, 8, HEIGHT))
    own[:, 0], own[:, 1] = row_coef[0::2], row_coef[1::2]
    own[:, 2], own[:, 3] = row_far[0::2], row_far[1::2]
    own[:, 4] = np.concatenate([col_coef[0::2], col_coef[1::2]], 1)
    own[:, 5] = np.concatenate([col_far[0::2], col_far[1::2]], 1)
    own[:, 6], own[:, 7] = vertical[0::2, None], vertical[1::2, None]
    t["own"] = own.astype(np.float32)
    border = np.zeros((WIDTH, HEIGHT))
    border[0], border[:, 0] = uy, ux
    t["pair"] = np.stack([np.outer(ux, uy), border]).astype(np.float32)
    signs = np.zeros((8, HEIGHT))
    signs[0] = sy
    signs[1] = np.concatenate([sx, sx])
    t["signs"] = signs.astype(np.float32)
    zero = np.zeros(WIDTH)
    left = np.zeros((8, HEIGHT))
    left[0], left[1] = np.concatenate([ux + ex, zero]), np.concatenate([zero, ux + ex])
    left[2], left[3] = np.concatenate([ux * sx, zero]), np.concatenate([zero, ux * sx])
    left[6], left[7] = np.concatenate([ex, zero]), np.concatenate([zero, ex])
    right = np.zeros((8, HEIGHT))
    right[4], right[5] = uy + ey, uy * sy
    t["left"], t["right"] = left.astype(np.float32), right.astype(np.float32)
    split = np.concatenate([np.arange(0, DEPTH, 2), np.arange(1, DEPTH, 2)])
    pair_x = np.concatenate(halves(np.kron(np.eye(2), sin_x)), 1)
    wide = np.zeros((DEPTH, 2 * HEIGHT))
    wide[:, :DEPTH] = cosines[split][:, split]
    t["square"] = np.concatenate([pair_x, pair_x] + list(halves(wide)), 0)
    return t


def halved(x):
    high = x.astype(BF16)
    return high, (x - high.astype(F32)).astype(BF16)


def dot(a, b, dims=((1,), (0,))):
    return lax.dot_general(a, b, (dims, ((), ())), preferred_element_type=F32)


def dot_table(table, b, dims=((1,), (0,))):
    count = table.shape[0] // 2
    both = dot(table, b[0], dims)
    return both[:count] + (both[count:] + dot(table[:count], b[1], dims))


def dot_packed(x, table):
    out = dot(jnp.concatenate(halved(x), 1), table)
    half = out.shape[1] // 2
    return out[:, :half] + out[:, half:]


def dot_exact(a, b, dims=((1,), (0,))):
    return lax.dot_general(
        a, b, (dims, ((), ())), precision=lax.Precision.HIGHEST, preferred_element_type=F32
    )


def lane_ids(shape):
    return lax.broadcasted_iota(jnp.int32, shape, len(shape) - 1)


def interior():
    row = lax.broadcasted_iota(jnp.int32, (WIDTH, HEIGHT), 0)
    return (row > 0) & (lane_ids((WIDTH, HEIGHT)) > 0)


def pair_lanes(parts):
    return jnp.concatenate(parts, 1)


def shift_x(n_gx, n_gy, field, by):
    cut = (by % n_gx) * n_gy
    return jnp.concatenate([field[cut:], field[:cut]], 0)


def shift_y(n_gx, n_gy, field, by):
    place = lax.broadcasted_iota(jnp.int32, field.shape, 0) % n_gy
    count = n_gx * n_gy
    ahead = by % count
    plain = jnp.concatenate([field[ahead:], field[:ahead]], 0)
    wrap = (by - n_gy if by > 0 else by + n_gy) % count
    wrapped = jnp.concatenate([field[wrap:], field[:wrap]], 0)
    edge = n_gy - 1 if by > 0 else 0
    return jnp.where(place == edge, wrapped, plain)


def turn_half(x):
    return jnp.concatenate([x[:, WIDTH:], x[:, :WIDTH]], 1)


def schur_modes(n_gx, n_gy, coef, table, row, col):
    row_coef, row_far, col_coef, col_far, row_sign, col_sign = coef
    sx = functools.partial(shift_x, n_gx, n_gy)
    sy = functools.partial(shift_y, n_gx, n_gy)
    count = n_gx * n_gy
    across = jnp.concatenate(halved(jnp.concatenate([col, col * col_sign], 0)), 1)
    across = dot(across, table[0]) + dot(across, table[1])
    along = dot(jnp.concatenate(halved(jnp.concatenate([row, row * row_sign], 0)), 0), table[2])
    along = along[:2 * count] + along[2 * count:]
    along = along[:, :HEIGHT] + along[:, HEIGHT:]
    v = across[:count] + sx(across[count:], -1)
    w = along[:count] + sy(along[count:], -1)
    row_out = row_coef * row - row_far * (sx(row, 1) + sx(row, -1)) - v - row_sign * sy(v, 1)
    col_out = col_coef * col - col_far * (sy(col, 1) + sy(col, -1)) - w - col_sign * sx(w, 1)
    lane = lane_ids((count, HEIGHT))
    row_out = row_out - jnp.concatenate(
        [jnp.where(lane == 0, w, 0.0), jnp.where(lane == 0, turn_half(w), 0.0)], 1
    )
    col_out = jnp.where(
        lane == 0, row_out[:, :HEIGHT], jnp.where(lane == WIDTH, turn_half(row_out[:, HEIGHT:]), col_out)
    )
    return row_out, col_out


def owner_tables(own, pair, turned, signs):
    inner = interior()
    blank = jnp.zeros((WIDTH, HEIGHT), F32)
    lane = lane_ids((HEIGHT, HEIGHT))
    inside = (lane % WIDTH > 0) & (lax.broadcasted_iota(jnp.int32, (HEIGHT, HEIGHT), 0) > 0)
    parts, other = [], []
    for s in range(2):
        vert = own[6 + s:7 + s]
        parts.append(jnp.where(inner, pair[0] / (pair[2] + vert), pair[1]))
        one = jnp.where(inside, turned[0] / (turned[2] + vert), turned[1])
        other.append(jnp.where((lane < WIDTH) == (s == 0), one, 0.0))
    high, low = halved(jnp.concatenate([pair_lanes([parts[0], blank]), pair_lanes([blank, parts[1]])], 0))
    table = (
        jnp.concatenate([high, high], 0),
        jnp.concatenate([low, low], 0),
        jnp.concatenate(halved(jnp.concatenate(other, 0)), 1),
    )
    coef = (
        pair_lanes([own[0:1], own[1:2]]),
        pair_lanes([own[2:3], own[3:4]]),
        own[4:5],
        own[5:6],
        pair_lanes([signs[0:1], signs[0:1]]),
        signs[1:2],
    )
    return coef, table


def start_modes(n_gx, n_gy, fields):
    sx = functools.partial(shift_x, n_gx, n_gy)
    sy = functools.partial(shift_y, n_gx, n_gy)
    row = pair_lanes([fields[0], fields[1]]) + sx(pair_lanes([fields[2], fields[3]]), -1)
    col = fields[4] + sy(fields[5], -1)
    return row, col


def inner_product(first, second):
    lane = lane_ids(first[1].shape)
    cols = jnp.where(lane % WIDTH == 0, 0.0, first[1] * second[1])
    rows = first[0] * second[0]
    down = jnp.sum(rows[:, :HEIGHT] + rows[:, HEIGHT:] + cols, 0, keepdims=True)
    return jnp.sum(down, 1, keepdims=True)


def face_fields(n_gx, n_gy, pair):
    row, col = pair
    beyond = shift_x(n_gx, n_gy, row, 1)
    return [
        row[:, :HEIGHT], row[:, HEIGHT:], beyond[:, :HEIGHT], beyond[:, HEIGHT:],
        col, shift_y(n_gx, n_gy, col, 1),
    ]


def steps(sums):
    rr, rw, ww, wv = sums
    alpha = rr / rw
    after = alpha * alpha * ww - rr
    beta = after / rr
    curve = (1 + beta) * (1 + beta) * rw - 2 * (1 + beta) * alpha * ww + alpha * alpha * wv
    second = after / curve
    return alpha + second * (1 + beta), -second * alpha


def slab_kernel(
    n_gx, n_gy,
    charge_hbm, surface_hbm, z_hbm, x_hbm, y_hbm, ur_hbm, uc_hbm, inv_hbm, own_hbm, pair_hbm, turned_hbm, signs_hbm,
    zi_hbm, small_hbm, square_hbm,
    potential_hbm, residual_hbm,
    charge, surface, z, x, y, ur, uc, inv, own_ref, pair_ref, turned_ref, signs_ref,
    zi, small, square,
    work, base, potential, residual, faces, msg, got, back, landed, load_sems, store_sems, sems,
):
    count = n_gx * n_gy
    gx, gy = lax.axis_index("gx"), lax.axis_index("gy")
    me = gx * n_gy + gy
    pairs = [(z_hbm, z), (surface_hbm, surface)]
    pairs += [(charge_hbm.at[:, pl.ds(16 * t, 16), :], charge.at[:, pl.ds(16 * t, 16), :]) for t in range(WIDTH // 16)]
    pairs += [(y_hbm, y), (x_hbm, x), (ur_hbm, ur), (uc_hbm, uc)]
    pairs += [(inv_hbm.at[pl.ds(8 * t, 8)], inv.at[pl.ds(8 * t, 8)]) for t in range(DEPTH // 8)]
    pairs += [(own_hbm, own_ref), (pair_hbm, pair_ref), (turned_hbm, turned_ref), (signs_hbm, signs_ref)]
    pairs += [(zi_hbm, zi), (small_hbm, small), (square_hbm, square)]
    copies = [pltpu.make_async_copy(s, d, load_sems.at[n]) for n, (s, d) in enumerate(pairs)]
    for copy in copies:
        copy.start()

    def partner(off):
        to_x, to_y = gx + off // n_gy, gy + off % n_gy
        to_x = jnp.where(to_x >= n_gx, to_x - n_gx, to_x)
        to_y = jnp.where(to_y >= n_gy, to_y - n_gy, to_y)
        return to_x * n_gy + to_y, {"gx": to_x, "gy": to_y}

    def send(source, target, which, off):
        to, device = partner(off)
        copy = pltpu.make_async_remote_copy(
            src_ref=source.at[to],
            dst_ref=target.at[me],
            send_sem=sems.at[which, 0],
            recv_sem=sems.at[which, 1],
            device_id=device,
            device_id_type=pl.DeviceIdType.MESH,
        )
        copy.start()

    def all_done(buffer, sem):
        whole = buffer.at[pl.ds(0, count - 1)]
        pltpu.make_async_copy(whole, whole, sem).wait()

    barrier = pltpu.get_barrier_semaphore()
    for off in range(1, count):
        pl.semaphore_signal(barrier, inc=1, device_id=partner(off)[1], device_id_type=pl.DeviceIdType.MESH)
    copies[0].wait()
    copies[1].wait()
    ztab = z[...]
    for t in range(WIDTH // 16):
        copies[2 + t].wait()
        sides = []
        for h in range(2):
            at = pl.ds(16 * t + 8 * h, 8)
            block = charge[:, at, :]
            block = jnp.concatenate(
                [block[:1] + surface[0:1, at, :], block[1:-1], block[-1:] + surface[1:2, at, :]], 0
            )
            sides.append(block.reshape(DEPTH * 8, HEIGHT))
        out = dot_table(ztab, halved(pair_lanes(sides)))
        if t == 0:
            copies[6].wait()
            ytab = y[...]
        for h in range(2):
            side = out[:, HEIGHT * h:HEIGHT * (h + 1)]
            side = dot_packed(side, ytab)
            work[:, 16 * t + 8 * h:16 * t + 8 * h + 8, :] = side.reshape(DEPTH, 8, HEIGHT)
    for copy in copies[7:10]:
        copy.wait()
    xtab, utab, ctab = x[...], ur[...], uc[...]
    inner = interior()
    lane = lane_ids((8, HEIGHT))
    pl.semaphore_wait(barrier, count - 1)
    for copy in copies[10:14]:
        copy.wait()
    for step in range(1, n_gx + 1):
        t = partner(n_gy * (step % n_gx))[1]["gx"]
        sides = [work[pl.ds(8 * t + 4 * h, 4)].reshape(4 * WIDTH, HEIGHT) for h in range(2)]
        out = dot_table(xtab, halved(pair_lanes(sides)))
        for h in range(2):
            side = out[:, HEIGHT * h:HEIGHT * (h + 1)].reshape(4, WIDTH, HEIGHT)
            full = []
            corner = []
            for s in range(4):
                k = 8 * t + 4 * h + s
                one = side[s] * inv[k]
                base[k] = jnp.where(inner, one, 0.0)
                full.append(one)
                corner.append(one[0:1])
            full = jnp.concatenate(full, 0)
            parts = halved(full)
            rows = dot_table(utab, parts)
            own = jnp.concatenate(corner + [jnp.zeros((4, HEIGHT), F32)], 0)
            rows = jnp.where(lane == 0, own, rows[:8])
            cols = dot_table(ctab, parts, ((1,), (1,)))
            edge = lane_ids((1, 4 * WIDTH)) % WIDTH == 0
            near = jnp.where(edge, cols[2:3], cols[0:1])
            far = jnp.where(edge, 0.0, cols[1:2])
            for g in range(2):
                at = slice(HEIGHT * g, HEIGHT * (g + 1))
                msg[4 * t + 2 * h + g] = jnp.concatenate(
                    [rows[2 * g:2 * g + 2], rows[4 + 2 * g:6 + 2 * g], near[:, at], far[:, at]],
                    0,
                )
        for ahead in range(1 if step == n_gx else 0, n_gy):
            send(msg, got, 0, n_gy * (step % n_gx) + ahead)
    for copy in copies[14:]:
        copy.wait()
    coef, table = owner_tables(own_ref[me], pair_ref[...], turned_ref[...], signs_ref[...])
    got[me] = msg[me]
    all_done(got, sems.at[0, 1])
    r = start_modes(n_gx, n_gy, [got[:, f, :] for f in range(6)])
    w = schur_modes(n_gx, n_gy, coef, table, *r)
    v = schur_modes(n_gx, n_gy, coef, table, *w)
    for f, field in enumerate(face_fields(n_gx, n_gy, r)):
        back[:, f, :] = field
    for f, field in enumerate(face_fields(n_gx, n_gy, w)):
        back[:, 8 + f, :] = field
    back[:, 6, :] = v[0][:, :HEIGHT]
    back[:, 7, :] = v[0][:, HEIGHT:]
    back[:, 14, :] = v[1]
    sums = (inner_product(r, r), inner_product(r, w), inner_product(w, w), inner_product(w, v))
    lanes = lane_ids((count, HEIGHT))
    back[:, 15, :] = sum(jnp.where(lanes == s, value, 0.0) for s, value in enumerate(sums))
    for off in range(1, count):
        send(back, landed, 1, off)
    landed[me] = back[me]
    all_done(msg, sems.at[0, 0])
    all_done(landed, sems.at[1, 1])
    faces[...] = combine(landed[...])
    stores = inverse(
        faces, base, x, y, zi, inv, small, square, potential_hbm, residual_hbm, potential, residual, work, store_sems
    )
    for copy in stores:
        copy.wait()
    all_done(back, sems.at[1, 0])


def combine(landed):
    near, far = landed[:, :8], landed[:, 8:]
    total = jnp.sum(far[:, 7:8, :], 0)
    lane = lane_ids((1, HEIGHT))
    c0, c1 = steps([jnp.sum(jnp.where(lane == s, total, 0.0), 1, keepdims=True) for s in range(4)])
    c0, c1 = c0[None], c1[None]
    lead = near - c0 * far
    rest = [lead[:, 0:2] - c1 * near[:, 6:8], lead[:, 4:5] - c1 * far[:, 6:7], jnp.zeros_like(near[:, :5])]
    return jnp.concatenate([c0 * near + c1 * far] + rest, 1)


def stacked(left, right):
    lh, ll = halved(left)
    rh, rl = halved(right)
    lhs = jnp.concatenate([lh.astype(F32), lh.astype(F32), ll.astype(F32)], 0).astype(BF16)
    rhs = jnp.concatenate([rh.astype(F32), rl.astype(F32), rh.astype(F32)], 0).astype(BF16)
    return dot(lhs, rhs, ((0,), (0,)))


def inverse(
    faces, base, x, y, z, inv, small, square, potential_hbm, residual_hbm, potential, residual, work, store_sems
):
    lane = lane_ids((8, HEIGHT))
    sub = lax.broadcasted_iota(jnp.int32, (8, HEIGHT), 0)
    const_left, const_right = small[0:8], small[8:16]
    xtab, ytab = x[...], y[...]
    half = DEPTH // 2
    rows = dot_packed(jnp.concatenate([faces[:, 8, :], faces[:, 9, :]], 0), ytab)
    cols = dot_packed(faces[:, 10, :], square[0:2 * HEIGHT])
    cols = jnp.concatenate([cols[:, :WIDTH], cols[:, WIDTH:]], 0)
    both = jnp.concatenate([rows, cols, jnp.zeros_like(cols)], 1)
    both = dot_table(square[2 * HEIGHT:, :DEPTH], halved(both))
    rows, cols = both[:, :HEIGHT], both[:, HEIGHT:HEIGHT + WIDTH]
    cols = jnp.concatenate([cols[:half], cols[half:]], 1)
    cols = jnp.where(lane_ids((half, HEIGHT)) % WIDTH == 0, 0.0, cols)
    unit = jnp.where(lane == 0, 1.0, 0.0)
    mark = jnp.where(((sub == 0) & (lane == 0)) | ((sub == 1) & (lane == WIDTH)), 1.0, 0.0)
    for o in range(half):
        lhs = jnp.where(sub == 2, cols[o:o + 1], mark)
        rhs = jnp.where(sub == 0, rows[o:o + 1], jnp.where(sub == 1, rows[half + o:half + o + 1], jnp.where(sub == 2, unit, 0.0)))
        out = stacked(lhs, rhs)
        residual[2 * o] = out[:WIDTH]
        residual[2 * o + 1] = out[WIDTH:]
    for t in range(DEPTH // 8):
        sides = []
        for h in range(2):
            blocks = []
            for g in range(2):
                o = 4 * t + 2 * h + g
                one = faces[o, :8]
                lhs = jnp.where((sub >= 4) & (sub < 6) & (lane % WIDTH > 0), one, const_left)
                up = jnp.concatenate([one[2:], one[:2]], 0)
                rhs = jnp.where((sub < 4) & (lane > 0), one, const_right)
                rhs = jnp.where((sub >= 6) & (lane == 0), up, rhs)
                out = stacked(lhs, rhs)
                for s in range(2):
                    k = 2 * o + s
                    blocks.append(out[WIDTH * s:WIDTH * (s + 1)] * inv[k] + base[k])
            sides.append(jnp.concatenate(blocks, 0))
        out = dot_table(xtab, halved(pair_lanes(sides)))
        for h in range(2):
            side = dot_packed(out[:, HEIGHT * h:HEIGHT * (h + 1)], ytab)
            work[8 * t + 4 * h:8 * t + 4 * h + 4] = side.reshape(4, WIDTH, HEIGHT)
        if t == 0:
            stores = [pltpu.make_async_copy(residual, residual_hbm, store_sems.at[WIDTH // 16])]
            stores[0].start()
    ztab = z[...]
    for t in range(WIDTH // 16):
        sides = [work[:, 16 * t + 8 * h:16 * t + 8 * h + 8, :].reshape(DEPTH * 8, HEIGHT) for h in range(2)]
        out = dot_table(ztab, halved(pair_lanes(sides)))
        for h in range(2):
            side = out[:, HEIGHT * h:HEIGHT * (h + 1)]
            potential[:, 16 * t + 8 * h:16 * t + 8 * h + 8, :] = side.reshape(DEPTH, 8, HEIGHT)
        at = pl.ds(16 * t, 16)
        stores.append(pltpu.make_async_copy(potential.at[:, at, :], potential_hbm.at[:, at, :], store_sems.at[t]))
        stores[-1].start()
    return stores


def on_device_modes(n_gx, n_gy, charge, surface_charge):
    t = host_tables()
    count = n_gx * n_gy
    block = jax.ShapeDtypeStruct(charge.shape, F32)
    hbm = pl.BlockSpec(memory_space=pl.ANY)

    def held(values):
        return [pltpu.VMEM(value.shape, value.dtype) for value in values]

    pair = np.concatenate([t["pair"], t["plane"][None]], 0)
    turned = np.concatenate([np.swapaxes(pair, 1, 2)] * 2, 2)
    args = [charge, surface_charge, t["zf"], t["x"], t["y"], t["ur"], t["uc"], t["inv"], t["own"], pair, turned, t["signs"]]
    six, sixteen = (count, 6, HEIGHT), (count, 16, HEIGHT)
    small = np.concatenate([t["left"], t["right"]], 0)
    args += [t["zi"], small, t["square"]]
    return pl.pallas_call(
        functools.partial(slab_kernel, n_gx, n_gy),
        out_shape=(block, block),
        in_specs=[hbm] * len(args),
        out_specs=(hbm, hbm),
        scratch_shapes=held(args)
        + [pltpu.VMEM(shape, F32) for shape in [charge.shape] * 4 + [sixteen, six, six, sixteen, sixteen]]
        + [
            pltpu.SemaphoreType.DMA((21,)),
            pltpu.SemaphoreType.DMA((WIDTH // 16 + 1,)),
            pltpu.SemaphoreType.DMA((2, 2)),
        ],
        compiler_params=pltpu.CompilerParams(collective_id=0, has_side_effects=True),
        name="slab",
    )(*args)


def solution(mesh):
    per_device = functools.partial(on_device_modes, mesh.shape["gx"], mesh.shape["gy"])
    if (mesh.shape["gx"], mesh.shape["gy"]) != (4, 4):
        per_device = on_device
    in_specs = (P(None, ("slab", "gx"), "gy"), P(None, ("slab", "gx"), "gy"))
    out_specs = (P(None, ("slab", "gx"), "gy"), P(None, ("slab", "gx"), "gy"))
    return jax.shard_map(
        per_device, mesh=mesh, in_specs=in_specs, out_specs=out_specs, check_vma=False
    )
```

```python
import functools

import jax
import jax.numpy as jnp
import ml_dtypes
import numpy as np
from jax import lax
from jax.experimental import pallas as pl
from jax.experimental.pallas import tpu as pltpu
from jax.sharding import PartitionSpec as P

ITERS = 2


SCREEN = 0.02


def padded(block, sides, width):
    for axis, dim in sides:
        count = lax.axis_size(axis)
        forward = [(i, i + 1) for i in range(count - 1)]
        forward.append((count - 1, 0))
        backward = [(target, source) for source, target in forward]
        low = lax.ppermute(
            lax.slice_in_dim(block, block.shape[dim] - width, None, axis=dim), axis, forward
        )
        high = lax.ppermute(lax.slice_in_dim(block, 0, width, axis=dim), axis, backward)
        block = jnp.concatenate([low, block, high], axis=dim)
    return block


def sine_full(count):
    index = jnp.arange(count).astype(jnp.float32)
    return jnp.sqrt(2.0 / count) * jnp.sin(jnp.pi * jnp.outer(index, index) / count)


def cosine_table(count):
    place = jnp.arange(count).astype(jnp.float32) + 0.5
    order = jnp.arange(count).astype(jnp.float32)
    factor = jnp.where(order == 0.0, jnp.sqrt(1.0 / count), jnp.sqrt(2.0 / count))
    return factor[None, :] * jnp.cos(jnp.pi * jnp.outer(place, order) / count)


def spectrum_table(depth, width, height):
    across = 2.0 - 2.0 * jnp.cos(jnp.pi * jnp.arange(width).astype(jnp.float32) / width)
    along = 2.0 - 2.0 * jnp.cos(jnp.pi * jnp.arange(height).astype(jnp.float32) / height)
    vertical = 2.0 - 2.0 * jnp.cos(jnp.pi * jnp.arange(depth).astype(jnp.float32) / depth)
    return SCREEN + vertical[:, None, None] + across[None, :, None] + along[None, None, :]


def apply_full(field):
    row_rims = jnp.stack([field[:, 0, :], field[:, -1, :]], 1)
    row_ext = padded(row_rims, (("gx", 1),), 1)
    col_rims = jnp.stack([field[:, :, 0], field[:, :, -1]], 0)
    col_ext = padded(col_rims, (("gy", 0),), 1)
    from_below_x = jnp.concatenate([row_ext[:, 0:1, :], field[:, :-1, :]], 1)
    from_above_x = jnp.concatenate([field[:, 1:, :], row_ext[:, 3:4, :]], 1)
    from_below_y = jnp.concatenate([col_ext[0][:, :, None], field[:, :, :-1]], 2)
    from_above_y = jnp.concatenate([field[:, :, 1:], col_ext[3][:, :, None]], 2)
    beside = from_below_x + from_above_x + from_below_y + from_above_y
    upper = jnp.concatenate([field[1:], field[-1:]], 0)
    lower = jnp.concatenate([field[:1], field[:-1]], 0)
    return (6.0 + SCREEN) * field - beside - upper - lower


def solve_interior(field, sines_x, sines_y, cosines, spectrum):
    high = lax.Precision.HIGHEST
    depth, width, height = field.shape
    hat = jnp.dot(field.reshape(depth * width, height), sines_y, precision=high).reshape(
        depth, width, height
    )
    hat = jnp.matmul(sines_x, hat, precision=high)
    hat = jnp.dot(cosines.T, hat.reshape(depth, width * height), precision=high).reshape(
        depth, width, height
    )
    hat = hat / spectrum
    back = jnp.dot(cosines, hat.reshape(depth, width * height), precision=high).reshape(
        depth, width, height
    )
    back = jnp.matmul(sines_x, back, precision=high)
    back = jnp.dot(back.reshape(depth * width, height), sines_y, precision=high)
    return back.reshape(depth, width, height)


def norm_total(residual):
    return lax.psum(jnp.sum(residual * residual), ("gx", "gy"))


def curvature_total(direction, image):
    return lax.psum(jnp.sum(direction * image), ("gx", "gy"))


def on_device(charge, surface_charge):
    depth, width, height = charge.shape
    sines_x = sine_full(width)
    sines_y = sine_full(height)
    cosines = cosine_table(depth)
    spectrum = spectrum_table(depth, width, height)
    row_place = lax.broadcasted_iota(jnp.int32, (1, width, height), 1)
    col_place = lax.broadcasted_iota(jnp.int32, (1, width, height), 2)
    gamma = jnp.where((row_place == 0) | (col_place == 0), 1.0, 0.0).astype(jnp.float32)
    source = charge.at[0].add(surface_charge[0]).at[-1].add(surface_charge[1])
    base = solve_interior(source, sines_x, sines_y, cosines, spectrum)
    reduced = gamma * (source - apply_full(base))
    iterate = jnp.zeros_like(reduced)
    residual = reduced
    direction = reduced
    norm_now = norm_total(residual)
    for step in range(ITERS):
        lifted = -solve_interior(apply_full(direction), sines_x, sines_y, cosines, spectrum)
        image, lifted = (gamma * apply_full(direction + lifted), lifted)
        alpha = norm_now / curvature_total(direction, image)
        iterate = iterate + alpha * direction
        residual = residual - alpha * image
        if step + 1 < ITERS:
            norm_next = norm_total(residual)
            direction = residual + norm_next / norm_now * direction
            norm_now = norm_next
    correction = -solve_interior(apply_full(iterate), sines_x, sines_y, cosines, spectrum)
    potential = iterate + base + correction
    return (potential, residual)


DEPTH, WIDTH, HEIGHT = 32, 64, 128
F32, BF16 = jnp.float32, jnp.bfloat16


def halves(table):
    table = np.asarray(table, np.float64)
    high = table.astype(np.float32).astype(ml_dtypes.bfloat16)
    low = (table - high.astype(np.float64)).astype(np.float32).astype(ml_dtypes.bfloat16)
    return high, low


def sine_unit(count):
    index = np.arange(count)
    table = np.sqrt(2.0 / count) * np.sin(np.pi * np.outer(index, index) / count)
    table[0, 0] = 1.0
    return table


def host_tables():
    place, order = np.arange(DEPTH) + 0.5, np.arange(DEPTH)
    factor = np.where(order == 0, np.sqrt(1.0 / DEPTH), np.sqrt(2.0 / DEPTH))
    cosines = factor[None, :] * np.cos(np.pi * np.outer(place, order) / DEPTH)
    sin_x, sin_y = sine_unit(WIDTH), sine_unit(HEIGHT)
    vertical = 2.0 - 2.0 * np.cos(np.pi * order / DEPTH)
    across = 2.0 - 2.0 * np.cos(np.pi * np.arange(WIDTH) / WIDTH)
    along = 2.0 - 2.0 * np.cos(np.pi * np.arange(HEIGHT) / HEIGHT)
    ux = np.sqrt(2.0 / WIDTH) * np.sin(np.pi * np.arange(WIDTH) / WIDTH)
    uy = np.sqrt(2.0 / HEIGHT) * np.sin(np.pi * np.arange(HEIGHT) / HEIGHT)
    sx = np.where(np.arange(WIDTH) % 2 == 1, 1.0, -1.0)
    sy = np.where(np.arange(HEIGHT) % 2 == 1, 1.0, -1.0)
    sx[0] = sy[0] = 0.0
    ex, ey = np.eye(WIDTH)[0], np.eye(HEIGHT)[0]
    t = {}
    t["zf"] = np.concatenate(halves(np.kron(cosines.T, np.eye(8))))
    t["zi"] = np.concatenate(halves(np.kron(cosines, np.eye(8))))
    t["x"] = np.concatenate(halves(np.kron(np.eye(4), sin_x)))
    y_both = np.concatenate(halves(sin_y), 1)
    t["y"] = np.concatenate([y_both, y_both], 0)
    plane = SCREEN + across[:, None] + along[None, :]
    t["plane"] = plane.astype(np.float32)
    ur = np.concatenate([np.kron(np.eye(4), (ux + ex)[None]), np.kron(np.eye(4), (ux * sx)[None]), np.zeros((8, 4 * WIDTH))], 0)
    t["ur"] = np.concatenate(halves(ur))
    uc = np.zeros((16, HEIGHT))
    uc[0], uc[1], uc[2] = uy + ey, uy * sy, ey
    t["uc"] = np.concatenate(halves(uc))
    spec = plane[None] + vertical[:, None, None]
    inner = np.zeros((WIDTH, HEIGHT))
    inner[1:, 1:] = 1.0
    inv = inner / spec
    t["inv"] = np.where(inner > 0, inv, 1.0).astype(np.float32)
    row_near = np.einsum("a,kab->kb", ux * ux, inv)
    row_far = np.einsum("a,kab->kb", ux * ux * sx, inv)
    col_near = np.einsum("b,kab->ka", uy * uy, inv)
    col_far = np.einsum("b,kab->ka", uy * uy * sy, inv)
    row_coef = SCREEN + vertical[:, None] + 2.0 + along[None, :] - 2.0 * row_near
    col_coef = SCREEN + vertical[:, None] + 2.0 + across[None, :] - 2.0 * col_near
    row_coef[:, 0] = SCREEN + vertical + 4.0
    col_coef[:, 0] = 0.0
    own = np.zeros((DEPTH // 2, 8, HEIGHT))
    own[:, 0], own[:, 1] = row_coef[0::2], row_coef[1::2]
    own[:, 2], own[:, 3] = row_far[0::2], row_far[1::2]
    own[:, 4] = np.concatenate([col_coef[0::2], col_coef[1::2]], 1)
    own[:, 5] = np.concatenate([col_far[0::2], col_far[1::2]], 1)
    own[:, 6], own[:, 7] = vertical[0::2, None], vertical[1::2, None]
    t["own"] = own.astype(np.float32)
    border = np.zeros((WIDTH, HEIGHT))
    border[0], border[:, 0] = uy, ux
    t["pair"] = np.stack([np.outer(ux, uy), border]).astype(np.float32)
    signs = np.zeros((8, HEIGHT))
    signs[0] = sy
    signs[1] = np.concatenate([sx, sx])
    t["signs"] = signs.astype(np.float32)
    zero = np.zeros(WIDTH)
    left = np.zeros((8, HEIGHT))
    left[0], left[1] = np.concatenate([ux + ex, zero]), np.concatenate([zero, ux + ex])
    left[2], left[3] = np.concatenate([ux * sx, zero]), np.concatenate([zero, ux * sx])
    left[6], left[7] = np.concatenate([ex, zero]), np.concatenate([zero, ex])
    right = np.zeros((8, HEIGHT))
    right[4], right[5] = uy + ey, uy * sy
    t["left"], t["right"] = left.astype(np.float32), right.astype(np.float32)
    split = np.concatenate([np.arange(0, DEPTH, 2), np.arange(1, DEPTH, 2)])
    pair_x = np.concatenate(halves(np.kron(np.eye(2), sin_x)), 1)
    wide = np.zeros((DEPTH, 2 * HEIGHT))
    wide[:, :DEPTH] = cosines[split][:, split]
    t["square"] = np.concatenate([pair_x, pair_x] + list(halves(wide)), 0)
    return t


def halved(x):
    high = x.astype(BF16)
    return high, (x - high.astype(F32)).astype(BF16)


def dot(a, b, dims=((1,), (0,))):
    return lax.dot_general(a, b, (dims, ((), ())), preferred_element_type=F32)


def dot_table(table, b, dims=((1,), (0,))):
    count = table.shape[0] // 2
    both = dot(table, b[0], dims)
    return both[:count] + (both[count:] + dot(table[:count], b[1], dims))


def dot_packed(x, table):
    out = dot(jnp.concatenate(halved(x), 1), table)
    half = out.shape[1] // 2
    return out[:, :half] + out[:, half:]


def dot_exact(a, b, dims=((1,), (0,))):
    return lax.dot_general(
        a, b, (dims, ((), ())), precision=lax.Precision.HIGHEST, preferred_element_type=F32
    )


def lane_ids(shape):
    return lax.broadcasted_iota(jnp.int32, shape, len(shape) - 1)


def interior():
    row = lax.broadcasted_iota(jnp.int32, (WIDTH, HEIGHT), 0)
    return (row > 0) & (lane_ids((WIDTH, HEIGHT)) > 0)


def pair_lanes(parts):
    return jnp.concatenate(parts, 1)


def shift_x(n_gx, n_gy, field, by):
    cut = (by % n_gx) * n_gy
    return jnp.concatenate([field[cut:], field[:cut]], 0)


def shift_y(n_gx, n_gy, field, by):
    place = lax.broadcasted_iota(jnp.int32, field.shape, 0) % n_gy
    count = n_gx * n_gy
    ahead = by % count
    plain = jnp.concatenate([field[ahead:], field[:ahead]], 0)
    wrap = (by - n_gy if by > 0 else by + n_gy) % count
    wrapped = jnp.concatenate([field[wrap:], field[:wrap]], 0)
    edge = n_gy - 1 if by > 0 else 0
    return jnp.where(place == edge, wrapped, plain)


def turn_half(x):
    return jnp.concatenate([x[:, WIDTH:], x[:, :WIDTH]], 1)


def schur_modes(n_gx, n_gy, coef, table, row, col):
    row_coef, row_far, col_coef, col_far, row_sign, col_sign = coef
    sx = functools.partial(shift_x, n_gx, n_gy)
    sy = functools.partial(shift_y, n_gx, n_gy)
    count = n_gx * n_gy
    across = jnp.concatenate(halved(jnp.concatenate([col, col * col_sign], 0)), 1)
    across = dot(across, table[0]) + dot(across, table[1])
    along = dot(jnp.concatenate(halved(jnp.concatenate([row, row * row_sign], 0)), 0), table[2])
    along = along[:2 * count] + along[2 * count:]
    along = along[:, :HEIGHT] + along[:, HEIGHT:]
    v = across[:count] + sx(across[count:], -1)
    w = along[:count] + sy(along[count:], -1)
    row_out = row_coef * row - row_far * (sx(row, 1) + sx(row, -1)) - v - row_sign * sy(v, 1)
    col_out = col_coef * col - col_far * (sy(col, 1) + sy(col, -1)) - w - col_sign * sx(w, 1)
    lane = lane_ids((count, HEIGHT))
    row_out = row_out - jnp.concatenate(
        [jnp.where(lane == 0, w, 0.0), jnp.where(lane == 0, turn_half(w), 0.0)], 1
    )
    col_out = jnp.where(
        lane == 0, row_out[:, :HEIGHT], jnp.where(lane == WIDTH, turn_half(row_out[:, HEIGHT:]), col_out)
    )
    return row_out, col_out


def owner_tables(own, pair, turned, signs):
    inner = interior()
    blank = jnp.zeros((WIDTH, HEIGHT), F32)
    lane = lane_ids((HEIGHT, HEIGHT))
    inside = (lane % WIDTH > 0) & (lax.broadcasted_iota(jnp.int32, (HEIGHT, HEIGHT), 0) > 0)
    parts, other = [], []
    for s in range(2):
        vert = own[6 + s:7 + s]
        parts.append(jnp.where(inner, pair[0] / (pair[2] + vert), pair[1]))
        one = jnp.where(inside, turned[0] / (turned[2] + vert), turned[1])
        other.append(jnp.where((lane < WIDTH) == (s == 0), one, 0.0))
    high, low = halved(jnp.concatenate([pair_lanes([parts[0], blank]), pair_lanes([blank, parts[1]])], 0))
    table = (
        jnp.concatenate([high, high], 0),
        jnp.concatenate([low, low], 0),
        jnp.concatenate(halved(jnp.concatenate(other, 0)), 1),
    )
    coef = (
        pair_lanes([own[0:1], own[1:2]]),
        pair_lanes([own[2:3], own[3:4]]),
        own[4:5],
        own[5:6],
        pair_lanes([signs[0:1], signs[0:1]]),
        signs[1:2],
    )
    return coef, table


def start_modes(n_gx, n_gy, fields):
    sx = functools.partial(shift_x, n_gx, n_gy)
    sy = functools.partial(shift_y, n_gx, n_gy)
    row = pair_lanes([fields[0], fields[1]]) + sx(pair_lanes([fields[2], fields[3]]), -1)
    col = fields[4] + sy(fields[5], -1)
    return row, col


def inner_product(first, second):
    lane = lane_ids(first[1].shape)
    cols = jnp.where(lane % WIDTH == 0, 0.0, first[1] * second[1])
    rows = first[0] * second[0]
    down = jnp.sum(rows[:, :HEIGHT] + rows[:, HEIGHT:] + cols, 0, keepdims=True)
    return jnp.sum(down, 1, keepdims=True)


def face_fields(n_gx, n_gy, pair):
    row, col = pair
    beyond = shift_x(n_gx, n_gy, row, 1)
    return [
        row[:, :HEIGHT], row[:, HEIGHT:], beyond[:, :HEIGHT], beyond[:, HEIGHT:],
        col, shift_y(n_gx, n_gy, col, 1),
    ]


def steps(sums):
    rr, rw, ww, wv = sums
    alpha = rr / rw
    after = alpha * alpha * ww - rr
    beta = after / rr
    curve = (1 + beta) * (1 + beta) * rw - 2 * (1 + beta) * alpha * ww + alpha * alpha * wv
    second = after / curve
    return alpha + second * (1 + beta), -second * alpha


def slab_kernel(
    n_gx, n_gy,
    charge_hbm, surface_hbm, z_hbm, x_hbm, y_hbm, ur_hbm, uc_hbm, inv_hbm, own_hbm, pair_hbm, turned_hbm, signs_hbm,
    zi_hbm, small_hbm, square_hbm,
    potential_hbm, edges_hbm,
    charge, surface, z, x, y, ur, uc, inv, own_ref, pair_ref, turned_ref, signs_ref,
    zi, small, square,
    work, base, potential, edges, faces, msg, got, back, landed, load_sems, store_sems, sems,
):
    count = n_gx * n_gy
    gx, gy = lax.axis_index("gx"), lax.axis_index("gy")
    me = gx * n_gy + gy
    pairs = [(z_hbm, z), (surface_hbm, surface)]
    pairs += [(charge_hbm.at[:, pl.ds(16 * t, 16), :], charge.at[:, pl.ds(16 * t, 16), :]) for t in range(WIDTH // 16)]
    pairs += [(y_hbm, y), (x_hbm, x), (ur_hbm, ur), (uc_hbm, uc)]
    pairs += [(inv_hbm.at[pl.ds(8 * t, 8)], inv.at[pl.ds(8 * t, 8)]) for t in range(DEPTH // 8)]
    pairs += [(own_hbm, own_ref), (pair_hbm, pair_ref), (turned_hbm, turned_ref), (signs_hbm, signs_ref)]
    pairs += [(zi_hbm, zi), (small_hbm, small), (square_hbm, square)]
    copies = [pltpu.make_async_copy(s, d, load_sems.at[n]) for n, (s, d) in enumerate(pairs)]
    for copy in copies:
        copy.start()

    def partner(off):
        to_x, to_y = gx + off // n_gy, gy + off % n_gy
        to_x = jnp.where(to_x >= n_gx, to_x - n_gx, to_x)
        to_y = jnp.where(to_y >= n_gy, to_y - n_gy, to_y)
        return to_x * n_gy + to_y, {"gx": to_x, "gy": to_y}

    def send(source, target, which, off):
        to, device = partner(off)
        copy = pltpu.make_async_remote_copy(
            src_ref=source.at[to],
            dst_ref=target.at[me],
            send_sem=sems.at[which, 0],
            recv_sem=sems.at[which, 1],
            device_id=device,
            device_id_type=pl.DeviceIdType.MESH,
        )
        copy.start()

    def all_done(buffer, sem):
        whole = buffer.at[pl.ds(0, count - 1)]
        pltpu.make_async_copy(whole, whole, sem).wait()

    barrier = pltpu.get_barrier_semaphore()
    for off in range(1, count):
        pl.semaphore_signal(barrier, inc=1, device_id=partner(off)[1], device_id_type=pl.DeviceIdType.MESH)
    copies[0].wait()
    copies[1].wait()
    ztab = z[...]
    for t in range(WIDTH // 16):
        copies[2 + t].wait()
        sides = []
        for h in range(2):
            at = pl.ds(16 * t + 8 * h, 8)
            block = charge[:, at, :]
            block = jnp.concatenate(
                [block[:1] + surface[0:1, at, :], block[1:-1], block[-1:] + surface[1:2, at, :]], 0
            )
            sides.append(block.reshape(DEPTH * 8, HEIGHT))
        out = dot_table(ztab, halved(pair_lanes(sides)))
        if t == 0:
            copies[6].wait()
            ytab = y[...]
        for h in range(2):
            side = out[:, HEIGHT * h:HEIGHT * (h + 1)]
            side = dot_packed(side, ytab)
            work[:, 16 * t + 8 * h:16 * t + 8 * h + 8, :] = side.reshape(DEPTH, 8, HEIGHT)
    for copy in copies[7:10]:
        copy.wait()
    xtab, utab, ctab = x[...], ur[...], uc[...]
    inner = interior()
    lane = lane_ids((8, HEIGHT))
    pl.semaphore_wait(barrier, count - 1)
    for copy in copies[10:14]:
        copy.wait()
    for step in range(1, n_gx + 1):
        t = partner(n_gy * (step % n_gx))[1]["gx"]
        sides = [work[pl.ds(8 * t + 4 * h, 4)].reshape(4 * WIDTH, HEIGHT) for h in range(2)]
        out = dot_table(xtab, halved(pair_lanes(sides)))
        for h in range(2):
            side = out[:, HEIGHT * h:HEIGHT * (h + 1)].reshape(4, WIDTH, HEIGHT)
            full = []
            corner = []
            for s in range(4):
                k = 8 * t + 4 * h + s
                one = side[s] * inv[k]
                base[k] = jnp.where(inner, one, 0.0)
                full.append(one)
                corner.append(one[0:1])
            full = jnp.concatenate(full, 0)
            parts = halved(full)
            rows = dot_table(utab, parts)
            own = jnp.concatenate(corner + [jnp.zeros((4, HEIGHT), F32)], 0)
            rows = jnp.where(lane == 0, own, rows[:8])
            cols = dot_table(ctab, parts, ((1,), (1,)))
            edge = lane_ids((1, 4 * WIDTH)) % WIDTH == 0
            near = jnp.where(edge, cols[2:3], cols[0:1])
            far = jnp.where(edge, 0.0, cols[1:2])
            for g in range(2):
                at = slice(HEIGHT * g, HEIGHT * (g + 1))
                msg[4 * t + 2 * h + g] = jnp.concatenate(
                    [rows[2 * g:2 * g + 2], rows[4 + 2 * g:6 + 2 * g], near[:, at], far[:, at]],
                    0,
                )
        for ahead in range(1 if step == n_gx else 0, n_gy):
            send(msg, got, 0, n_gy * (step % n_gx) + ahead)
    for copy in copies[14:]:
        copy.wait()
    coef, table = owner_tables(own_ref[me], pair_ref[...], turned_ref[...], signs_ref[...])
    got[me] = msg[me]
    all_done(got, sems.at[0, 1])
    r = start_modes(n_gx, n_gy, [got[:, f, :] for f in range(6)])
    w = schur_modes(n_gx, n_gy, coef, table, *r)
    v = schur_modes(n_gx, n_gy, coef, table, *w)
    for f, field in enumerate(face_fields(n_gx, n_gy, r)):
        back[:, f, :] = field
    for f, field in enumerate(face_fields(n_gx, n_gy, w)):
        back[:, 8 + f, :] = field
    back[:, 6, :] = v[0][:, :HEIGHT]
    back[:, 7, :] = v[0][:, HEIGHT:]
    back[:, 14, :] = v[1]
    sums = (inner_product(r, r), inner_product(r, w), inner_product(w, w), inner_product(w, v))
    lanes = lane_ids((count, HEIGHT))
    back[:, 15, :] = sum(jnp.where(lanes == s, value, 0.0) for s, value in enumerate(sums))
    for off in range(1, count):
        send(back, landed, 1, off)
    landed[me] = back[me]
    all_done(msg, sems.at[0, 0])
    all_done(landed, sems.at[1, 1])
    faces[...] = combine(landed[...])
    stores = inverse(
        faces, base, x, y, zi, inv, small, square, potential_hbm, edges_hbm, potential, edges, work, store_sems
    )
    for copy in stores:
        copy.wait()
    all_done(back, sems.at[1, 0])


def combine(landed):
    near, far = landed[:, :8], landed[:, 8:]
    total = jnp.sum(far[:, 7:8, :], 0)
    lane = lane_ids((1, HEIGHT))
    c0, c1 = steps([jnp.sum(jnp.where(lane == s, total, 0.0), 1, keepdims=True) for s in range(4)])
    c0, c1 = c0[None], c1[None]
    lead = near - c0 * far
    rest = [lead[:, 0:2] - c1 * near[:, 6:8], lead[:, 4:5] - c1 * far[:, 6:7], jnp.zeros_like(near[:, :5])]
    return jnp.concatenate([c0 * near + c1 * far] + rest, 1)


def stacked(left, right):
    lh, ll = halved(left)
    rh, rl = halved(right)
    lhs = jnp.concatenate([lh.astype(F32), lh.astype(F32), ll.astype(F32)], 0).astype(BF16)
    rhs = jnp.concatenate([rh.astype(F32), rl.astype(F32), rh.astype(F32)], 0).astype(BF16)
    return dot(lhs, rhs, ((0,), (0,)))


def inverse(
    faces, base, x, y, z, inv, small, square, potential_hbm, edges_hbm, potential, edges, work, store_sems
):
    lane = lane_ids((8, HEIGHT))
    sub = lax.broadcasted_iota(jnp.int32, (8, HEIGHT), 0)
    const_left, const_right = small[0:8], small[8:16]
    xtab, ytab = x[...], y[...]
    half = DEPTH // 2
    rows = dot_packed(jnp.concatenate([faces[:, 8, :], faces[:, 9, :]], 0), ytab)
    cols = dot_packed(faces[:, 10, :], square[0:2 * HEIGHT])
    cols = jnp.concatenate([cols[:, :WIDTH], cols[:, WIDTH:]], 0)
    both = jnp.concatenate([rows, cols, jnp.zeros_like(cols)], 1)
    both = dot_table(square[2 * HEIGHT:, :DEPTH], halved(both))
    rows, cols = both[:, :HEIGHT], both[:, HEIGHT:HEIGHT + WIDTH]
    cols = jnp.concatenate([cols[:half], cols[half:]], 1)
    cols = jnp.where(lane_ids((half, HEIGHT)) % WIDTH == 0, 0.0, cols)
    edges[0:DEPTH] = rows
    edges[DEPTH:] = cols
    for t in range(DEPTH // 8):
        sides = []
        for h in range(2):
            blocks = []
            for g in range(2):
                o = 4 * t + 2 * h + g
                one = faces[o, :8]
                lhs = jnp.where((sub >= 4) & (sub < 6) & (lane % WIDTH > 0), one, const_left)
                up = jnp.concatenate([one[2:], one[:2]], 0)
                rhs = jnp.where((sub < 4) & (lane > 0), one, const_right)
                rhs = jnp.where((sub >= 6) & (lane == 0), up, rhs)
                out = stacked(lhs, rhs)
                for s in range(2):
                    k = 2 * o + s
                    blocks.append(out[WIDTH * s:WIDTH * (s + 1)] * inv[k] + base[k])
            sides.append(jnp.concatenate(blocks, 0))
        out = dot_table(xtab, halved(pair_lanes(sides)))
        for h in range(2):
            side = dot_packed(out[:, HEIGHT * h:HEIGHT * (h + 1)], ytab)
            work[8 * t + 4 * h:8 * t + 4 * h + 4] = side.reshape(4, WIDTH, HEIGHT)
        if t == 0:
            stores = [pltpu.make_async_copy(edges, edges_hbm, store_sems.at[WIDTH // 16])]
            stores[0].start()
    ztab = z[...]
    for t in range(WIDTH // 16):
        sides = [work[:, 16 * t + 8 * h:16 * t + 8 * h + 8, :].reshape(DEPTH * 8, HEIGHT) for h in range(2)]
        out = dot_table(ztab, halved(pair_lanes(sides)))
        for h in range(2):
            side = out[:, HEIGHT * h:HEIGHT * (h + 1)]
            potential[:, 16 * t + 8 * h:16 * t + 8 * h + 8, :] = side.reshape(DEPTH, 8, HEIGHT)
        at = pl.ds(16 * t, 16)
        stores.append(pltpu.make_async_copy(potential.at[:, at, :], potential_hbm.at[:, at, :], store_sems.at[t]))
        stores[-1].start()
    return stores


def expand_kernel(
    source_hbm, edges_hbm, potential_hbm, residual_hbm, edges, residual, load_sems, store_sems
):
    parts = [pl.ds(8 * t, 8) for t in range(DEPTH // 8)]
    load = pltpu.make_async_copy(edges_hbm, edges, load_sems.at[0])
    load.start()
    copies = [
        pltpu.make_async_copy(source_hbm.at[part], potential_hbm.at[part], store_sems.at[n])
        for n, part in enumerate(parts)
    ]
    for copy in copies:
        copy.start()
    lane = lane_ids((8, HEIGHT))
    sub = lax.broadcasted_iota(jnp.int32, (8, HEIGHT), 0)
    half = DEPTH // 2
    load.wait()
    unit = jnp.where(lane == 0, 1.0, 0.0)
    mark = jnp.where(((sub == 0) & (lane == 0)) | ((sub == 1) & (lane == WIDTH)), 1.0, 0.0)
    for o in range(half):
        lhs = jnp.where(sub == 2, edges[DEPTH + o:DEPTH + o + 1], mark)
        rhs = jnp.where(sub == 0, edges[o:o + 1], jnp.where(sub == 1, edges[half + o:half + o + 1], jnp.where(sub == 2, unit, 0.0)))
        out = stacked(lhs, rhs)
        residual[2 * o] = out[:WIDTH]
        residual[2 * o + 1] = out[WIDTH:]
        if o % 4 == 3:
            part = parts[o // 4]
            copies.append(
                pltpu.make_async_copy(residual.at[part], residual_hbm.at[part], store_sems.at[len(copies)])
            )
            copies[-1].start()
    for copy in copies:
        copy.wait()


def on_device_modes(n_gx, n_gy, charge, surface_charge):
    t = host_tables()
    count = n_gx * n_gy
    block = jax.ShapeDtypeStruct(charge.shape, F32)
    hbm = pl.BlockSpec(memory_space=pl.ANY)

    def held(values):
        return [pltpu.VMEM(value.shape, value.dtype) for value in values]

    pair = np.concatenate([t["pair"], t["plane"][None]], 0)
    turned = np.concatenate([np.swapaxes(pair, 1, 2)] * 2, 2)
    args = [charge, surface_charge, t["zf"], t["x"], t["y"], t["ur"], t["uc"], t["inv"], t["own"], pair, turned, t["signs"]]
    six, sixteen = (count, 6, HEIGHT), (count, 16, HEIGHT)
    small = np.concatenate([t["left"], t["right"]], 0)
    args += [t["zi"], small, t["square"]]
    edges = jax.ShapeDtypeStruct((DEPTH + DEPTH // 2, HEIGHT), F32)
    potential, rims = pl.pallas_call(
        functools.partial(slab_kernel, n_gx, n_gy),
        out_shape=(block, edges),
        in_specs=[hbm] * len(args),
        out_specs=(hbm, hbm),
        scratch_shapes=held(args)
        + [pltpu.VMEM(shape, F32) for shape in [charge.shape] * 3 + [edges.shape, sixteen, six, six, sixteen, sixteen]]
        + [
            pltpu.SemaphoreType.DMA((21,)),
            pltpu.SemaphoreType.DMA((WIDTH // 16 + 1,)),
            pltpu.SemaphoreType.DMA((2, 2)),
        ],
        compiler_params=pltpu.CompilerParams(collective_id=0, has_side_effects=True),
        name="slab",
    )(*args)
    return pl.pallas_call(
        expand_kernel,
        out_shape=(block, block),
        in_specs=[hbm, hbm],
        out_specs=(hbm, hbm),
        scratch_shapes=[
            pltpu.VMEM(edges.shape, F32),
            pltpu.VMEM(charge.shape, F32),
            pltpu.SemaphoreType.DMA((1,)),
            pltpu.SemaphoreType.DMA((DEPTH // 4,)),
        ],
        name="expand",
    )(potential, rims)


def solution(mesh):
    per_device = functools.partial(on_device_modes, mesh.shape["gx"], mesh.shape["gy"])
    if (mesh.shape["gx"], mesh.shape["gy"]) != (4, 4):
        per_device = on_device
    in_specs = (P(None, ("slab", "gx"), "gy"), P(None, ("slab", "gx"), "gy"))
    out_specs = (P(None, ("slab", "gx"), "gy"), P(None, ("slab", "gx"), "gy"))
    return jax.shard_map(
        per_device, mesh=mesh, in_specs=in_specs, out_specs=out_specs, check_vma=False
    )
```

```python
import functools

import jax
import jax.numpy as jnp
import ml_dtypes
import numpy as np
from jax import lax
from jax.experimental import pallas as pl
from jax.experimental.pallas import tpu as pltpu
from jax.sharding import PartitionSpec as P

ITERS = 2


SCREEN = 0.02


def padded(block, sides, width):
    for axis, dim in sides:
        count = lax.axis_size(axis)
        forward = [(i, i + 1) for i in range(count - 1)]
        forward.append((count - 1, 0))
        backward = [(target, source) for source, target in forward]
        low = lax.ppermute(
            lax.slice_in_dim(block, block.shape[dim] - width, None, axis=dim), axis, forward
        )
        high = lax.ppermute(lax.slice_in_dim(block, 0, width, axis=dim), axis, backward)
        block = jnp.concatenate([low, block, high], axis=dim)
    return block


def sine_full(count):
    index = jnp.arange(count).astype(jnp.float32)
    return jnp.sqrt(2.0 / count) * jnp.sin(jnp.pi * jnp.outer(index, index) / count)


def cosine_table(count):
    place = jnp.arange(count).astype(jnp.float32) + 0.5
    order = jnp.arange(count).astype(jnp.float32)
    factor = jnp.where(order == 0.0, jnp.sqrt(1.0 / count), jnp.sqrt(2.0 / count))
    return factor[None, :] * jnp.cos(jnp.pi * jnp.outer(place, order) / count)


def spectrum_table(depth, width, height):
    across = 2.0 - 2.0 * jnp.cos(jnp.pi * jnp.arange(width).astype(jnp.float32) / width)
    along = 2.0 - 2.0 * jnp.cos(jnp.pi * jnp.arange(height).astype(jnp.float32) / height)
    vertical = 2.0 - 2.0 * jnp.cos(jnp.pi * jnp.arange(depth).astype(jnp.float32) / depth)
    return SCREEN + vertical[:, None, None] + across[None, :, None] + along[None, None, :]


def apply_full(field):
    row_rims = jnp.stack([field[:, 0, :], field[:, -1, :]], 1)
    row_ext = padded(row_rims, (("gx", 1),), 1)
    col_rims = jnp.stack([field[:, :, 0], field[:, :, -1]], 0)
    col_ext = padded(col_rims, (("gy", 0),), 1)
    from_below_x = jnp.concatenate([row_ext[:, 0:1, :], field[:, :-1, :]], 1)
    from_above_x = jnp.concatenate([field[:, 1:, :], row_ext[:, 3:4, :]], 1)
    from_below_y = jnp.concatenate([col_ext[0][:, :, None], field[:, :, :-1]], 2)
    from_above_y = jnp.concatenate([field[:, :, 1:], col_ext[3][:, :, None]], 2)
    beside = from_below_x + from_above_x + from_below_y + from_above_y
    upper = jnp.concatenate([field[1:], field[-1:]], 0)
    lower = jnp.concatenate([field[:1], field[:-1]], 0)
    return (6.0 + SCREEN) * field - beside - upper - lower


def solve_interior(field, sines_x, sines_y, cosines, spectrum):
    high = lax.Precision.HIGHEST
    depth, width, height = field.shape
    hat = jnp.dot(field.reshape(depth * width, height), sines_y, precision=high).reshape(
        depth, width, height
    )
    hat = jnp.matmul(sines_x, hat, precision=high)
    hat = jnp.dot(cosines.T, hat.reshape(depth, width * height), precision=high).reshape(
        depth, width, height
    )
    hat = hat / spectrum
    back = jnp.dot(cosines, hat.reshape(depth, width * height), precision=high).reshape(
        depth, width, height
    )
    back = jnp.matmul(sines_x, back, precision=high)
    back = jnp.dot(back.reshape(depth * width, height), sines_y, precision=high)
    return back.reshape(depth, width, height)


def norm_total(residual):
    return lax.psum(jnp.sum(residual * residual), ("gx", "gy"))


def curvature_total(direction, image):
    return lax.psum(jnp.sum(direction * image), ("gx", "gy"))


def on_device(charge, surface_charge):
    depth, width, height = charge.shape
    sines_x = sine_full(width)
    sines_y = sine_full(height)
    cosines = cosine_table(depth)
    spectrum = spectrum_table(depth, width, height)
    row_place = lax.broadcasted_iota(jnp.int32, (1, width, height), 1)
    col_place = lax.broadcasted_iota(jnp.int32, (1, width, height), 2)
    gamma = jnp.where((row_place == 0) | (col_place == 0), 1.0, 0.0).astype(jnp.float32)
    source = charge.at[0].add(surface_charge[0]).at[-1].add(surface_charge[1])
    base = solve_interior(source, sines_x, sines_y, cosines, spectrum)
    reduced = gamma * (source - apply_full(base))
    iterate = jnp.zeros_like(reduced)
    residual = reduced
    direction = reduced
    norm_now = norm_total(residual)
    for step in range(ITERS):
        lifted = -solve_interior(apply_full(direction), sines_x, sines_y, cosines, spectrum)
        image, lifted = (gamma * apply_full(direction + lifted), lifted)
        alpha = norm_now / curvature_total(direction, image)
        iterate = iterate + alpha * direction
        residual = residual - alpha * image
        if step + 1 < ITERS:
            norm_next = norm_total(residual)
            direction = residual + norm_next / norm_now * direction
            norm_now = norm_next
    correction = -solve_interior(apply_full(iterate), sines_x, sines_y, cosines, spectrum)
    potential = iterate + base + correction
    return (potential, residual)


DEPTH, WIDTH, HEIGHT = 32, 64, 128
F32, BF16 = jnp.float32, jnp.bfloat16


def halves(table):
    table = np.asarray(table, np.float64)
    high = table.astype(np.float32).astype(ml_dtypes.bfloat16)
    low = (table - high.astype(np.float64)).astype(np.float32).astype(ml_dtypes.bfloat16)
    return high, low


def sine_unit(count):
    index = np.arange(count)
    table = np.sqrt(2.0 / count) * np.sin(np.pi * np.outer(index, index) / count)
    table[0, 0] = 1.0
    return table


def host_tables():
    place, order = np.arange(DEPTH) + 0.5, np.arange(DEPTH)
    factor = np.where(order == 0, np.sqrt(1.0 / DEPTH), np.sqrt(2.0 / DEPTH))
    cosines = factor[None, :] * np.cos(np.pi * np.outer(place, order) / DEPTH)
    sin_x, sin_y = sine_unit(WIDTH), sine_unit(HEIGHT)
    vertical = 2.0 - 2.0 * np.cos(np.pi * order / DEPTH)
    across = 2.0 - 2.0 * np.cos(np.pi * np.arange(WIDTH) / WIDTH)
    along = 2.0 - 2.0 * np.cos(np.pi * np.arange(HEIGHT) / HEIGHT)
    ux = np.sqrt(2.0 / WIDTH) * np.sin(np.pi * np.arange(WIDTH) / WIDTH)
    uy = np.sqrt(2.0 / HEIGHT) * np.sin(np.pi * np.arange(HEIGHT) / HEIGHT)
    sx = np.where(np.arange(WIDTH) % 2 == 1, 1.0, -1.0)
    sy = np.where(np.arange(HEIGHT) % 2 == 1, 1.0, -1.0)
    sx[0] = sy[0] = 0.0
    ex, ey = np.eye(WIDTH)[0], np.eye(HEIGHT)[0]
    t = {}
    t["zf"] = np.concatenate(halves(np.kron(cosines.T, np.eye(8))))
    t["zi"] = np.concatenate(halves(np.kron(cosines, np.eye(8))))
    t["x"] = np.concatenate(halves(np.kron(np.eye(4), sin_x)))
    y_both = np.concatenate(halves(sin_y), 1)
    t["y"] = np.concatenate([y_both, y_both], 0)
    plane = SCREEN + across[:, None] + along[None, :]
    t["plane"] = plane.astype(np.float32)
    ur = np.concatenate([np.kron(np.eye(4), (ux + ex)[None]), np.kron(np.eye(4), (ux * sx)[None]), np.zeros((8, 4 * WIDTH))], 0)
    t["ur"] = np.concatenate(halves(ur))
    uc = np.zeros((16, HEIGHT))
    uc[0], uc[1], uc[2] = uy + ey, uy * sy, ey
    t["uc"] = np.concatenate(halves(uc))
    spec = plane[None] + vertical[:, None, None]
    inner = np.zeros((WIDTH, HEIGHT))
    inner[1:, 1:] = 1.0
    inv = inner / spec
    t["inv"] = np.where(inner > 0, inv, 1.0).astype(np.float32)
    row_near = np.einsum("a,kab->kb", ux * ux, inv)
    row_far = np.einsum("a,kab->kb", ux * ux * sx, inv)
    col_near = np.einsum("b,kab->ka", uy * uy, inv)
    col_far = np.einsum("b,kab->ka", uy * uy * sy, inv)
    row_coef = SCREEN + vertical[:, None] + 2.0 + along[None, :] - 2.0 * row_near
    col_coef = SCREEN + vertical[:, None] + 2.0 + across[None, :] - 2.0 * col_near
    row_coef[:, 0] = SCREEN + vertical + 4.0
    col_coef[:, 0] = 0.0
    own = np.zeros((DEPTH // 2, 8, HEIGHT))
    own[:, 0], own[:, 1] = row_coef[0::2], row_coef[1::2]
    own[:, 2], own[:, 3] = row_far[0::2], row_far[1::2]
    own[:, 4] = np.concatenate([col_coef[0::2], col_coef[1::2]], 1)
    own[:, 5] = np.concatenate([col_far[0::2], col_far[1::2]], 1)
    own[:, 6], own[:, 7] = vertical[0::2, None], vertical[1::2, None]
    t["own"] = own.astype(np.float32)
    border = np.zeros((WIDTH, HEIGHT))
    border[0], border[:, 0] = uy, ux
    t["pair"] = np.stack([np.outer(ux, uy), border]).astype(np.float32)
    signs = np.zeros((8, HEIGHT))
    signs[0] = sy
    signs[1] = np.concatenate([sx, sx])
    t["signs"] = signs.astype(np.float32)
    zero = np.zeros(WIDTH)
    left = np.zeros((8, HEIGHT))
    left[0], left[1] = np.concatenate([ux + ex, zero]), np.concatenate([zero, ux + ex])
    left[2], left[3] = np.concatenate([ux * sx, zero]), np.concatenate([zero, ux * sx])
    left[6], left[7] = np.concatenate([ex, zero]), np.concatenate([zero, ex])
    right = np.zeros((8, HEIGHT))
    right[4], right[5] = uy + ey, uy * sy
    t["left"], t["right"] = left.astype(np.float32), right.astype(np.float32)
    split = np.concatenate([np.arange(0, DEPTH, 2), np.arange(1, DEPTH, 2)])
    pair_x = np.concatenate(halves(np.kron(np.eye(2), sin_x)), 1)
    wide = np.zeros((DEPTH, 2 * HEIGHT))
    wide[:, :DEPTH] = cosines[split][:, split]
    t["square"] = np.concatenate([pair_x, pair_x] + list(halves(wide)), 0)
    return t


def halved(x):
    high = x.astype(BF16)
    return high, (x - high.astype(F32)).astype(BF16)


def dot(a, b, dims=((1,), (0,))):
    return lax.dot_general(a, b, (dims, ((), ())), preferred_element_type=F32)


def dot_table(table, b, dims=((1,), (0,))):
    count = table.shape[0] // 2
    both = dot(table, b[0], dims)
    return both[:count] + (both[count:] + dot(table[:count], b[1], dims))


def dot_packed(x, table):
    out = dot(jnp.concatenate(halved(x), 1), table)
    half = out.shape[1] // 2
    return out[:, :half] + out[:, half:]


def dot_exact(a, b, dims=((1,), (0,))):
    return lax.dot_general(
        a, b, (dims, ((), ())), precision=lax.Precision.HIGHEST, preferred_element_type=F32
    )


def lane_ids(shape):
    return lax.broadcasted_iota(jnp.int32, shape, len(shape) - 1)


def interior():
    row = lax.broadcasted_iota(jnp.int32, (WIDTH, HEIGHT), 0)
    return (row > 0) & (lane_ids((WIDTH, HEIGHT)) > 0)


def pair_lanes(parts):
    return jnp.concatenate(parts, 1)


def shift_x(n_gx, n_gy, field, by):
    cut = (by % n_gx) * n_gy
    return jnp.concatenate([field[cut:], field[:cut]], 0)


def shift_y(n_gx, n_gy, field, by):
    place = lax.broadcasted_iota(jnp.int32, field.shape, 0) % n_gy
    count = n_gx * n_gy
    ahead = by % count
    plain = jnp.concatenate([field[ahead:], field[:ahead]], 0)
    wrap = (by - n_gy if by > 0 else by + n_gy) % count
    wrapped = jnp.concatenate([field[wrap:], field[:wrap]], 0)
    edge = n_gy - 1 if by > 0 else 0
    return jnp.where(place == edge, wrapped, plain)


def turn_half(x):
    return jnp.concatenate([x[:, WIDTH:], x[:, :WIDTH]], 1)


def schur_modes(n_gx, n_gy, coef, table, row, col):
    row_coef, row_far, col_coef, col_far, row_sign, col_sign = coef
    sx = functools.partial(shift_x, n_gx, n_gy)
    sy = functools.partial(shift_y, n_gx, n_gy)
    count = n_gx * n_gy
    across = jnp.concatenate(halved(jnp.concatenate([col, col * col_sign], 0)), 1)
    across = dot(across, table[0]) + dot(across, table[1])
    along = dot(jnp.concatenate(halved(jnp.concatenate([row, row * row_sign], 0)), 0), table[2])
    along = along[:2 * count] + along[2 * count:]
    along = along[:, :HEIGHT] + along[:, HEIGHT:]
    v = across[:count] + sx(across[count:], -1)
    w = along[:count] + sy(along[count:], -1)
    row_out = row_coef * row - row_far * (sx(row, 1) + sx(row, -1)) - v - row_sign * sy(v, 1)
    col_out = col_coef * col - col_far * (sy(col, 1) + sy(col, -1)) - w - col_sign * sx(w, 1)
    lane = lane_ids((count, HEIGHT))
    row_out = row_out - jnp.concatenate(
        [jnp.where(lane == 0, w, 0.0), jnp.where(lane == 0, turn_half(w), 0.0)], 1
    )
    col_out = jnp.where(
        lane == 0, row_out[:, :HEIGHT], jnp.where(lane == WIDTH, turn_half(row_out[:, HEIGHT:]), col_out)
    )
    return row_out, col_out


def owner_tables(own, pair, turned, signs):
    inner = interior()
    blank = jnp.zeros((WIDTH, HEIGHT), F32)
    lane = lane_ids((HEIGHT, HEIGHT))
    inside = (lane % WIDTH > 0) & (lax.broadcasted_iota(jnp.int32, (HEIGHT, HEIGHT), 0) > 0)
    parts, other = [], []
    for s in range(2):
        vert = own[6 + s:7 + s]
        parts.append(jnp.where(inner, pair[0] / (pair[2] + vert), pair[1]))
        one = jnp.where(inside, turned[0] / (turned[2] + vert), turned[1])
        other.append(jnp.where((lane < WIDTH) == (s == 0), one, 0.0))
    high, low = halved(jnp.concatenate([pair_lanes([parts[0], blank]), pair_lanes([blank, parts[1]])], 0))
    table = (
        jnp.concatenate([high, high], 0),
        jnp.concatenate([low, low], 0),
        jnp.concatenate(halved(jnp.concatenate(other, 0)), 1),
    )
    coef = (
        pair_lanes([own[0:1], own[1:2]]),
        pair_lanes([own[2:3], own[3:4]]),
        own[4:5],
        own[5:6],
        pair_lanes([signs[0:1], signs[0:1]]),
        signs[1:2],
    )
    return coef, table


def start_modes(n_gx, n_gy, fields):
    sx = functools.partial(shift_x, n_gx, n_gy)
    sy = functools.partial(shift_y, n_gx, n_gy)
    row = pair_lanes([fields[0], fields[1]]) + sx(pair_lanes([fields[2], fields[3]]), -1)
    col = fields[4] + sy(fields[5], -1)
    return row, col


def inner_product(first, second):
    lane = lane_ids(first[1].shape)
    cols = jnp.where(lane % WIDTH == 0, 0.0, first[1] * second[1])
    rows = first[0] * second[0]
    down = jnp.sum(rows[:, :HEIGHT] + rows[:, HEIGHT:] + cols, 0, keepdims=True)
    return jnp.sum(down, 1, keepdims=True)


def face_fields(n_gx, n_gy, pair):
    row, col = pair
    beyond = shift_x(n_gx, n_gy, row, 1)
    return [
        row[:, :HEIGHT], row[:, HEIGHT:], beyond[:, :HEIGHT], beyond[:, HEIGHT:],
        col, shift_y(n_gx, n_gy, col, 1),
    ]


def steps(sums):
    rr, rw, ww, wv = sums
    alpha = rr / rw
    after = alpha * alpha * ww - rr
    beta = after / rr
    curve = (1 + beta) * (1 + beta) * rw - 2 * (1 + beta) * alpha * ww + alpha * alpha * wv
    second = after / curve
    return alpha + second * (1 + beta), -second * alpha


def slab_kernel(
    n_gx, n_gy,
    charge_hbm, surface_hbm, z_hbm, x_hbm, y_hbm, ur_hbm, uc_hbm, inv_hbm, own_hbm, pair_hbm, turned_hbm, signs_hbm,
    small_hbm, square_hbm,
    work_hbm, edges_hbm,
    charge, surface, z, x, y, ur, uc, inv, own_ref, pair_ref, turned_ref, signs_ref,
    small, square,
    work, base, edges, faces, msg, got, back, landed, load_sems, store_sems, sems,
):
    count = n_gx * n_gy
    gx, gy = lax.axis_index("gx"), lax.axis_index("gy")
    me = gx * n_gy + gy
    pairs = [(z_hbm, z), (surface_hbm, surface)]
    pairs += [(charge_hbm.at[:, pl.ds(16 * t, 16), :], charge.at[:, pl.ds(16 * t, 16), :]) for t in range(WIDTH // 16)]
    pairs += [(y_hbm, y), (x_hbm, x), (ur_hbm, ur), (uc_hbm, uc)]
    pairs += [(inv_hbm.at[pl.ds(8 * t, 8)], inv.at[pl.ds(8 * t, 8)]) for t in range(DEPTH // 8)]
    pairs += [(own_hbm, own_ref), (pair_hbm, pair_ref), (turned_hbm, turned_ref), (signs_hbm, signs_ref)]
    pairs += [(small_hbm, small), (square_hbm, square)]
    copies = [pltpu.make_async_copy(s, d, load_sems.at[n]) for n, (s, d) in enumerate(pairs)]
    for copy in copies:
        copy.start()

    def partner(off):
        to_x, to_y = gx + off // n_gy, gy + off % n_gy
        to_x = jnp.where(to_x >= n_gx, to_x - n_gx, to_x)
        to_y = jnp.where(to_y >= n_gy, to_y - n_gy, to_y)
        return to_x * n_gy + to_y, {"gx": to_x, "gy": to_y}

    def send(source, target, which, off):
        to, device = partner(off)
        copy = pltpu.make_async_remote_copy(
            src_ref=source.at[to],
            dst_ref=target.at[me],
            send_sem=sems.at[which, 0],
            recv_sem=sems.at[which, 1],
            device_id=device,
            device_id_type=pl.DeviceIdType.MESH,
        )
        copy.start()

    def all_done(buffer, sem):
        whole = buffer.at[pl.ds(0, count - 1)]
        pltpu.make_async_copy(whole, whole, sem).wait()

    barrier = pltpu.get_barrier_semaphore()
    for off in range(1, count):
        pl.semaphore_signal(barrier, inc=1, device_id=partner(off)[1], device_id_type=pl.DeviceIdType.MESH)
    copies[0].wait()
    copies[1].wait()
    ztab = z[...]
    for t in range(WIDTH // 16):
        copies[2 + t].wait()
        sides = []
        for h in range(2):
            at = pl.ds(16 * t + 8 * h, 8)
            block = charge[:, at, :]
            block = jnp.concatenate(
                [block[:1] + surface[0:1, at, :], block[1:-1], block[-1:] + surface[1:2, at, :]], 0
            )
            sides.append(block.reshape(DEPTH * 8, HEIGHT))
        out = dot_table(ztab, halved(pair_lanes(sides)))
        if t == 0:
            copies[6].wait()
            ytab = y[...]
        for h in range(2):
            side = out[:, HEIGHT * h:HEIGHT * (h + 1)]
            side = dot_packed(side, ytab)
            work[:, 16 * t + 8 * h:16 * t + 8 * h + 8, :] = side.reshape(DEPTH, 8, HEIGHT)
    for copy in copies[7:10]:
        copy.wait()
    xtab, utab, ctab = x[...], ur[...], uc[...]
    inner = interior()
    lane = lane_ids((8, HEIGHT))
    pl.semaphore_wait(barrier, count - 1)
    for copy in copies[10:14]:
        copy.wait()
    for step in range(1, n_gx + 1):
        t = partner(n_gy * (step % n_gx))[1]["gx"]
        sides = [work[pl.ds(8 * t + 4 * h, 4)].reshape(4 * WIDTH, HEIGHT) for h in range(2)]
        out = dot_table(xtab, halved(pair_lanes(sides)))
        for h in range(2):
            side = out[:, HEIGHT * h:HEIGHT * (h + 1)].reshape(4, WIDTH, HEIGHT)
            full = []
            corner = []
            for s in range(4):
                k = 8 * t + 4 * h + s
                one = side[s] * inv[k]
                base[k] = jnp.where(inner, one, 0.0)
                full.append(one)
                corner.append(one[0:1])
            full = jnp.concatenate(full, 0)
            parts = halved(full)
            rows = dot_table(utab, parts)
            own = jnp.concatenate(corner + [jnp.zeros((4, HEIGHT), F32)], 0)
            rows = jnp.where(lane == 0, own, rows[:8])
            cols = dot_table(ctab, parts, ((1,), (1,)))
            edge = lane_ids((1, 4 * WIDTH)) % WIDTH == 0
            near = jnp.where(edge, cols[2:3], cols[0:1])
            far = jnp.where(edge, 0.0, cols[1:2])
            for g in range(2):
                at = slice(HEIGHT * g, HEIGHT * (g + 1))
                msg[4 * t + 2 * h + g] = jnp.concatenate(
                    [rows[2 * g:2 * g + 2], rows[4 + 2 * g:6 + 2 * g], near[:, at], far[:, at]],
                    0,
                )
        for ahead in range(1 if step == n_gx else 0, n_gy):
            send(msg, got, 0, n_gy * (step % n_gx) + ahead)
    for copy in copies[14:]:
        copy.wait()
    coef, table = owner_tables(own_ref[me], pair_ref[...], turned_ref[...], signs_ref[...])
    got[me] = msg[me]
    all_done(got, sems.at[0, 1])
    r = start_modes(n_gx, n_gy, [got[:, f, :] for f in range(6)])
    w = schur_modes(n_gx, n_gy, coef, table, *r)
    v = schur_modes(n_gx, n_gy, coef, table, *w)
    for f, field in enumerate(face_fields(n_gx, n_gy, r)):
        back[:, f, :] = field
    for f, field in enumerate(face_fields(n_gx, n_gy, w)):
        back[:, 8 + f, :] = field
    back[:, 6, :] = v[0][:, :HEIGHT]
    back[:, 7, :] = v[0][:, HEIGHT:]
    back[:, 14, :] = v[1]
    sums = (inner_product(r, r), inner_product(r, w), inner_product(w, w), inner_product(w, v))
    lanes = lane_ids((count, HEIGHT))
    back[:, 15, :] = sum(jnp.where(lanes == s, value, 0.0) for s, value in enumerate(sums))
    for off in range(1, count):
        send(back, landed, 1, off)
    landed[me] = back[me]
    all_done(msg, sems.at[0, 0])
    all_done(landed, sems.at[1, 1])
    faces[...] = combine(landed[...])
    stores = inverse(
        faces, base, x, y, inv, small, square, work_hbm, edges_hbm, edges, work, store_sems
    )
    for copy in stores:
        copy.wait()
    all_done(back, sems.at[1, 0])


def combine(landed):
    near, far = landed[:, :8], landed[:, 8:]
    total = jnp.sum(far[:, 7:8, :], 0)
    lane = lane_ids((1, HEIGHT))
    c0, c1 = steps([jnp.sum(jnp.where(lane == s, total, 0.0), 1, keepdims=True) for s in range(4)])
    c0, c1 = c0[None], c1[None]
    lead = near - c0 * far
    rest = [lead[:, 0:2] - c1 * near[:, 6:8], lead[:, 4:5] - c1 * far[:, 6:7], jnp.zeros_like(near[:, :5])]
    return jnp.concatenate([c0 * near + c1 * far] + rest, 1)


def stacked(left, right):
    lh, ll = halved(left)
    rh, rl = halved(right)
    lhs = jnp.concatenate([lh.astype(F32), lh.astype(F32), ll.astype(F32)], 0).astype(BF16)
    rhs = jnp.concatenate([rh.astype(F32), rl.astype(F32), rh.astype(F32)], 0).astype(BF16)
    return dot(lhs, rhs, ((0,), (0,)))


def inverse(
    faces, base, x, y, inv, small, square, work_hbm, edges_hbm, edges, work, store_sems
):
    lane = lane_ids((8, HEIGHT))
    sub = lax.broadcasted_iota(jnp.int32, (8, HEIGHT), 0)
    const_left, const_right = small[0:8], small[8:16]
    xtab, ytab = x[...], y[...]
    half = DEPTH // 2
    rows = dot_packed(jnp.concatenate([faces[:, 8, :], faces[:, 9, :]], 0), ytab)
    cols = dot_packed(faces[:, 10, :], square[0:2 * HEIGHT])
    cols = jnp.concatenate([cols[:, :WIDTH], cols[:, WIDTH:]], 0)
    both = jnp.concatenate([rows, cols, jnp.zeros_like(cols)], 1)
    both = dot_table(square[2 * HEIGHT:, :DEPTH], halved(both))
    rows, cols = both[:, :HEIGHT], both[:, HEIGHT:HEIGHT + WIDTH]
    cols = jnp.concatenate([cols[:half], cols[half:]], 1)
    cols = jnp.where(lane_ids((half, HEIGHT)) % WIDTH == 0, 0.0, cols)
    edges[0:DEPTH] = rows
    edges[DEPTH:] = cols
    for t in range(DEPTH // 8):
        sides = []
        for h in range(2):
            blocks = []
            for g in range(2):
                o = 4 * t + 2 * h + g
                one = faces[o, :8]
                lhs = jnp.where((sub >= 4) & (sub < 6) & (lane % WIDTH > 0), one, const_left)
                up = jnp.concatenate([one[2:], one[:2]], 0)
                rhs = jnp.where((sub < 4) & (lane > 0), one, const_right)
                rhs = jnp.where((sub >= 6) & (lane == 0), up, rhs)
                out = stacked(lhs, rhs)
                for s in range(2):
                    k = 2 * o + s
                    blocks.append(out[WIDTH * s:WIDTH * (s + 1)] * inv[k] + base[k])
            sides.append(jnp.concatenate(blocks, 0))
        out = dot_table(xtab, halved(pair_lanes(sides)))
        for h in range(2):
            side = dot_packed(out[:, HEIGHT * h:HEIGHT * (h + 1)], ytab)
            work[8 * t + 4 * h:8 * t + 4 * h + 4] = side.reshape(4, WIDTH, HEIGHT)
        if t == 0:
            stores = [pltpu.make_async_copy(edges, edges_hbm, store_sems.at[DEPTH // 8])]
            stores[0].start()
        part = pl.ds(8 * t, 8)
        stores.append(pltpu.make_async_copy(work.at[part], work_hbm.at[part], store_sems.at[t]))
        stores[-1].start()
    return stores


def finish_kernel(
    edges_hbm, z_hbm, work_hbm, potential_hbm, residual_hbm,
    edges, z, work, potential, residual, load_sems, store_sems,
):
    pairs = [(edges_hbm, edges), (z_hbm, z)]
    columns = [pl.ds(16 * t, 16) for t in range(WIDTH // 16)]
    pairs += [(work_hbm.at[:, at, :], work.at[:, at, :]) for at in columns]
    loads = [pltpu.make_async_copy(s, d, load_sems.at[n]) for n, (s, d) in enumerate(pairs)]
    for load in loads:
        load.start()
    copies = []
    lane = lane_ids((8, HEIGHT))
    sub = lax.broadcasted_iota(jnp.int32, (8, HEIGHT), 0)
    half = DEPTH // 2
    loads[0].wait()
    unit = jnp.where(lane == 0, 1.0, 0.0)
    mark = jnp.where(((sub == 0) & (lane == 0)) | ((sub == 1) & (lane == WIDTH)), 1.0, 0.0)
    for o in range(half):
        lhs = jnp.where(sub == 2, edges[DEPTH + o:DEPTH + o + 1], mark)
        rhs = jnp.where(sub == 0, edges[o:o + 1], jnp.where(sub == 1, edges[half + o:half + o + 1], jnp.where(sub == 2, unit, 0.0)))
        out = stacked(lhs, rhs)
        residual[2 * o] = out[:WIDTH]
        residual[2 * o + 1] = out[WIDTH:]
        if o % 4 == 3:
            part = pl.ds(2 * (o - 3), 8)
            copies.append(
                pltpu.make_async_copy(residual.at[part], residual_hbm.at[part], store_sems.at[len(copies)])
            )
            copies[-1].start()
    loads[1].wait()
    ztab = z[...]
    for t, at in enumerate(columns):
        loads[2 + t].wait()
        sides = [work[:, 16 * t + 8 * h:16 * t + 8 * h + 8, :].reshape(DEPTH * 8, HEIGHT) for h in range(2)]
        out = dot_table(ztab, halved(pair_lanes(sides)))
        for h in range(2):
            side = out[:, HEIGHT * h:HEIGHT * (h + 1)]
            potential[:, 16 * t + 8 * h:16 * t + 8 * h + 8, :] = side.reshape(DEPTH, 8, HEIGHT)
        copies.append(
            pltpu.make_async_copy(potential.at[:, at, :], potential_hbm.at[:, at, :], store_sems.at[len(copies)])
        )
        copies[-1].start()
    for copy in copies:
        copy.wait()


def on_device_modes(n_gx, n_gy, charge, surface_charge):
    t = host_tables()
    count = n_gx * n_gy
    block = jax.ShapeDtypeStruct(charge.shape, F32)
    hbm = pl.BlockSpec(memory_space=pl.ANY)

    def held(values):
        return [pltpu.VMEM(value.shape, value.dtype) for value in values]

    pair = np.concatenate([t["pair"], t["plane"][None]], 0)
    turned = np.concatenate([np.swapaxes(pair, 1, 2)] * 2, 2)
    args = [charge, surface_charge, t["zf"], t["x"], t["y"], t["ur"], t["uc"], t["inv"], t["own"], pair, turned, t["signs"]]
    six, sixteen = (count, 6, HEIGHT), (count, 16, HEIGHT)
    small = np.concatenate([t["left"], t["right"]], 0)
    args += [small, t["square"]]
    edges = jax.ShapeDtypeStruct((DEPTH + DEPTH // 2, HEIGHT), F32)
    field, rims = pl.pallas_call(
        functools.partial(slab_kernel, n_gx, n_gy),
        out_shape=(block, edges),
        in_specs=[hbm] * len(args),
        out_specs=(hbm, hbm),
        scratch_shapes=held(args)
        + [pltpu.VMEM(shape, F32) for shape in [charge.shape] * 2 + [edges.shape, sixteen, six, six, sixteen, sixteen]]
        + [
            pltpu.SemaphoreType.DMA((20,)),
            pltpu.SemaphoreType.DMA((DEPTH // 8 + 1,)),
            pltpu.SemaphoreType.DMA((2, 2)),
        ],
        compiler_params=pltpu.CompilerParams(collective_id=0, has_side_effects=True),
        name="slab",
    )(*args)
    args = [rims, t["zi"], field]
    return pl.pallas_call(
        finish_kernel,
        out_shape=(block, block),
        in_specs=[hbm] * len(args),
        out_specs=(hbm, hbm),
        scratch_shapes=held(args)
        + [pltpu.VMEM(charge.shape, F32)] * 2
        + [pltpu.SemaphoreType.DMA((2 + WIDTH // 16,)), pltpu.SemaphoreType.DMA((DEPTH // 8 + WIDTH // 16,))],
        name="finish",
    )(*args)


def solution(mesh):
    per_device = functools.partial(on_device_modes, mesh.shape["gx"], mesh.shape["gy"])
    if (mesh.shape["gx"], mesh.shape["gy"]) != (4, 4):
        per_device = on_device
    in_specs = (P(None, ("slab", "gx"), "gy"), P(None, ("slab", "gx"), "gy"))
    out_specs = (P(None, ("slab", "gx"), "gy"), P(None, ("slab", "gx"), "gy"))
    return jax.shard_map(
        per_device, mesh=mesh, in_specs=in_specs, out_specs=out_specs, check_vma=False
    )
```

```python
import functools

import jax
import jax.numpy as jnp
import ml_dtypes
import numpy as np
from jax import lax
from jax.experimental import pallas as pl
from jax.experimental.pallas import tpu as pltpu
from jax.sharding import PartitionSpec as P

ITERS = 2


SCREEN = 0.02


def padded(block, sides, width):
    for axis, dim in sides:
        count = lax.axis_size(axis)
        forward = [(i, i + 1) for i in range(count - 1)]
        forward.append((count - 1, 0))
        backward = [(target, source) for source, target in forward]
        low = lax.ppermute(
            lax.slice_in_dim(block, block.shape[dim] - width, None, axis=dim), axis, forward
        )
        high = lax.ppermute(lax.slice_in_dim(block, 0, width, axis=dim), axis, backward)
        block = jnp.concatenate([low, block, high], axis=dim)
    return block


def sine_full(count):
    index = jnp.arange(count).astype(jnp.float32)
    return jnp.sqrt(2.0 / count) * jnp.sin(jnp.pi * jnp.outer(index, index) / count)


def cosine_table(count):
    place = jnp.arange(count).astype(jnp.float32) + 0.5
    order = jnp.arange(count).astype(jnp.float32)
    factor = jnp.where(order == 0.0, jnp.sqrt(1.0 / count), jnp.sqrt(2.0 / count))
    return factor[None, :] * jnp.cos(jnp.pi * jnp.outer(place, order) / count)


def spectrum_table(depth, width, height):
    across = 2.0 - 2.0 * jnp.cos(jnp.pi * jnp.arange(width).astype(jnp.float32) / width)
    along = 2.0 - 2.0 * jnp.cos(jnp.pi * jnp.arange(height).astype(jnp.float32) / height)
    vertical = 2.0 - 2.0 * jnp.cos(jnp.pi * jnp.arange(depth).astype(jnp.float32) / depth)
    return SCREEN + vertical[:, None, None] + across[None, :, None] + along[None, None, :]


def apply_full(field):
    row_rims = jnp.stack([field[:, 0, :], field[:, -1, :]], 1)
    row_ext = padded(row_rims, (("gx", 1),), 1)
    col_rims = jnp.stack([field[:, :, 0], field[:, :, -1]], 0)
    col_ext = padded(col_rims, (("gy", 0),), 1)
    from_below_x = jnp.concatenate([row_ext[:, 0:1, :], field[:, :-1, :]], 1)
    from_above_x = jnp.concatenate([field[:, 1:, :], row_ext[:, 3:4, :]], 1)
    from_below_y = jnp.concatenate([col_ext[0][:, :, None], field[:, :, :-1]], 2)
    from_above_y = jnp.concatenate([field[:, :, 1:], col_ext[3][:, :, None]], 2)
    beside = from_below_x + from_above_x + from_below_y + from_above_y
    upper = jnp.concatenate([field[1:], field[-1:]], 0)
    lower = jnp.concatenate([field[:1], field[:-1]], 0)
    return (6.0 + SCREEN) * field - beside - upper - lower


def solve_interior(field, sines_x, sines_y, cosines, spectrum):
    high = lax.Precision.HIGHEST
    depth, width, height = field.shape
    hat = jnp.dot(field.reshape(depth * width, height), sines_y, precision=high).reshape(
        depth, width, height
    )
    hat = jnp.matmul(sines_x, hat, precision=high)
    hat = jnp.dot(cosines.T, hat.reshape(depth, width * height), precision=high).reshape(
        depth, width, height
    )
    hat = hat / spectrum
    back = jnp.dot(cosines, hat.reshape(depth, width * height), precision=high).reshape(
        depth, width, height
    )
    back = jnp.matmul(sines_x, back, precision=high)
    back = jnp.dot(back.reshape(depth * width, height), sines_y, precision=high)
    return back.reshape(depth, width, height)


def norm_total(residual):
    return lax.psum(jnp.sum(residual * residual), ("gx", "gy"))


def curvature_total(direction, image):
    return lax.psum(jnp.sum(direction * image), ("gx", "gy"))


def on_device(charge, surface_charge):
    depth, width, height = charge.shape
    sines_x = sine_full(width)
    sines_y = sine_full(height)
    cosines = cosine_table(depth)
    spectrum = spectrum_table(depth, width, height)
    row_place = lax.broadcasted_iota(jnp.int32, (1, width, height), 1)
    col_place = lax.broadcasted_iota(jnp.int32, (1, width, height), 2)
    gamma = jnp.where((row_place == 0) | (col_place == 0), 1.0, 0.0).astype(jnp.float32)
    source = charge.at[0].add(surface_charge[0]).at[-1].add(surface_charge[1])
    base = solve_interior(source, sines_x, sines_y, cosines, spectrum)
    reduced = gamma * (source - apply_full(base))
    iterate = jnp.zeros_like(reduced)
    residual = reduced
    direction = reduced
    norm_now = norm_total(residual)
    for step in range(ITERS):
        lifted = -solve_interior(apply_full(direction), sines_x, sines_y, cosines, spectrum)
        image, lifted = (gamma * apply_full(direction + lifted), lifted)
        alpha = norm_now / curvature_total(direction, image)
        iterate = iterate + alpha * direction
        residual = residual - alpha * image
        if step + 1 < ITERS:
            norm_next = norm_total(residual)
            direction = residual + norm_next / norm_now * direction
            norm_now = norm_next
    correction = -solve_interior(apply_full(iterate), sines_x, sines_y, cosines, spectrum)
    potential = iterate + base + correction
    return (potential, residual)


DEPTH, WIDTH, HEIGHT = 32, 64, 128
F32, BF16 = jnp.float32, jnp.bfloat16


def halves(table):
    table = np.asarray(table, np.float64)
    high = table.astype(np.float32).astype(ml_dtypes.bfloat16)
    low = (table - high.astype(np.float64)).astype(np.float32).astype(ml_dtypes.bfloat16)
    return high, low


def sine_unit(count):
    index = np.arange(count)
    table = np.sqrt(2.0 / count) * np.sin(np.pi * np.outer(index, index) / count)
    table[0, 0] = 1.0
    return table


def host_tables():
    place, order = np.arange(DEPTH) + 0.5, np.arange(DEPTH)
    factor = np.where(order == 0, np.sqrt(1.0 / DEPTH), np.sqrt(2.0 / DEPTH))
    cosines = factor[None, :] * np.cos(np.pi * np.outer(place, order) / DEPTH)
    sin_x, sin_y = sine_unit(WIDTH), sine_unit(HEIGHT)
    vertical = 2.0 - 2.0 * np.cos(np.pi * order / DEPTH)
    across = 2.0 - 2.0 * np.cos(np.pi * np.arange(WIDTH) / WIDTH)
    along = 2.0 - 2.0 * np.cos(np.pi * np.arange(HEIGHT) / HEIGHT)
    ux = np.sqrt(2.0 / WIDTH) * np.sin(np.pi * np.arange(WIDTH) / WIDTH)
    uy = np.sqrt(2.0 / HEIGHT) * np.sin(np.pi * np.arange(HEIGHT) / HEIGHT)
    sx = np.where(np.arange(WIDTH) % 2 == 1, 1.0, -1.0)
    sy = np.where(np.arange(HEIGHT) % 2 == 1, 1.0, -1.0)
    sx[0] = sy[0] = 0.0
    ex, ey = np.eye(WIDTH)[0], np.eye(HEIGHT)[0]
    t = {}
    t["zf"] = np.concatenate(halves(np.kron(cosines.T, np.eye(8))))
    t["zi"] = np.concatenate(halves(np.kron(cosines, np.eye(8))))
    t["x"] = np.concatenate(halves(np.kron(np.eye(4), sin_x)))
    y_both = np.concatenate(halves(sin_y), 1)
    t["y"] = np.concatenate([y_both, y_both], 0)
    plane = SCREEN + across[:, None] + along[None, :]
    t["plane"] = plane.astype(np.float32)
    ur = np.concatenate([np.kron(np.eye(4), (ux + ex)[None]), np.kron(np.eye(4), (ux * sx)[None]), np.zeros((8, 4 * WIDTH))], 0)
    t["ur"] = np.concatenate(halves(ur))
    uc = np.zeros((16, HEIGHT))
    uc[0], uc[1], uc[2] = uy + ey, uy * sy, ey
    t["uc"] = np.concatenate(halves(uc))
    spec = plane[None] + vertical[:, None, None]
    inner = np.zeros((WIDTH, HEIGHT))
    inner[1:, 1:] = 1.0
    inv = inner / spec
    t["inv"] = np.where(inner > 0, inv, 1.0).astype(np.float32)
    row_near = np.einsum("a,kab->kb", ux * ux, inv)
    row_far = np.einsum("a,kab->kb", ux * ux * sx, inv)
    col_near = np.einsum("b,kab->ka", uy * uy, inv)
    col_far = np.einsum("b,kab->ka", uy * uy * sy, inv)
    row_coef = SCREEN + vertical[:, None] + 2.0 + along[None, :] - 2.0 * row_near
    col_coef = SCREEN + vertical[:, None] + 2.0 + across[None, :] - 2.0 * col_near
    row_coef[:, 0] = SCREEN + vertical + 4.0
    col_coef[:, 0] = 0.0
    own = np.zeros((DEPTH // 2, 8, HEIGHT))
    own[:, 0], own[:, 1] = row_coef[0::2], row_coef[1::2]
    own[:, 2], own[:, 3] = row_far[0::2], row_far[1::2]
    own[:, 4] = np.concatenate([col_coef[0::2], col_coef[1::2]], 1)
    own[:, 5] = np.concatenate([col_far[0::2], col_far[1::2]], 1)
    own[:, 6], own[:, 7] = vertical[0::2, None], vertical[1::2, None]
    t["own"] = own.astype(np.float32)
    border = np.zeros((WIDTH, HEIGHT))
    border[0], border[:, 0] = uy, ux
    t["pair"] = np.stack([np.outer(ux, uy), border]).astype(np.float32)
    signs = np.zeros((8, HEIGHT))
    signs[0] = sy
    signs[1] = np.concatenate([sx, sx])
    t["signs"] = signs.astype(np.float32)
    zero = np.zeros(WIDTH)
    left = np.zeros((8, HEIGHT))
    left[0], left[1] = np.concatenate([ux + ex, zero]), np.concatenate([zero, ux + ex])
    left[2], left[3] = np.concatenate([ux * sx, zero]), np.concatenate([zero, ux * sx])
    left[6], left[7] = np.concatenate([ex, zero]), np.concatenate([zero, ex])
    right = np.zeros((8, HEIGHT))
    right[4], right[5] = uy + ey, uy * sy
    t["left"], t["right"] = left.astype(np.float32), right.astype(np.float32)
    split = np.concatenate([np.arange(0, DEPTH, 2), np.arange(1, DEPTH, 2)])
    pair_x = np.concatenate(halves(np.kron(np.eye(2), sin_x)), 1)
    wide = np.zeros((DEPTH, 2 * HEIGHT))
    wide[:, :DEPTH] = cosines[split][:, split]
    t["square"] = np.concatenate([pair_x, pair_x] + list(halves(wide)), 0)
    return t


def halved(x):
    high = x.astype(BF16)
    return high, (x - high.astype(F32)).astype(BF16)


def dot(a, b, dims=((1,), (0,))):
    return lax.dot_general(a, b, (dims, ((), ())), preferred_element_type=F32)


def dot_table(table, b, dims=((1,), (0,))):
    count = table.shape[0] // 2
    both = dot(table, b[0], dims)
    return both[:count] + (both[count:] + dot(table[:count], b[1], dims))


def dot_packed(x, table):
    out = dot(jnp.concatenate(halved(x), 1), table)
    half = out.shape[1] // 2
    return out[:, :half] + out[:, half:]


def dot_exact(a, b, dims=((1,), (0,))):
    return lax.dot_general(
        a, b, (dims, ((), ())), precision=lax.Precision.HIGHEST, preferred_element_type=F32
    )


def lane_ids(shape):
    return lax.broadcasted_iota(jnp.int32, shape, len(shape) - 1)


def interior():
    row = lax.broadcasted_iota(jnp.int32, (WIDTH, HEIGHT), 0)
    return (row > 0) & (lane_ids((WIDTH, HEIGHT)) > 0)


def pair_lanes(parts):
    return jnp.concatenate(parts, 1)


def shift_x(n_gx, n_gy, field, by):
    cut = (by % n_gx) * n_gy
    return jnp.concatenate([field[cut:], field[:cut]], 0)


def shift_y(n_gx, n_gy, field, by):
    place = lax.broadcasted_iota(jnp.int32, field.shape, 0) % n_gy
    count = n_gx * n_gy
    ahead = by % count
    plain = jnp.concatenate([field[ahead:], field[:ahead]], 0)
    wrap = (by - n_gy if by > 0 else by + n_gy) % count
    wrapped = jnp.concatenate([field[wrap:], field[:wrap]], 0)
    edge = n_gy - 1 if by > 0 else 0
    return jnp.where(place == edge, wrapped, plain)


def turn_half(x):
    return jnp.concatenate([x[:, WIDTH:], x[:, :WIDTH]], 1)


def schur_modes(n_gx, n_gy, coef, table, row, col):
    row_coef, row_far, col_coef, col_far, row_sign, col_sign = coef
    sx = functools.partial(shift_x, n_gx, n_gy)
    sy = functools.partial(shift_y, n_gx, n_gy)
    count = n_gx * n_gy
    across = jnp.concatenate(halved(jnp.concatenate([col, col * col_sign], 0)), 1)
    across = dot(across, table[0]) + dot(across, table[1])
    along = dot(jnp.concatenate(halved(jnp.concatenate([row, row * row_sign], 0)), 0), table[2])
    along = along[:2 * count] + along[2 * count:]
    along = along[:, :HEIGHT] + along[:, HEIGHT:]
    v = across[:count] + sx(across[count:], -1)
    w = along[:count] + sy(along[count:], -1)
    row_out = row_coef * row - row_far * (sx(row, 1) + sx(row, -1)) - v - row_sign * sy(v, 1)
    col_out = col_coef * col - col_far * (sy(col, 1) + sy(col, -1)) - w - col_sign * sx(w, 1)
    lane = lane_ids((count, HEIGHT))
    row_out = row_out - jnp.concatenate(
        [jnp.where(lane == 0, w, 0.0), jnp.where(lane == 0, turn_half(w), 0.0)], 1
    )
    col_out = jnp.where(
        lane == 0, row_out[:, :HEIGHT], jnp.where(lane == WIDTH, turn_half(row_out[:, HEIGHT:]), col_out)
    )
    return row_out, col_out


def owner_tables(own, pair, turned, signs):
    inner = interior()
    blank = jnp.zeros((WIDTH, HEIGHT), F32)
    lane = lane_ids((HEIGHT, HEIGHT))
    inside = (lane % WIDTH > 0) & (lax.broadcasted_iota(jnp.int32, (HEIGHT, HEIGHT), 0) > 0)
    parts, other = [], []
    for s in range(2):
        vert = own[6 + s:7 + s]
        parts.append(jnp.where(inner, pair[0] / (pair[2] + vert), pair[1]))
        one = jnp.where(inside, turned[0] / (turned[2] + vert), turned[1])
        other.append(jnp.where((lane < WIDTH) == (s == 0), one, 0.0))
    high, low = halved(jnp.concatenate([pair_lanes([parts[0], blank]), pair_lanes([blank, parts[1]])], 0))
    table = (
        jnp.concatenate([high, high], 0),
        jnp.concatenate([low, low], 0),
        jnp.concatenate(halved(jnp.concatenate(other, 0)), 1),
    )
    coef = (
        pair_lanes([own[0:1], own[1:2]]),
        pair_lanes([own[2:3], own[3:4]]),
        own[4:5],
        own[5:6],
        pair_lanes([signs[0:1], signs[0:1]]),
        signs[1:2],
    )
    return coef, table


def start_modes(n_gx, n_gy, fields):
    sx = functools.partial(shift_x, n_gx, n_gy)
    sy = functools.partial(shift_y, n_gx, n_gy)
    row = pair_lanes([fields[0], fields[1]]) + sx(pair_lanes([fields[2], fields[3]]), -1)
    col = fields[4] + sy(fields[5], -1)
    return row, col


def inner_product(first, second):
    lane = lane_ids(first[1].shape)
    cols = jnp.where(lane % WIDTH == 0, 0.0, first[1] * second[1])
    rows = first[0] * second[0]
    down = jnp.sum(rows[:, :HEIGHT] + rows[:, HEIGHT:] + cols, 0, keepdims=True)
    return jnp.sum(down, 1, keepdims=True)


def face_fields(n_gx, n_gy, pair):
    row, col = pair
    beyond = shift_x(n_gx, n_gy, row, 1)
    return [
        row[:, :HEIGHT], row[:, HEIGHT:], beyond[:, :HEIGHT], beyond[:, HEIGHT:],
        col, shift_y(n_gx, n_gy, col, 1),
    ]


def steps(sums):
    rr, rw, ww, wv = sums
    alpha = rr / rw
    after = alpha * alpha * ww - rr
    beta = after / rr
    curve = (1 + beta) * (1 + beta) * rw - 2 * (1 + beta) * alpha * ww + alpha * alpha * wv
    second = after / curve
    return alpha + second * (1 + beta), -second * alpha


def slab_kernel(
    n_gx, n_gy,
    charge_hbm, surface_hbm, z_hbm, x_hbm, y_hbm, ur_hbm, uc_hbm, inv_hbm, own_hbm, pair_hbm, turned_hbm, signs_hbm,
    small_hbm, square_hbm,
    work_hbm, edges_hbm,
    charge, surface, z, x, y, ur, uc, inv, own_ref, pair_ref, turned_ref, signs_ref,
    small, square,
    work, base, edges, faces, msg, got, back, landed, load_sems, store_sems, sems,
):
    count = n_gx * n_gy
    gx, gy = lax.axis_index("gx"), lax.axis_index("gy")
    me = gx * n_gy + gy
    pairs = [(z_hbm, z), (surface_hbm, surface)]
    pairs += [(charge_hbm.at[:, pl.ds(16 * t, 16), :], charge.at[:, pl.ds(16 * t, 16), :]) for t in range(WIDTH // 16)]
    pairs += [(y_hbm, y), (x_hbm, x), (ur_hbm, ur), (uc_hbm, uc)]
    pairs += [(inv_hbm.at[pl.ds(8 * t, 8)], inv.at[pl.ds(8 * t, 8)]) for t in range(DEPTH // 8)]
    pairs += [(own_hbm, own_ref), (pair_hbm, pair_ref), (turned_hbm, turned_ref), (signs_hbm, signs_ref)]
    pairs += [(small_hbm, small), (square_hbm, square)]
    copies = [pltpu.make_async_copy(s, d, load_sems.at[n]) for n, (s, d) in enumerate(pairs)]
    for copy in copies:
        copy.start()

    def partner(off):
        to_x, to_y = gx + off // n_gy, gy + off % n_gy
        to_x = jnp.where(to_x >= n_gx, to_x - n_gx, to_x)
        to_y = jnp.where(to_y >= n_gy, to_y - n_gy, to_y)
        return to_x * n_gy + to_y, {"gx": to_x, "gy": to_y}

    def send(source, target, which, off):
        to, device = partner(off)
        copy = pltpu.make_async_remote_copy(
            src_ref=source.at[to],
            dst_ref=target.at[me],
            send_sem=sems.at[which, 0],
            recv_sem=sems.at[which, 1],
            device_id=device,
            device_id_type=pl.DeviceIdType.MESH,
        )
        copy.start()

    def all_done(buffer, sem):
        whole = buffer.at[pl.ds(0, count - 1)]
        pltpu.make_async_copy(whole, whole, sem).wait()

    barrier = pltpu.get_barrier_semaphore()
    for off in range(1, count):
        pl.semaphore_signal(barrier, inc=1, device_id=partner(off)[1], device_id_type=pl.DeviceIdType.MESH)
    copies[0].wait()
    copies[1].wait()
    ztab = z[...]
    for t in range(WIDTH // 16):
        copies[2 + t].wait()
        sides = []
        for h in range(2):
            at = pl.ds(16 * t + 8 * h, 8)
            block = charge[:, at, :]
            block = jnp.concatenate(
                [block[:1] + surface[0:1, at, :], block[1:-1], block[-1:] + surface[1:2, at, :]], 0
            )
            sides.append(block.reshape(DEPTH * 8, HEIGHT))
        out = dot_table(ztab, halved(pair_lanes(sides)))
        if t == 0:
            copies[6].wait()
            ytab = y[...]
        for h in range(2):
            side = out[:, HEIGHT * h:HEIGHT * (h + 1)]
            side = dot_packed(side, ytab)
            work[:, 16 * t + 8 * h:16 * t + 8 * h + 8, :] = side.reshape(DEPTH, 8, HEIGHT)
    for copy in copies[7:10]:
        copy.wait()
    xtab, utab, ctab = x[...], ur[...], uc[...]
    inner = interior()
    lane = lane_ids((8, HEIGHT))
    pl.semaphore_wait(barrier, count - 1)
    for copy in copies[10:14]:
        copy.wait()
    far_first = sorted(range(n_gx), key=lambda d: -min(d, n_gx - d))
    for step in far_first:
        t = partner(n_gy * (step % n_gx))[1]["gx"]
        sides = [work[pl.ds(8 * t + 4 * h, 4)].reshape(4 * WIDTH, HEIGHT) for h in range(2)]
        out = dot_table(xtab, halved(pair_lanes(sides)))
        for h in range(2):
            side = out[:, HEIGHT * h:HEIGHT * (h + 1)].reshape(4, WIDTH, HEIGHT)
            full = []
            corner = []
            for s in range(4):
                k = 8 * t + 4 * h + s
                one = side[s] * inv[k]
                base[k] = jnp.where(inner, one, 0.0)
                full.append(one)
                corner.append(one[0:1])
            full = jnp.concatenate(full, 0)
            parts = halved(full)
            rows = dot_table(utab, parts)
            own = jnp.concatenate(corner + [jnp.zeros((4, HEIGHT), F32)], 0)
            rows = jnp.where(lane == 0, own, rows[:8])
            cols = dot_table(ctab, parts, ((1,), (1,)))
            edge = lane_ids((1, 4 * WIDTH)) % WIDTH == 0
            near = jnp.where(edge, cols[2:3], cols[0:1])
            far = jnp.where(edge, 0.0, cols[1:2])
            for g in range(2):
                at = slice(HEIGHT * g, HEIGHT * (g + 1))
                msg[4 * t + 2 * h + g] = jnp.concatenate(
                    [rows[2 * g:2 * g + 2], rows[4 + 2 * g:6 + 2 * g], near[:, at], far[:, at]],
                    0,
                )
        for ahead in range(1 if step == 0 else 0, n_gy):
            send(msg, got, 0, n_gy * (step % n_gx) + ahead)
    for copy in copies[14:]:
        copy.wait()
    coef, table = owner_tables(own_ref[me], pair_ref[...], turned_ref[...], signs_ref[...])
    got[me] = msg[me]
    all_done(got, sems.at[0, 1])
    r = start_modes(n_gx, n_gy, [got[:, f, :] for f in range(6)])
    w = schur_modes(n_gx, n_gy, coef, table, *r)
    v = schur_modes(n_gx, n_gy, coef, table, *w)
    for f, field in enumerate(face_fields(n_gx, n_gy, r)):
        back[:, f, :] = field
    for f, field in enumerate(face_fields(n_gx, n_gy, w)):
        back[:, 8 + f, :] = field
    back[:, 6, :] = v[0][:, :HEIGHT]
    back[:, 7, :] = v[0][:, HEIGHT:]
    back[:, 14, :] = v[1]
    sums = (inner_product(r, r), inner_product(r, w), inner_product(w, w), inner_product(w, v))
    lanes = lane_ids((count, HEIGHT))
    back[:, 15, :] = sum(jnp.where(lanes == s, value, 0.0) for s, value in enumerate(sums))
    for step in far_first:
        for ahead in range(1 if step == 0 else 0, n_gy):
            send(back, landed, 1, n_gy * step + ahead)
    landed[me] = back[me]
    all_done(msg, sems.at[0, 0])
    all_done(landed, sems.at[1, 1])
    faces[...] = combine(landed[...])
    stores = inverse(
        faces, base, x, y, inv, small, square, work_hbm, edges_hbm, edges, work, store_sems
    )
    for copy in stores:
        copy.wait()
    all_done(back, sems.at[1, 0])


def combine(landed):
    near, far = landed[:, :8], landed[:, 8:]
    total = jnp.sum(far[:, 7:8, :], 0)
    lane = lane_ids((1, HEIGHT))
    c0, c1 = steps([jnp.sum(jnp.where(lane == s, total, 0.0), 1, keepdims=True) for s in range(4)])
    c0, c1 = c0[None], c1[None]
    lead = near - c0 * far
    rest = [lead[:, 0:2] - c1 * near[:, 6:8], lead[:, 4:5] - c1 * far[:, 6:7], jnp.zeros_like(near[:, :5])]
    return jnp.concatenate([c0 * near + c1 * far] + rest, 1)


def stacked(left, right):
    lh, ll = halved(left)
    rh, rl = halved(right)
    lhs = jnp.concatenate([lh.astype(F32), lh.astype(F32), ll.astype(F32)], 0).astype(BF16)
    rhs = jnp.concatenate([rh.astype(F32), rl.astype(F32), rh.astype(F32)], 0).astype(BF16)
    return dot(lhs, rhs, ((0,), (0,)))


def inverse(
    faces, base, x, y, inv, small, square, work_hbm, edges_hbm, edges, work, store_sems
):
    lane = lane_ids((8, HEIGHT))
    sub = lax.broadcasted_iota(jnp.int32, (8, HEIGHT), 0)
    const_left, const_right = small[0:8], small[8:16]
    xtab, ytab = x[...], y[...]
    half = DEPTH // 2
    rows = dot_packed(jnp.concatenate([faces[:, 8, :], faces[:, 9, :]], 0), ytab)
    cols = dot_packed(faces[:, 10, :], square[0:2 * HEIGHT])
    cols = jnp.concatenate([cols[:, :WIDTH], cols[:, WIDTH:]], 0)
    both = jnp.concatenate([rows, cols, jnp.zeros_like(cols)], 1)
    both = dot_table(square[2 * HEIGHT:, :DEPTH], halved(both))
    rows, cols = both[:, :HEIGHT], both[:, HEIGHT:HEIGHT + WIDTH]
    cols = jnp.concatenate([cols[:half], cols[half:]], 1)
    cols = jnp.where(lane_ids((half, HEIGHT)) % WIDTH == 0, 0.0, cols)
    edges[0:DEPTH] = rows
    edges[DEPTH:] = cols
    for t in range(DEPTH // 8):
        sides = []
        for h in range(2):
            blocks = []
            for g in range(2):
                o = 4 * t + 2 * h + g
                one = faces[o, :8]
                lhs = jnp.where((sub >= 4) & (sub < 6) & (lane % WIDTH > 0), one, const_left)
                up = jnp.concatenate([one[2:], one[:2]], 0)
                rhs = jnp.where((sub < 4) & (lane > 0), one, const_right)
                rhs = jnp.where((sub >= 6) & (lane == 0), up, rhs)
                out = stacked(lhs, rhs)
                for s in range(2):
                    k = 2 * o + s
                    blocks.append(out[WIDTH * s:WIDTH * (s + 1)] * inv[k] + base[k])
            sides.append(jnp.concatenate(blocks, 0))
        out = dot_table(xtab, halved(pair_lanes(sides)))
        for h in range(2):
            side = dot_packed(out[:, HEIGHT * h:HEIGHT * (h + 1)], ytab)
            work[8 * t + 4 * h:8 * t + 4 * h + 4] = side.reshape(4, WIDTH, HEIGHT)
        if t == 0:
            stores = [pltpu.make_async_copy(edges, edges_hbm, store_sems.at[DEPTH // 8])]
            stores[0].start()
        part = pl.ds(8 * t, 8)
        stores.append(pltpu.make_async_copy(work.at[part], work_hbm.at[part], store_sems.at[t]))
        stores[-1].start()
    return stores


def finish_kernel(
    edges_hbm, z_hbm, work_hbm, potential_hbm, residual_hbm,
    edges, z, work, potential, residual, load_sems, store_sems,
):
    pairs = [(edges_hbm, edges), (z_hbm, z)]
    columns = [pl.ds(16 * t, 16) for t in range(WIDTH // 16)]
    pairs += [(work_hbm.at[:, at, :], work.at[:, at, :]) for at in columns]
    loads = [pltpu.make_async_copy(s, d, load_sems.at[n]) for n, (s, d) in enumerate(pairs)]
    for load in loads:
        load.start()
    copies = []
    lane = lane_ids((8, HEIGHT))
    sub = lax.broadcasted_iota(jnp.int32, (8, HEIGHT), 0)
    half = DEPTH // 2
    loads[0].wait()
    unit = jnp.where(lane == 0, 1.0, 0.0)
    mark = jnp.where(((sub == 0) & (lane == 0)) | ((sub == 1) & (lane == WIDTH)), 1.0, 0.0)
    for o in range(half):
        lhs = jnp.where(sub == 2, edges[DEPTH + o:DEPTH + o + 1], mark)
        rhs = jnp.where(sub == 0, edges[o:o + 1], jnp.where(sub == 1, edges[half + o:half + o + 1], jnp.where(sub == 2, unit, 0.0)))
        out = stacked(lhs, rhs)
        residual[2 * o] = out[:WIDTH]
        residual[2 * o + 1] = out[WIDTH:]
        if o % 4 == 3:
            part = pl.ds(2 * (o - 3), 8)
            copies.append(
                pltpu.make_async_copy(residual.at[part], residual_hbm.at[part], store_sems.at[len(copies)])
            )
            copies[-1].start()
    loads[1].wait()
    ztab = z[...]
    for t, at in enumerate(columns):
        loads[2 + t].wait()
        sides = [work[:, 16 * t + 8 * h:16 * t + 8 * h + 8, :].reshape(DEPTH * 8, HEIGHT) for h in range(2)]
        out = dot_table(ztab, halved(pair_lanes(sides)))
        for h in range(2):
            side = out[:, HEIGHT * h:HEIGHT * (h + 1)]
            potential[:, 16 * t + 8 * h:16 * t + 8 * h + 8, :] = side.reshape(DEPTH, 8, HEIGHT)
        copies.append(
            pltpu.make_async_copy(potential.at[:, at, :], potential_hbm.at[:, at, :], store_sems.at[len(copies)])
        )
        copies[-1].start()
    for copy in copies:
        copy.wait()


def on_device_modes(n_gx, n_gy, charge, surface_charge):
    t = host_tables()
    count = n_gx * n_gy
    block = jax.ShapeDtypeStruct(charge.shape, F32)
    hbm = pl.BlockSpec(memory_space=pl.ANY)

    def held(values):
        return [pltpu.VMEM(value.shape, value.dtype) for value in values]

    pair = np.concatenate([t["pair"], t["plane"][None]], 0)
    turned = np.concatenate([np.swapaxes(pair, 1, 2)] * 2, 2)
    args = [charge, surface_charge, t["zf"], t["x"], t["y"], t["ur"], t["uc"], t["inv"], t["own"], pair, turned, t["signs"]]
    six, sixteen = (count, 6, HEIGHT), (count, 16, HEIGHT)
    small = np.concatenate([t["left"], t["right"]], 0)
    args += [small, t["square"]]
    edges = jax.ShapeDtypeStruct((DEPTH + DEPTH // 2, HEIGHT), F32)
    field, rims = pl.pallas_call(
        functools.partial(slab_kernel, n_gx, n_gy),
        out_shape=(block, edges),
        in_specs=[hbm] * len(args),
        out_specs=(hbm, hbm),
        scratch_shapes=held(args)
        + [pltpu.VMEM(shape, F32) for shape in [charge.shape] * 2 + [edges.shape, sixteen, six, six, sixteen, sixteen]]
        + [
            pltpu.SemaphoreType.DMA((20,)),
            pltpu.SemaphoreType.DMA((DEPTH // 8 + 1,)),
            pltpu.SemaphoreType.DMA((2, 2)),
        ],
        compiler_params=pltpu.CompilerParams(collective_id=0, has_side_effects=True),
        name="slab",
    )(*args)
    args = [rims, t["zi"], field]
    return pl.pallas_call(
        finish_kernel,
        out_shape=(block, block),
        in_specs=[hbm] * len(args),
        out_specs=(hbm, hbm),
        scratch_shapes=held(args)
        + [pltpu.VMEM(charge.shape, F32)] * 2
        + [pltpu.SemaphoreType.DMA((2 + WIDTH // 16,)), pltpu.SemaphoreType.DMA((DEPTH // 8 + WIDTH // 16,))],
        name="finish",
    )(*args)


def solution(mesh):
    per_device = functools.partial(on_device_modes, mesh.shape["gx"], mesh.shape["gy"])
    if (mesh.shape["gx"], mesh.shape["gy"]) != (4, 4):
        per_device = on_device
    in_specs = (P(None, ("slab", "gx"), "gy"), P(None, ("slab", "gx"), "gy"))
    out_specs = (P(None, ("slab", "gx"), "gy"), P(None, ("slab", "gx"), "gy"))
    return jax.shard_map(
        per_device, mesh=mesh, in_specs=in_specs, out_specs=out_specs, check_vma=False
    )
```
